32 devices in a mesh: sec: 4 (over y, core), tile: 8 (over z, x).
Axes of the slice: x: 2, y: 2, z: 4, core: 2. Of those that a mesh axis runs over, the one named last changes fastest.
Arguments:
- fields: float32 [4, 4, 512, 256], P('sec', None, 'tile'), may hold values from -6 to 6
- coefficients: float32 [4, 2, 512, 256], P('sec', None, 'tile'), may hold values from 0.04 to 0.24
- owner_tile: int32 [1536, 2], replicated, may hold values from 0 to 7, all different within a row; in each aligned block of 64 rows (0 to 63, 64 to 127, ...) at most 32 rows name the same one
- dest_block: int32 [1536, 2], replicated, may hold values from 0 to 63
- table_index: int32 [1536, 2], replicated, may hold values from 0 to 3
- tables: float32 [4, 256, 256], replicated, may hold values from -0.375 to 0.375
- land_mask: int32 [512, 256], P('tile'), may hold values 0 or 1
Outputs:
- fields_out: float32 [4, 4, 512, 256], P('sec', None, 'tile')
- surface: float32 [4, 512, 256], P('sec', 'tile')
The draws below stay inside these ranges and needn't reach their ends.
Inputs may be any that keep to these rules, and one draw needn't show every extreme that they name: `owner_tile`: each row names 2 different ocean tiles; in each aligned block of 64 rows (the blocks of one atmosphere device) no tile is named more than 32 times.
All inputs are finite; a program needn't handle non-finite values. No bound on the sum of `land_mask` on one device may be relied on, other than what follows from the above.
Results may differ from the reference program's by a relative error of at most 0.0001.
Values sent between devices are 32-bit elements; how exact they have to be, the bound alone decides.
No kernel may reach another device: no remote copies, remote signals or barrier semaphores. Data moves between devices by JAX's collectives and lax.ppermute only.
A program may use at most 64 MiB of HBM per device.

```python
import math
import jax
import jax.numpy as jnp
import numpy as np
from jax import lax

LEV = 4
BY = 64
BX = 256
STENCIL_SUBSTEPS = 2
R = 2
NTAB = 4
NY = 512
ATM_BLOCKS = 1536
CAP = 32
N_SEC = 4
N_TILE = 8


def with_ends(values, key, least, largest):
    dims = values.shape
    place = [jax.random.randint(jax.random.fold_in(key, axis), (), 0, dims[axis]) for axis in range(len(dims))]
    values = values.at[tuple(place)].set(least)
    longest = dims.index(max(dims))
    place[longest] = (place[longest] + 1) % dims[longest]
    return values.at[tuple(place)].set(largest)


def level_of(rng, shape, split, least, top_value):
    def one(position, blocks):
        steps = jax.random.uniform(jax.random.fold_in(jax.random.fold_in(rng, 6), position), (blocks,), jnp.float32, least / len(split), top_value / len(split))
        return jnp.repeat(jnp.exp(steps), shape[position] // blocks).reshape((-1,) + (1,) * (len(shape) - position - 1))

    factor_of = one(*split[0])
    for cut in split[1:]:
        factor_of = factor_of * one(*cut)
    return factor_of


def assign_block(key, own, number, rows, count, top, most, skew):
    ranking = jax.random.permutation(key, count)
    packed, common = shares(count, rows * top, most, skew, True), shares(count, rows * top, most, skew, False)
    places = jnp.arange(count)

    def named(sizes, turn):
        used = int((sizes > 0).sum())
        fixed = max(1, used // 4)
        passed = fixed + (places - fixed + turn * (used - fixed)) % max(1, count - fixed)
        return jnp.zeros((count,), jnp.int32).at[ranking[jnp.where(places < fixed, places, passed)]].set(jnp.asarray(sizes, jnp.int32))

    sizes = jnp.where(number % 4 == 0, named(packed, number // 4), named(common, number - number // 4 - 1))
    mixed = jax.random.permutation(jax.random.fold_in(own, 3), count)
    source_of, taker = mixed[0:count // 2 * 2:2], mixed[1:count // 2 * 2:2]
    slack = jnp.minimum(sizes[source_of] - 1, most - sizes[taker]) // 2
    slack = jnp.where((source_of == ranking[0]) | (taker == ranking[0]) | (sizes[taker] == 0), 0, jnp.maximum(slack, 0))
    passed = jax.random.randint(jax.random.fold_in(own, 4), (count // 2,), 0, 1 << 20) % (slack + 1)
    sizes = sizes.at[source_of].add(-passed).at[taker].add(passed)
    members = jnp.searchsorted(jnp.cumsum(sizes), jnp.arange(rows * top), side="right").astype(jnp.int32)
    table = members.reshape(top, rows).T
    table = table[jax.random.permutation(jax.random.fold_in(own, 1), rows)]
    turn = jax.random.randint(jax.random.fold_in(own, 2), (rows, 1), 0, top)
    return jnp.take_along_axis(table, (jnp.arange(top)[None, :] + turn) % top, axis=1)


def shares(count, total, limit, lean, full):
    weights = [(1 << 20) // math.isqrt(grade ** lean) + 1 for grade in range(1, count + 1)]
    largest = limit if full else min(limit, max(-(-total // count), total * weights[0] // sum(weights)))
    least = 1 if total - largest >= count - 1 else 0
    holding, rest = [largest] + [least] * (count - 1), total - largest - least * (count - 1)
    while rest > 0:
        candidates = [i for i in range(1, count) if holding[i] < largest] or [i for i in range(1, count) if holding[i] < limit]
        mass, budget = sum([weights[i] for i in candidates]), rest
        for i in candidates:
            addition = min(limit - holding[i], max(1, budget * weights[i] // mass), rest)
            holding[i] = holding[i] + addition
            rest = rest - addition
    return np.array(holding)


def scatter_about(rng, dims, width, most, pieces=(), kind=jnp.bfloat16):
    values = jax.random.normal(rng, dims, jnp.float32) * width
    if len(pieces) > 0:
        values = level_of(rng, dims, pieces, -0.22, 0.18) * values
    return jnp.clip(values, min=-most, max=most).astype(kind)


def setup_inputs(seed: int = 0) -> dict:
    key_of = jax.random.split(jax.random.key(seed), 8)
    fields = scatter_about(key_of[0], (N_SEC, LEV, NY, BX), 1.0, 6.0, ((0, 4), (2, 8)), jnp.float32)
    coefficients = jnp.clip(0.04 + 0.19999999552965164 * jax.random.uniform(key_of[1], (N_SEC, 2, NY, BX), jnp.float32) ** level_of(key_of[1], (N_SEC, 2, NY, BX), ((0, 4), (2, 8)), -0.2, 0.2), 0.04, 0.24)
    owner_tile_keys = jax.random.split(jax.random.fold_in(key_of[2], 1), ATM_BLOCKS // BY)
    owner_tile_turns = jax.random.permutation(jax.random.fold_in(key_of[2], 3), ATM_BLOCKS // BY)
    owner_tile = jax.vmap(lambda own, number: assign_block(jax.random.fold_in(key_of[2], 2), own, number, BY, N_TILE, R, CAP, 2))(owner_tile_keys, owner_tile_turns).reshape((ATM_BLOCKS, R))
    dest_block = with_ends(jax.random.randint(key_of[3], (ATM_BLOCKS, R), 0, BY), jax.random.fold_in(key_of[3], 1), 0, BY - 1).astype(jnp.int32)
    table_index = with_ends(jax.random.randint(key_of[4], (ATM_BLOCKS, R), 0, NTAB), jax.random.fold_in(key_of[4], 1), 0, NTAB - 1).astype(jnp.int32)
    tables = scatter_about(key_of[5], (NTAB, BX, BX), BX ** -0.5, 0.375, (), jnp.float32)
    land_mask = with_ends((jax.random.randint(key_of[6], (NY, BX), 0, 4) < 3).astype(jnp.int32), jax.random.fold_in(key_of[6], 1), 0, 1)
    return {"fields": fields, "coefficients": coefficients, "owner_tile": owner_tile, "dest_block": dest_block, "table_index": table_index, "tables": tables, "land_mask": land_mask}


forcing_rate = 0.5


def substep(field, kappa, speed):
    padded = jnp.pad(field, ((0, 0), (0, 0), (1, 1), (0, 0)))
    upper_row = padded[:, :, :-2]
    lower_row = padded[:, :, 2:]
    laplace = upper_row + lower_row + jnp.roll(field, 1, axis=3) + jnp.roll(field, -1, axis=3) - 4.0 * field
    return field + kappa[:, None] * laplace - 0.5 * speed[:, None] * (lower_row - upper_row)


def reference(fields, coefficients, owner_tile, dest_block, table_index, tables, land_mask):
    current = fields
    for _ in range(STENCIL_SUBSTEPS):
        current = substep(current, coefficients[:, 0], coefficients[:, 1])
    atmos = current[:N_SEC - 1]
    message_values = jnp.stack([atmos[:, 0], atmos[:, 0] - atmos[:, 1]], axis=2).reshape(ATM_BLOCKS, 2, BX)
    flux = jnp.zeros((NY, 2, BX), jnp.float32)
    for owner_slot in range(R):
        target_rows = owner_tile[:, owner_slot] * BY + dest_block[:, owner_slot]
        contrib = jnp.zeros((ATM_BLOCKS, 2, BX), jnp.float32)
        for table_ordinal in range(NTAB):
            weighted_values = jnp.einsum("wok,kt->wot", message_values, tables[table_ordinal], precision=lax.Precision.HIGHEST)
            chosen = (table_index[:, owner_slot] == table_ordinal)[:, None, None]
            contrib = contrib + jnp.where(chosen, weighted_values, 0.0)
        flux = flux.at[target_rows].add(contrib)
    ocean = current[N_SEC - 1]
    water = land_mask.astype(jnp.float32)
    top_level = ocean[0] + forcing_rate * water * flux[:, 0]
    second_level = ocean[1] + forcing_rate * water * flux[:, 1]
    forced = jnp.concatenate([top_level[None], second_level[None], ocean[2:]], axis=0)
    sea = water * top_level
    atmosphere_surface_field = jnp.zeros((ATM_BLOCKS, BX), jnp.float32)
    for owner_slot in range(R):
        target_rows = owner_tile[:, owner_slot] * BY + dest_block[:, owner_slot]
        values = sea[target_rows]
        for table_ordinal in range(NTAB):
            mirrored = jnp.dot(values, tables[table_ordinal].T, precision=lax.Precision.HIGHEST)
            chosen = (table_index[:, owner_slot] == table_ordinal)[:, None]
            atmosphere_surface_field = atmosphere_surface_field + jnp.where(chosen, mirrored, 0.0)
    fields_out = jnp.concatenate([current[:N_SEC - 1], forced[None]], axis=0)
    surface = jnp.concatenate([atmosphere_surface_field.reshape(N_SEC - 1, NY, BX), sea[None]], axis=0)
    return fields_out, surface
```

```python
import jax
import jax.numpy as jnp
from jax import lax
from jax.sharding import PartitionSpec as P

SUBSTEPS = 2
FORCING = 0.5
HIGH = lax.Precision.HIGH


def from_neighbours(up_rows, down_rows):
    size = lax.axis_size("tile")
    up = [(i, (i + 1) % size) for i in range(size - 1)]
    down = [(j, i) for i, j in up]
    return lax.ppermute(up_rows, "tile", up), lax.ppermute(down_rows, "tile", down)


def advance(extended, kappa, speed):
    center = extended[:, 1:-1]
    upper, lower = extended[:, :-2], extended[:, 2:]
    laplace = upper + lower + jnp.roll(center, 1, axis=2) + jnp.roll(center, -1, axis=2) - 4.0 * center
    return center + kappa * laplace - 0.5 * speed * (lower - upper)


def stencil(fields, coefficients):
    levels, rows, width = fields.shape
    w = SUBSTEPS
    last = jnp.concatenate(
        [fields[:, rows - w:].reshape(levels * w, width), coefficients[:, rows - w + 1:].reshape(2 * (w - 1), width)]
    )
    first = jnp.concatenate(
        [fields[:, :w].reshape(levels * w, width), coefficients[:, :w - 1].reshape(2 * (w - 1), width)]
    )
    before, after = from_neighbours(last, first)
    cut = levels * w
    wide = jnp.concatenate(
        [before[:cut].reshape(levels, w, width), fields, after[:cut].reshape(levels, w, width)], axis=1
    )
    coef = jnp.concatenate(
        [before[cut:].reshape(2, w - 1, width), coefficients, after[cut:].reshape(2, w - 1, width)], axis=1
    )
    for step in range(w):
        inner = slice(step, coef.shape[1] - step)
        wide = advance(wide, coef[0, inner], coef[1, inner])
    return wide


def local(fields, coefficients, owner_tile, dest_block, table_index, tables, land_mask):
    n_sec, n_tile = lax.axis_size("sec"), lax.axis_size("tile")
    sec, tile = lax.axis_index("sec"), lax.axis_index("tile")
    rows, width = fields.shape[2:]
    n_tables = tables.shape[0]
    ocean_here = sec == n_sec - 1
    span = n_tile * rows

    start = jnp.minimum(sec, n_sec - 2) * span
    owner = lax.dynamic_slice_in_dim(owner_tile, start, span, 0)
    dest = lax.dynamic_slice_in_dim(dest_block, start, span, 0)
    table = lax.dynamic_slice_in_dim(table_index, start, span, 0)
    key = jnp.where((owner == tile) & jnp.logical_not(ocean_here), table * rows + dest, -1).T
    slots = jnp.arange(n_tables * rows, dtype=jnp.int32)[:, None]
    gather_in = sum((slots == key[r][None]).astype(jnp.float32) for r in range(key.shape[0]))

    cut = lambda a: lax.dynamic_slice_in_dim(a, tile * rows, rows, 0)
    sea_row = cut(owner) * rows + cut(dest)
    my_table = cut(table)
    places = jnp.arange(span, dtype=jnp.int32)
    gather_back = sum(
        (
            (places == sea_row[:, r][None, :, None])
            & (my_table[:, r][None, :, None] == jnp.arange(n_tables, dtype=jnp.int32)[:, None, None])
        ).astype(jnp.float32)
        for r in range(key.shape[0])
    ).reshape(n_tables * rows, span)

    current = stencil(fields[0], coefficients[0])
    stacked = tables.reshape(n_tables * width, width)

    def partial_flux(payload):
        whole = lax.all_gather(payload, "tile", tiled=True)
        grouped = jnp.dot(gather_in, whole, precision=HIGH).reshape(n_tables, rows, width)
        grouped = jnp.swapaxes(grouped, 0, 1).reshape(rows, n_tables * width)
        return jnp.dot(grouped, stacked, precision=HIGH)

    water = land_mask.astype(jnp.float32)
    half = FORCING * water
    top_level = lax.psum(jnp.where(ocean_here, current[0], half * partial_flux(current[0])), "sec")
    second = lax.psum(jnp.where(ocean_here, current[1], half * partial_flux(current[0] - current[1])), "sec")
    sea = water * top_level
    all_sea = lax.all_gather(sea, "tile", tiled=True)
    picked = jnp.dot(gather_back, all_sea, precision=HIGH).reshape(n_tables, rows, width)
    seen = jnp.einsum("kgc,kdc->gd", picked, tables, precision=HIGH)
    surface = jnp.where(ocean_here, sea, seen)[None]
    forced = jnp.concatenate([top_level[None], second[None], current[2:]], axis=0)
    return jnp.where(ocean_here, forced, current)[None], surface


def solution(mesh):
    placed = (P("sec", None, "tile", None), P("sec", None, "tile", None), P(), P(), P(), P(), P("tile", None))
    return jax.shard_map(
        local,
        mesh=mesh,
        in_specs=placed,
        out_specs=(P("sec", None, "tile", None), P("sec", "tile", None)),
        check_vma=False,
    )
```

```python
import jax
import jax.numpy as jnp
from jax import lax
from jax.sharding import PartitionSpec as P

FORCING = 0.5
HIGH = lax.Precision.HIGH
HIGHEST = lax.Precision.HIGHEST


def sideways(x, kappa):
    return x + kappa * (jnp.roll(x, 1, axis=-1) + jnp.roll(x, -1, axis=-1) - 4.0 * x)


def substep(field, kappa, speed):
    padded = jnp.pad(field, ((0, 0), (1, 1), (0, 0)))
    upper, lower = padded[:, :-2], padded[:, 2:]
    laplace = upper + lower + jnp.roll(field, 1, axis=2) + jnp.roll(field, -1, axis=2) - 4.0 * field
    return field + kappa * laplace - 0.5 * speed * (lower - upper)


def bottom_part(b, bb, kappa, u, u_next, q_next, a_next):
    return bb * u_next, sideways(b * u_next, kappa) + b * (q_next + a_next * u)


def top_part(a, aa, kappa, u, u_prev, q_prev, b_prev):
    return sideways(a * u_prev, kappa) + a * (q_prev + b_prev * u), aa * u_prev


def ahead(x):
    return jnp.concatenate([x[1:], jnp.zeros_like(x[:1])], axis=0)


def behind(x):
    return jnp.concatenate([jnp.zeros_like(x[:1]), x[:-1]], axis=0)


def local(fields, coefficients, owner_tile, dest_block, table_index, tables, land_mask):
    n_sec, n_tile = lax.axis_size("sec"), lax.axis_size("tile")
    sec, tile = lax.axis_index("sec"), lax.axis_index("tile")
    u = fields[0]
    kappa, speed = coefficients[0, 0], coefficients[0, 1]
    levels, rows, width = u.shape
    n_tables = tables.shape[0]
    fan = owner_tile.shape[1]
    ocean_here = sec == n_sec - 1
    span = n_tile * rows
    cap = 2 * fan * rows // n_tile
    f32, i32 = jnp.float32, jnp.int32

    start = jnp.minimum(sec, n_sec - 2) * span
    owner = lax.dynamic_slice_in_dim(owner_tile, start, span, 0)
    dest = lax.dynamic_slice_in_dim(dest_block, start, span, 0)
    table = lax.dynamic_slice_in_dim(table_index, start, span, 0)
    cut = lambda a: lax.dynamic_slice_in_dim(a, tile * rows, rows, 0)
    my_owner, my_table = cut(owner), cut(table)
    hot = (my_owner.reshape(-1)[:, None] == jnp.arange(n_tile, dtype=i32)[None, :]).astype(i32)
    rank = jnp.sum((jnp.cumsum(hot, axis=0) - hot) * hot, axis=1).reshape(rows, fan)
    target = my_owner * cap + rank
    slots = jnp.arange(n_tile * cap, dtype=i32)
    placing = sum((slots[:, None] == target[:, r][None, :]).astype(f32) for r in range(fan))
    placing = placing * jnp.logical_not(ocean_here).astype(f32)

    stepped = substep(substep(u, kappa, speed), kappa, speed)
    a = kappa + 0.5 * speed
    b = kappa - 0.5 * speed
    q_top = sideways(u[:, 0], kappa[0]) + b[0] * u[:, 1]
    q_bot = sideways(u[:, -1], kappa[-1]) + a[-1] * u[:, -2]
    coef_edges = jnp.stack([a[0], a[0] * a[1], kappa[0], b[-1], b[-1] * b[-2], kappa[-1]])
    level_edges = jnp.stack([u[:, 0], q_top, u[:, -1], q_bot], axis=1)

    def outgoing(values, extra):
        sent = jnp.dot(placing, values, precision=HIGHEST).reshape(n_tile, cap, width)
        short = -(cap + extra.shape[0]) % 8
        extra = jnp.concatenate([extra, jnp.zeros((short, width), f32)])
        extra = jnp.broadcast_to(extra[None], (n_tile,) + extra.shape)
        return jnp.concatenate([sent, extra], axis=1)

    first = outgoing(stepped[0], jnp.concatenate([coef_edges, level_edges[0], level_edges[1]]))
    second = outgoing(stepped[0] - stepped[1], level_edges[2:].reshape(-1, width))
    exchange = lambda x, axis: lax.all_to_all(x, axis, split_axis=0, concat_axis=0, tiled=True)
    first = exchange(first, "tile")
    second = exchange(second, "tile")

    mine = (owner == tile).astype(i32).reshape(n_tile, rows * fan)
    ranking = jnp.cumsum(mine, axis=1) - mine
    slot_hot = mine[:, None, :] * (ranking[:, None, :] == jnp.arange(cap, dtype=i32)[None, :, None]).astype(i32)
    pick = lambda a: jnp.sum(slot_hot * a.reshape(n_tile, 1, rows * fan), axis=2).reshape(-1)
    valid = (pick(jnp.ones_like(owner)) > 0) & jnp.logical_not(ocean_here)
    slot_dest = jnp.where(valid, pick(dest), -1)
    slot_key = jnp.where(valid, slot_dest + rows * pick(table), -1)
    lines = jnp.arange(n_tables * rows, dtype=i32)[:, None]
    collect = (lines == slot_key[None, :]).astype(f32)
    spread = (slot_dest[:, None] == jnp.arange(rows, dtype=i32)[None, :]).astype(f32)
    key = jnp.where((owner == tile) & jnp.logical_not(ocean_here), table * rows + dest, -1)
    key = key.reshape(n_tile, rows, fan)
    edge_key = jnp.stack([key[:, 0], key[:, 1], key[:, -2], key[:, -1]]).reshape(-1, fan)
    collect_edges = sum((lines == edge_key[:, r][None, :]).astype(f32) for r in range(fan))

    coef = [first[:, cap + i] for i in range(6)]
    a0, aa, k0, b1, bb, k1 = coef

    def corrections(u0, q0, u1, q1):
        r0, r1 = top_part(a0, aa, k0, u0, behind(u1), behind(q1), behind(b1))
        r2, r3 = bottom_part(b1, bb, k1, u1, ahead(u0), ahead(q0), ahead(a0))
        return jnp.stack([r0, r1, r2, r3])

    edges = [corrections(*[first[:, cap + 6 + 4 * l + i] for i in range(4)]) for l in range(2)]
    edges += [corrections(*[second[:, cap + 4 * l + i] for i in range(4)]) for l in range(2)]
    mine_edges = lax.dynamic_index_in_dim(jnp.stack(edges), tile, axis=2, keepdims=False)
    stepped = jnp.concatenate(
        [stepped[:, :2] + mine_edges[:, :2], stepped[:, 2:-2], stepped[:, -2:] + mine_edges[:, 2:]], axis=1
    )

    stacked = tables.reshape(n_tables * width, width)

    def partial_flux(arrived, edge_rows):
        grouped = jnp.dot(collect, arrived[:, :cap].reshape(-1, width), precision=HIGH)
        grouped += jnp.dot(collect_edges, edge_rows.reshape(-1, width), precision=HIGH)
        grouped = jnp.swapaxes(grouped.reshape(n_tables, rows, width), 0, 1)
        return jnp.dot(grouped.reshape(rows, n_tables * width), stacked, precision=HIGH)

    water = land_mask.astype(f32)
    half = FORCING * water

    def over_sections(part):
        part = jnp.broadcast_to(part[None], (n_sec,) + part.shape)
        return jnp.sum(exchange(part, "sec"), axis=0)

    top_level = over_sections(jnp.where(ocean_here, stepped[0], half * partial_flux(first, edges[0])))
    sea = water * top_level
    back = jnp.dot(spread, sea, precision=HIGHEST).reshape(n_tile, cap, width)
    back = exchange(back, "tile").reshape(n_tile * cap, width)
    second_level = over_sections(jnp.where(ocean_here, stepped[1], half * partial_flux(second, edges[0] - edges[1])))

    table_of = jnp.arange(n_tables, dtype=i32)[:, None, None]
    gather_back = sum(
        ((slots == target[:, r][None, :, None]) & (my_table[:, r][None, :, None] == table_of)).astype(f32)
        for r in range(fan)
    ).reshape(n_tables * rows, n_tile * cap)
    picked = jnp.dot(gather_back, back, precision=HIGH).reshape(n_tables, rows, width)
    seen = jnp.einsum("kgc,kdc->gd", picked, tables, precision=HIGH)
    surface = jnp.where(ocean_here, sea, seen)[None]
    forced = jnp.concatenate([top_level[None], second_level[None], stepped[2:]], axis=0)
    return jnp.where(ocean_here, forced, stepped)[None], surface


def solution(mesh):
    placed = (P("sec", None, "tile", None), P("sec", None, "tile", None), P(), P(), P(), P(), P("tile", None))
    return jax.shard_map(
        local,
        mesh=mesh,
        in_specs=placed,
        out_specs=(P("sec", None, "tile", None), P("sec", "tile", None)),
        check_vma=False,
    )
```

```python
import jax
import jax.numpy as jnp
from jax import lax
from jax.sharding import PartitionSpec as P

FORCING = 0.5
HIGH = lax.Precision.HIGH
HIGHEST = lax.Precision.HIGHEST


def sideways(x, kappa):
    return x + kappa * (jnp.roll(x, 1, axis=-1) + jnp.roll(x, -1, axis=-1) - 4.0 * x)


def substep(field, kappa, speed):
    padded = jnp.pad(field, ((0, 0), (1, 1), (0, 0)))
    upper, lower = padded[:, :-2], padded[:, 2:]
    laplace = upper + lower + jnp.roll(field, 1, axis=2) + jnp.roll(field, -1, axis=2) - 4.0 * field
    return field + kappa * laplace - 0.5 * speed * (lower - upper)


def bottom_part(b, bb, kappa, u, u_next, q_next, a_next):
    return bb * u_next, sideways(b * u_next, kappa) + b * (q_next + a_next * u)


def top_part(a, aa, kappa, u, u_prev, q_prev, b_prev):
    return sideways(a * u_prev, kappa) + a * (q_prev + b_prev * u), aa * u_prev


def ahead(x):
    return jnp.concatenate([x[1:], jnp.zeros_like(x[:1])], axis=0)


def behind(x):
    return jnp.concatenate([jnp.zeros_like(x[:1]), x[:-1]], axis=0)


def local(fields, coefficients, owner_tile, dest_block, table_index, tables, land_mask):
    n_sec, n_tile = lax.axis_size("sec"), lax.axis_size("tile")
    sec, tile = lax.axis_index("sec"), lax.axis_index("tile")
    u = fields[0]
    kappa, speed = coefficients[0, 0], coefficients[0, 1]
    levels, rows, width = u.shape
    n_tables = tables.shape[0]
    fan = owner_tile.shape[1]
    ocean_here = sec == n_sec - 1
    span = n_tile * rows
    cap = 2 * fan * rows // n_tile
    f32, i32 = jnp.float32, jnp.int32

    start = jnp.minimum(sec, n_sec - 2) * span
    owner = lax.dynamic_slice_in_dim(owner_tile, start, span, 0)
    dest = lax.dynamic_slice_in_dim(dest_block, start, span, 0)
    table = lax.dynamic_slice_in_dim(table_index, start, span, 0)
    cut = lambda a: lax.dynamic_slice_in_dim(a, tile * rows, rows, 0)
    my_owner, my_table = cut(owner), cut(table)
    hot = (my_owner.reshape(-1)[:, None] == jnp.arange(n_tile, dtype=i32)[None, :]).astype(i32)
    rank = jnp.sum((jnp.cumsum(hot, axis=0) - hot) * hot, axis=1).reshape(rows, fan)
    target = my_owner * cap + rank
    slots = jnp.arange(n_tile * cap, dtype=i32)
    placing = sum((slots[:, None] == target[:, r][None, :]).astype(f32) for r in range(fan))
    placing = placing * jnp.logical_not(ocean_here).astype(f32)

    stepped = substep(substep(u, kappa, speed), kappa, speed)
    a = kappa + 0.5 * speed
    b = kappa - 0.5 * speed
    q_top = sideways(u[:, 0], kappa[0]) + b[0] * u[:, 1]
    q_bot = sideways(u[:, -1], kappa[-1]) + a[-1] * u[:, -2]
    coef_edges = jnp.stack([a[0], a[0] * a[1], kappa[0], b[-1], b[-1] * b[-2], kappa[-1]])
    level_edges = jnp.stack([u[:, 0], q_top, u[:, -1], q_bot], axis=1)

    exchange = lambda x, axis: lax.all_to_all(x, axis, split_axis=0, concat_axis=0, tiled=True)
    payload = jnp.concatenate([stepped[0], stepped[0] - stepped[1]], axis=1)
    sent = jnp.dot(placing, payload, precision=HIGHEST).reshape(n_tile, cap, 2 * width)
    extra = jnp.concatenate([coef_edges, level_edges.reshape(-1, width)])
    extra = jnp.concatenate([extra, jnp.zeros((-(2 * cap + extra.shape[0]) % 8, width), f32)])
    extra = jnp.broadcast_to(extra[None], (n_tile,) + extra.shape)
    first = exchange(jnp.concatenate([sent[:, :, :width], sent[:, :, width:], extra], axis=1), "tile")

    mine = (owner == tile).astype(i32).reshape(n_tile, rows * fan)
    ranking = jnp.cumsum(mine, axis=1) - mine
    slot_hot = mine[:, None, :] * (ranking[:, None, :] == jnp.arange(cap, dtype=i32)[None, :, None]).astype(i32)
    pick = lambda a: jnp.sum(slot_hot * a.reshape(n_tile, 1, rows * fan), axis=2).reshape(-1)
    valid = (pick(jnp.ones_like(owner)) > 0) & jnp.logical_not(ocean_here)
    slot_dest = jnp.where(valid, pick(dest), -1)
    slot_key = jnp.where(valid, slot_dest + rows * pick(table), -1)
    lines = jnp.arange(n_tables * rows, dtype=i32)[:, None]
    collect = (lines == slot_key[None, :]).astype(f32)
    spread = (slot_dest[:, None] == jnp.arange(rows, dtype=i32)[None, :]).astype(f32)
    key = jnp.where((owner == tile) & jnp.logical_not(ocean_here), table * rows + dest, -1)
    key = key.reshape(n_tile, rows, fan)
    edge_key = jnp.stack([key[:, 0], key[:, 1], key[:, -2], key[:, -1]]).reshape(-1, fan)
    collect_edges = sum((lines == edge_key[:, r][None, :]).astype(f32) for r in range(fan))

    coef = [first[:, 2 * cap + i] for i in range(6)]
    a0, aa, k0, b1, bb, k1 = coef

    def corrections(u0, q0, u1, q1):
        r0, r1 = top_part(a0, aa, k0, u0, behind(u1), behind(q1), behind(b1))
        r2, r3 = bottom_part(b1, bb, k1, u1, ahead(u0), ahead(q0), ahead(a0))
        return jnp.stack([r0, r1, r2, r3])

    edges = [corrections(*[first[:, 2 * cap + 6 + 4 * l + i] for i in range(4)]) for l in range(levels)]
    own = lambda e: lax.dynamic_index_in_dim(e, tile, axis=1, keepdims=False)

    def whole_level(level):
        mine_edges = own(edges[level])
        plane = stepped[level]
        return jnp.concatenate([plane[:2] + mine_edges[:2], plane[2:-2], plane[-2:] + mine_edges[2:]], axis=0)

    level0, level1, level2, level3 = [whole_level(l) for l in range(levels)]

    stacked = tables.reshape(n_tables * width, width)

    arrived = jnp.concatenate([first[:, :cap], first[:, cap:2 * cap]], axis=2).reshape(-1, 2 * width)
    edge_rows = jnp.concatenate([edges[0], edges[0] - edges[1]], axis=-1).reshape(-1, 2 * width)
    grouped = jnp.dot(collect, arrived, precision=HIGH) + jnp.dot(collect_edges, edge_rows, precision=HIGH)
    grouped = grouped.reshape(n_tables, rows, 2, width).transpose(2, 1, 0, 3)
    partial_flux = jnp.dot(grouped.reshape(2 * rows, n_tables * width), stacked, precision=HIGH).reshape(2, rows, width)

    water = land_mask.astype(f32)
    half = FORCING * water

    part = jnp.where(ocean_here, jnp.stack([level0, level1]), half * partial_flux)
    part = jnp.broadcast_to(part[None], (n_sec,) + part.shape)
    top_level, second_level = jnp.sum(exchange(part, "sec"), axis=0)
    sea = water * top_level
    back = jnp.dot(spread, sea, precision=HIGHEST).reshape(n_tile, cap, width)
    back = exchange(back, "tile").reshape(n_tile * cap, width)
    table_of = jnp.arange(n_tables, dtype=i32)[:, None, None]
    gather_back = sum(
        ((slots == target[:, r][None, :, None]) & (my_table[:, r][None, :, None] == table_of)).astype(f32)
        for r in range(fan)
    ).reshape(n_tables * rows, n_tile * cap)
    picked = jnp.dot(gather_back, back, precision=HIGH).reshape(n_tables, rows, width)
    seen = jnp.einsum("kgc,kdc->gd", picked, tables, precision=HIGH)
    surface = jnp.where(ocean_here, sea, seen)[None]
    ended = [jnp.where(ocean_here, top_level, level0), jnp.where(ocean_here, second_level, level1), level2, level3]
    return jnp.stack(ended)[None], surface


def solution(mesh):
    placed = (P("sec", None, "tile", None), P("sec", None, "tile", None), P(), P(), P(), P(), P("tile", None))
    return jax.shard_map(
        local,
        mesh=mesh,
        in_specs=placed,
        out_specs=(P("sec", None, "tile", None), P("sec", "tile", None)),
        check_vma=False,
    )
```

```python
import functools

import jax
import jax.numpy as jnp
from jax import lax
from jax.experimental import pallas as pl
from jax.experimental.pallas import tpu as pltpu
from jax.sharding import PartitionSpec as P

FORCING = 0.5
F32, BF16, I32 = jnp.float32, jnp.bfloat16, jnp.int32
N_COEF = 6
VMEM = pl.BlockSpec(memory_space=pltpu.VMEM)


def iota(shape, axis):
    return lax.broadcasted_iota(I32, shape, axis)


def roll(x, shift, axis):
    return pltpu.roll(x, shift % x.shape[axis], axis)


def split(x, parts):
    out = []
    for _ in range(parts):
        out.append(x.astype(BF16))
        x = x - out[-1].astype(F32)
    return out


def mm(a, b):
    return lax.dot_general(a, b, (((1,), (0,)), ((), ())), preferred_element_type=F32)


def mm_t(a, b):
    return lax.dot_general(a, b, (((1,), (1,)), ((), ())), preferred_element_type=F32)


def select_rows(hot, x, parts):
    return sum(mm(hot, p) for p in split(x, parts))


def product(a, b, dot):
    (a1, a2), (b1, b2) = split(a, 2), split(b, 2)
    rows = a.shape[0]
    both = dot(jnp.concatenate([a1, a2]), b1)
    return both[:rows] + both[rows:] + dot(a1, b2)


def sideways(x, kappa):
    return x + kappa * (roll(x, 1, x.ndim - 1) + roll(x, -1, x.ndim - 1) - 4.0 * x)


def substep(u, kappa, speed):
    rows = u.shape[1]
    row = iota(u.shape, 1)
    upper = jnp.where(row == 0, 0.0, roll(u, 1, 1))
    lower = jnp.where(row == rows - 1, 0.0, roll(u, -1, 1))
    laplace = upper + lower + roll(u, 1, 2) + roll(u, -1, 2) - 4.0 * u
    return u + kappa * laplace - 0.5 * speed * (lower - upper)


def place():
    sec, tile = lax.axis_index("sec"), lax.axis_index("tile")
    return sec, tile, sec < lax.axis_size("sec") - 1


def own_slots(owner_ref, rows, cap):
    sec, tile, atmos = place()
    n_sec, n_tile = lax.axis_size("sec"), lax.axis_size("tile")
    block = (jnp.minimum(sec, n_sec - 2) * n_tile + tile) * rows
    first = pl.multiple_of(block // 128 * 128, 128)
    half = block - first
    shape = (n_tile * cap, 128)
    lane = iota((1, 128), 1)
    inside = (lane >= half) & (lane < half + rows) & atmos
    owner = jnp.where(inside, owner_ref[:, pl.ds(first, 128)], -1)
    slot = iota(shape, 0)
    hot = [(owner[r : r + 1] == slot // cap).astype(F32) for r in range(owner.shape[0])]
    both = sum(hot)
    before = (iota((128, 128), 0) < iota((128, 128), 1)).astype(BF16)
    rank = mm(both.astype(BF16), before)
    placed = rank == (slot % cap).astype(F32)
    return first, [jnp.where(placed, h, 0.0) for h in hot]


def send_kernel(cap, fields_ref, coef_ref, owner_ref, send_ref, stepped_ref):
    u = fields_ref[0]
    kappa, speed = coef_ref[0, 0], coef_ref[0, 1]
    levels, rows, width = u.shape
    stepped = substep(substep(u, kappa, speed), kappa, speed)
    stepped_ref[...] = stepped
    payload = jnp.concatenate([stepped[0], stepped[0] - stepped[1]], axis=1)
    _, placed = own_slots(owner_ref, rows, cap)
    sent = select_rows(sum(placed).astype(BF16), jnp.concatenate([payload] * (128 // rows)), 3)
    n_tile = send_ref.shape[0]
    send_ref[:, :cap] = sent[:, :width].reshape(n_tile, cap, width)
    send_ref[:, cap : 2 * cap] = sent[:, width:].reshape(n_tile, cap, width)
    a = kappa + 0.5 * speed
    b = kappa - 0.5 * speed
    top, bot = slice(0, 1), slice(rows - 1, rows)
    extra = [a[0:1], a[0:1] * a[1:2], kappa[top], b[bot], b[rows - 1 :] * b[rows - 2 : rows - 1], kappa[bot]]
    for l in range(levels):
        q_top = sideways(u[l, top], kappa[top]) + b[top] * u[l, 1:2]
        q_bot = sideways(u[l, bot], kappa[bot]) + a[bot] * u[l, rows - 2 : rows - 1]
        extra += [u[l, top], q_top, u[l, bot], q_bot]
    fill = send_ref.shape[1] - 2 * cap - len(extra)
    if fill:
        extra.append(jnp.zeros((fill, width), F32))
    extra = jnp.concatenate(extra)
    send_ref[:, 2 * cap :] = jnp.broadcast_to(extra[None], (n_tile,) + extra.shape)


def index_kernel(cap, rows, n_tables, owner_ref, dest_ref, table_ref, arrive_ref, collect_ref, edge_ref, back_ref):
    sec, tile, atmos = place()
    n_sec, n_tile = lax.axis_size("sec"), lax.axis_size("tile")
    span = n_tile * rows
    start = jnp.minimum(sec, n_sec - 2) * span
    fan = owner_ref.shape[0]
    lines = n_tables * rows
    per = 128 // rows
    g, h = iota((128, 128), 0), iota((128, 128), 1)
    before = ((g < h) & (g // rows == h // rows)).astype(BF16)
    line = iota((lines, 128), 0)
    seat = iota((per * cap, 128), 0)
    lane = iota((per * cap, 128), 1)
    edges = jnp.zeros((lines, 128), F32)
    for group in range(span // 128):
        at = pl.ds(pl.multiple_of(start + group * 128, 128), 128)
        mine = [(owner_ref[r : r + 1, at] == tile) & atmos for r in range(fan)]
        key = jnp.full((1, 128), -1, I32)
        for r in range(fan):
            key = jnp.where(mine[r], table_ref[r : r + 1, at] * rows + dest_ref[r : r + 1, at], key)
        held = (key >= 0).astype(F32)
        rank = mm(jnp.broadcast_to(held, (16, 128)).astype(BF16), before)[:1]
        sits = (rank == (seat % cap).astype(F32)) & (lane // rows == seat // cap) & (held > 0)
        hit = (line == key).astype(BF16)
        arrive = mm_t(sits.astype(BF16), hit)
        arrive_ref[group * per * cap : (group + 1) * per * cap] = arrive
        block, within = group * per + g // rows, g % rows
        column = sum(jnp.where(within == w, i, 0) for i, w in enumerate((0, 1, rows - 2, rows - 1)))
        is_edge = (within < 2) | (within >= rows - 2)
        edges += mm(hit, (is_edge & (h == column * n_tile + block)).astype(BF16))
    arrive = arrive_ref[...]
    collect_ref[...] = arrive.T.astype(BF16)
    edge_ref[...] = edges.astype(BF16)
    first, placed = own_slots(owner_ref, rows, cap)
    table = table_ref[:, pl.ds(first, 128)]
    for k in range(n_tables):
        here = sum(jnp.where(table[r : r + 1] == k, placed[r], 0.0) for r in range(fan))
        back_ref[k * 128 : (k + 1) * 128] = here.T.astype(BF16)


def shifted(x, by):
    row = iota(x.shape, 0)
    return jnp.where(row == (0 if by > 0 else x.shape[0] - 1), 0.0, roll(x, by, 0))


def flux_kernel(cap, got_ref, collect_ref, edge_ref, tables_ref, stepped_ref, mask_ref, part_ref, whole_ref):
    sec, tile, atmos = place()
    n_tile = got_ref.shape[0]
    levels, rows, width = stepped_ref.shape
    n_tables = tables_ref.shape[0]
    line = lambda i: got_ref[:, 2 * cap + i, :]
    a0, aa, k0, b1, bb, k1 = [line(i) for i in range(N_COEF)]
    b_prev, a_next = shifted(b1, 1), shifted(a0, -1)
    here = iota((n_tile, width), 0) == tile
    corrections = []
    for l in range(levels):
        u0, q0, u1, q1 = [line(N_COEF + 4 * l + i) for i in range(4)]
        u_prev, q_prev, u_next, q_next = shifted(u1, 1), shifted(q1, 1), shifted(u0, -1), shifted(q0, -1)
        correction = [
            sideways(a0 * u_prev, k0) + a0 * (q_prev + b_prev * u0),
            aa * u_prev,
            bb * u_next,
            sideways(b1 * u_next, k1) + b1 * (q_next + a_next * u1),
        ]
        corrections.append(correction)
        own = [jnp.sum(jnp.where(here, c, 0.0), axis=0, keepdims=True) for c in correction]
        plane = stepped_ref[l]
        whole_ref[l] = jnp.concatenate(
            [plane[:2] + jnp.concatenate(own[:2]), plane[2 : rows - 2], plane[rows - 2 :] + jnp.concatenate(own[2:])]
        )
    c0, c1 = jnp.concatenate(corrections[0]), jnp.concatenate(corrections[1])
    correction = jnp.concatenate([c0, c0 - c1], axis=1)
    if correction.shape[0] < 128:
        correction = jnp.concatenate([correction, jnp.zeros((128 - correction.shape[0], 2 * width), F32)])
    slots = [got_ref[:, i * cap : (i + 1) * cap, :].reshape(n_tile * cap, width) for i in range(2)]
    grouped = select_rows(collect_ref[...], jnp.concatenate(slots, axis=1), 2) + select_rows(edge_ref[...], correction, 2)
    flux = jnp.zeros((2 * rows, width), F32)
    for k in range(n_tables):
        lines = grouped[k * rows : (k + 1) * rows]
        flux += product(jnp.concatenate([lines[:, :width], lines[:, width:]]), tables_ref[k], mm)
    half = FORCING * mask_ref[...].astype(F32)
    for l in range(2):
        part = jnp.where(atmos, half * flux[l * rows : (l + 1) * rows], whole_ref[l])
        for s in range(part_ref.shape[0]):
            part_ref[s, l] = part


def sea_kernel(n_tables, parts_ref, mask_ref, arrive_ref, sea_ref, back_ref):
    top = parts_ref[0, 0]
    for s in range(1, parts_ref.shape[0]):
        top += parts_ref[s, 0]
    sea = mask_ref[...].astype(F32) * top
    sea_ref[...] = sea
    back_ref[...] = select_rows(arrive_ref[...].astype(BF16), jnp.concatenate([sea] * n_tables), 3)


def surface_kernel(came_ref, back_ref, tables_ref, sea_ref, out_ref):
    sec, tile, atmos = place()
    rows, width = sea_ref.shape
    picked = select_rows(back_ref[...], came_ref[...], 2)
    seen = jnp.zeros((rows, width), F32)
    for k in range(tables_ref.shape[0]):
        lines = picked[k * 128 : (k + 1) * 128]
        lines = sum(lines[i : i + rows] for i in range(0, 128, rows))
        seen += product(lines, tables_ref[k], mm_t)
    out_ref[...] = jnp.where(atmos, seen, sea_ref[...])


def call(kernel, n_in, outs, flops=0):
    shapes = [jax.ShapeDtypeStruct(s, d) for s, d in outs]
    return pl.pallas_call(
        kernel,
        out_shape=shapes,
        in_specs=[VMEM] * n_in,
        out_specs=[VMEM] * len(shapes),
        compiler_params=pltpu.CompilerParams(vmem_limit_bytes=32 * 1024 * 1024),
        cost_estimate=pl.CostEstimate(flops=flops, bytes_accessed=1 << 20, transcendentals=0),
    )


def local(fields, coefficients, owner_tile, dest_block, table_index, tables, land_mask):
    n_sec, n_tile = lax.axis_size("sec"), lax.axis_size("tile")
    levels, rows, width = fields.shape[1:]
    fan = owner_tile.shape[1]
    n_tables = tables.shape[0]
    cap = 2 * fan * rows // n_tile
    slots, lines = n_tile * cap, n_tables * rows
    chunk = -(-(2 * cap + N_COEF + 4 * levels) // 8) * 8
    owner, dest, table = owner_tile.T, dest_block.T, table_index.T
    exchange = lambda x, axis: lax.all_to_all(x, axis, split_axis=0, concat_axis=0, tiled=True)

    send, stepped = call(
        functools.partial(send_kernel, cap), 3, [((n_tile, chunk, width), F32), ((levels, rows, width), F32)]
    )(fields, coefficients, owner)
    got = exchange(send, "tile")
    arrive, collect, edge, back_hot = call(
        functools.partial(index_kernel, cap, rows, n_tables),
        3,
        [((slots, lines), F32), ((lines, slots), BF16), ((lines, 128), BF16), ((n_tables * 128, slots), BF16)],
        flops=1 << 28,
    )(owner, dest, table)
    part, whole = call(
        functools.partial(flux_kernel, cap), 6, [((n_sec, 2, rows, width), F32), ((levels, rows, width), F32)]
    )(got, collect, edge, tables, stepped, land_mask)
    parts = exchange(part, "sec")
    sea, back = call(functools.partial(sea_kernel, n_tables), 3, [((rows, width), F32), ((slots, width), F32)])(
        parts, land_mask, arrive
    )
    came = exchange(back.reshape(n_tile, cap, width), "tile").reshape(slots, width)
    (surface,) = call(surface_kernel, 4, [((rows, width), F32)])(came, back_hot, tables, sea)
    ocean_here = lax.axis_index("sec") == n_sec - 1
    forced = jnp.where(ocean_here, jnp.sum(parts, axis=0), whole[:2])
    return jnp.concatenate([forced, whole[2:]])[None], surface[None]


def solution(mesh):
    placed = (P("sec", None, "tile", None), P("sec", None, "tile", None), P(), P(), P(), P(), P("tile", None))
    return jax.shard_map(
        local,
        mesh=mesh,
        in_specs=placed,
        out_specs=(P("sec", None, "tile", None), P("sec", "tile", None)),
        check_vma=False,
    )
```

```python
import functools

import jax
import jax.numpy as jnp
from jax import lax
from jax.experimental import pallas as pl
from jax.experimental.pallas import tpu as pltpu
from jax.sharding import PartitionSpec as P

FORCING = 0.5
F32, BF16, I32 = jnp.float32, jnp.bfloat16, jnp.int32
N_COEF = 6
VMEM = pl.BlockSpec(memory_space=pltpu.VMEM)


def iota(shape, axis):
    return lax.broadcasted_iota(I32, shape, axis)


def roll(x, shift, axis):
    return pltpu.roll(x, shift % x.shape[axis], axis)


def split(x, parts):
    out = []
    for _ in range(parts):
        out.append(x.astype(BF16))
        x = x - out[-1].astype(F32)
    return out


def mm(a, b):
    return lax.dot_general(a, b, (((1,), (0,)), ((), ())), preferred_element_type=F32)


def mm_t(a, b):
    return lax.dot_general(a, b, (((1,), (1,)), ((), ())), preferred_element_type=F32)


def select_rows(hot, x, parts):
    return sum(mm(hot, p) for p in split(x, parts))


def product(a, b, dot):
    (a1, a2), (b1, b2) = split(a, 2), split(b, 2)
    rows = a.shape[0]
    both = dot(jnp.concatenate([a1, a2]), b1)
    return both[:rows] + both[rows:] + dot(a1, b2)


def sideways(x, kappa):
    return x + kappa * (roll(x, 1, x.ndim - 1) + roll(x, -1, x.ndim - 1) - 4.0 * x)


def substep(u, kappa, speed):
    rows = u.shape[1]
    row = iota(u.shape, 1)
    upper = jnp.where(row == 0, 0.0, roll(u, 1, 1))
    lower = jnp.where(row == rows - 1, 0.0, roll(u, -1, 1))
    laplace = upper + lower + roll(u, 1, 2) + roll(u, -1, 2) - 4.0 * u
    return u + kappa * laplace - 0.5 * speed * (lower - upper)


def place():
    sec, tile = lax.axis_index("sec"), lax.axis_index("tile")
    return sec, tile, sec < lax.axis_size("sec") - 1


def own_slots(owner_ref, rows, cap):
    sec, tile, atmos = place()
    n_sec, n_tile = lax.axis_size("sec"), lax.axis_size("tile")
    block = (jnp.minimum(sec, n_sec - 2) * n_tile + tile) * rows
    first = pl.multiple_of(block // 128 * 128, 128)
    half = block - first
    shape = (n_tile * cap, 128)
    lane = iota((1, 128), 1)
    inside = (lane >= half) & (lane < half + rows) & atmos
    owner = jnp.where(inside, owner_ref[:, pl.ds(first, 128)], -1)
    slot = iota(shape, 0)
    hot = [(owner[r : r + 1] == slot // cap).astype(F32) for r in range(owner.shape[0])]
    both = sum(hot)
    before = (iota((128, 128), 0) < iota((128, 128), 1)).astype(BF16)
    rank = mm(both.astype(BF16), before)
    placed = rank == (slot % cap).astype(F32)
    return first, [jnp.where(placed, h, 0.0) for h in hot]


def edge_rows(u, kappa, a, b):
    top, bot = slice(0, 1), slice(u.shape[0] - 1, u.shape[0])
    q_top = sideways(u[top], kappa[top]) + b[top] * u[1:2]
    q_bot = sideways(u[bot], kappa[bot]) + a[bot] * u[-2:-1]
    return [u[top], q_top, u[bot], q_bot]


def padded(lines, count, width):
    if count > len(lines):
        lines = lines + [jnp.zeros((count - len(lines), width), F32)]
    return jnp.concatenate(lines)


def placed_rows(placed, payload):
    return select_rows(sum(placed).astype(BF16), jnp.concatenate([payload] * (128 // payload.shape[0])), 3)


def send_kernel(cap, fields_hbm, coef_hbm, owner_hbm, send_ref, stepped_ref, fields_ref, coef_ref, owner_ref, sems):
    copies = [
        pltpu.make_async_copy(src, dst, sems.at[i])
        for i, (src, dst) in enumerate(((owner_hbm, owner_ref), (coef_hbm, coef_ref), (fields_hbm, fields_ref)))
    ]
    for copy in copies:
        copy.start()
    copies[0].wait()
    levels, rows, width = stepped_ref.shape
    _, placed = own_slots(owner_ref, rows, cap)
    copies[1].wait()
    copies[2].wait()
    u = fields_ref[0]
    kappa, speed = coef_ref[0, 0], coef_ref[0, 1]
    stepped = substep(substep(u, kappa, speed), kappa, speed)
    stepped_ref[...] = stepped
    n_tile = send_ref.shape[0]
    send_ref[:, :cap] = placed_rows(placed, stepped[0]).reshape(n_tile, cap, width)
    a = kappa + 0.5 * speed
    b = kappa - 0.5 * speed
    bot = slice(rows - 1, rows)
    extra = [a[0:1], a[0:1] * a[1:2], kappa[0:1], b[bot], b[bot] * b[rows - 2 : rows - 1], kappa[bot]]
    extra += edge_rows(u[0], kappa, a, b) + edge_rows(u[1], kappa, a, b)
    extra = padded(extra, send_ref.shape[1] - cap, width)
    send_ref[:, cap:] = jnp.broadcast_to(extra[None], (n_tile,) + extra.shape)


def swap_kernel(cap, fields_ref, coef_ref, owner_ref, stepped_ref, keep_ref, give_ref, slots_ref):
    _, tile, _ = place()
    levels, rows, width = stepped_ref.shape
    _, placed = own_slots(owner_ref, rows, cap)
    count = slots_ref.shape[0]
    slots_ref[...] = placed_rows(placed, stepped_ref[0] - stepped_ref[1]).reshape(count, cap, width)
    kappa, speed = coef_ref[0, 0], coef_ref[0, 1]
    a = kappa + 0.5 * speed
    b = kappa - 0.5 * speed
    extra = sum([edge_rows(fields_ref[0, l], kappa, a, b) for l in range(2, levels)], [])
    extra = padded(extra, keep_ref.shape[1] - cap, width)
    for m in range(count):
        ref = (keep_ref, give_ref)[m % 2]
        ref[m // 2, :cap] = slots_ref[tile ^ m]
        ref[m // 2, cap:] = extra


def index_kernel(cap, rows, n_tables, owner_ref, dest_ref, table_ref, arrive_ref, collect_ref, edge_ref, back_ref):
    sec, tile, atmos = place()
    n_sec, n_tile = lax.axis_size("sec"), lax.axis_size("tile")
    span = n_tile * rows
    start = jnp.minimum(sec, n_sec - 2) * span
    fan = owner_ref.shape[0]
    lines = n_tables * rows
    per = 128 // rows
    g, h = iota((128, 128), 0), iota((128, 128), 1)
    before = ((g < h) & (g // rows == h // rows)).astype(BF16)
    line = iota((lines, 128), 0)
    seat = iota((per * cap, 128), 0)
    lane = iota((per * cap, 128), 1)
    edges = jnp.zeros((lines, 128), F32)
    for group in range(span // 128):
        at = pl.ds(pl.multiple_of(start + group * 128, 128), 128)
        mine = [(owner_ref[r : r + 1, at] == tile) & atmos for r in range(fan)]
        key = jnp.full((1, 128), -1, I32)
        for r in range(fan):
            key = jnp.where(mine[r], table_ref[r : r + 1, at] * rows + dest_ref[r : r + 1, at], key)
        held = (key >= 0).astype(F32)
        rank = mm(jnp.broadcast_to(held, (16, 128)).astype(BF16), before)[:1]
        sits = (rank == (seat % cap).astype(F32)) & (lane // rows == seat // cap) & (held > 0)
        hit = (line == key).astype(BF16)
        arrive = mm_t(sits.astype(BF16), hit)
        arrive_ref[group * per * cap : (group + 1) * per * cap] = arrive
        block, within = group * per + g // rows, g % rows
        column = sum(jnp.where(within == w, i, 0) for i, w in enumerate((0, 1, rows - 2, rows - 1)))
        is_edge = (within < 2) | (within >= rows - 2)
        edges += mm(hit, (is_edge & (h == column * n_tile + block)).astype(BF16))
    arrive = arrive_ref[...]
    collect_ref[...] = arrive.T.astype(BF16)
    edge_ref[...] = edges.astype(BF16)
    first, placed = own_slots(owner_ref, rows, cap)
    table = table_ref[:, pl.ds(first, 128)]
    for k in range(n_tables):
        here = sum(jnp.where(table[r : r + 1] == k, placed[r], 0.0) for r in range(fan))
        back_ref[k * 128 : (k + 1) * 128] = here.T.astype(BF16)


def shifted(x, by):
    row = iota(x.shape, 0)
    return jnp.where(row == (0 if by > 0 else x.shape[0] - 1), 0.0, roll(x, by, 0))


def corrections(coef, edges):
    a0, aa, k0, b1, bb, k1 = coef
    u0, q0, u1, q1 = edges
    b_prev, a_next = shifted(b1, 1), shifted(a0, -1)
    u_prev, q_prev, u_next, q_next = shifted(u1, 1), shifted(q1, 1), shifted(u0, -1), shifted(q0, -1)
    return [
        sideways(a0 * u_prev, k0) + a0 * (q_prev + b_prev * u0),
        aa * u_prev,
        bb * u_next,
        sideways(b1 * u_next, k1) + b1 * (q_next + a_next * u1),
    ]


def whole_level(plane, correction):
    _, tile, _ = place()
    rows = plane.shape[0]
    here = iota(correction[0].shape, 0) == tile
    own = [jnp.sum(jnp.where(here, c, 0.0), axis=0, keepdims=True) for c in correction]
    return jnp.concatenate(
        [plane[:2] + jnp.concatenate(own[:2]), plane[2 : rows - 2], plane[rows - 2 :] + jnp.concatenate(own[2:])]
    )


def flux_of(slots, correction, collect, edge, tables_ref, rows):
    width = slots.shape[1]
    if correction.shape[0] < 128:
        correction = jnp.concatenate([correction, jnp.zeros((128 - correction.shape[0], width), F32)])
    grouped = select_rows(collect, slots, 2) + select_rows(edge, correction, 2)
    flux = jnp.zeros((rows, width), F32)
    for k in range(tables_ref.shape[0]):
        flux += product(grouped[k * rows : (k + 1) * rows], tables_ref[k], mm)
    return flux


def lines_of(ref, first, count):
    return [ref[:, first + i, :] for i in range(count)]


def flux_kernel(cap, got_ref, collect_ref, edge_ref, tables_ref, stepped_ref, mask_ref, part_ref, whole_ref):
    _, _, atmos = place()
    n_tile, _, width = got_ref.shape
    rows = stepped_ref.shape[1]
    correction = corrections(lines_of(got_ref, cap, N_COEF), lines_of(got_ref, cap + N_COEF, 4))
    whole = whole_level(stepped_ref[0], correction)
    whole_ref[...] = whole
    slots = got_ref[:, :cap, :].reshape(n_tile * cap, width)
    flux = flux_of(slots, jnp.concatenate(correction), collect_ref[...], edge_ref[...], tables_ref, rows)
    part = jnp.where(atmos, FORCING * mask_ref[...].astype(F32) * flux, whole)
    for s in range(part_ref.shape[0]):
        part_ref[s] = part


def second_kernel(cap, sources, got_ref, collect_ref, edge_ref, tables_ref, stepped_ref, mask_ref, *refs):
    swapped, (part_ref, whole_ref, came_ref) = refs[:-3], refs[-3:]
    _, tile, _ = place()
    n_tile, _, width = got_ref.shape
    levels, rows, _ = stepped_ref.shape
    for m, (i, j) in enumerate(sources):
        came_ref[tile ^ m] = swapped[i][j]
    coef = lines_of(got_ref, cap, N_COEF)
    first, second = [corrections(coef, lines_of(got_ref, cap + N_COEF + 4 * l, 4)) for l in range(2)]
    whole_ref[0] = whole_level(stepped_ref[1], second)
    for l in range(2, levels):
        whole_ref[l - 1] = whole_level(stepped_ref[l], corrections(coef, lines_of(came_ref, cap + 4 * (l - 2), 4)))
    slots = came_ref[:, :cap, :].reshape(n_tile * cap, width)
    correction = jnp.concatenate([x - y for x, y in zip(first, second)])
    flux = flux_of(slots, correction, collect_ref[...], edge_ref[...], tables_ref, rows)
    part_ref[...] = FORCING * mask_ref[...].astype(F32) * flux


def sea_kernel(n_tables, parts_ref, mask_ref, arrive_ref, top_ref, sea_ref, back_ref):
    top = parts_ref[0]
    for s in range(1, parts_ref.shape[0]):
        top += parts_ref[s]
    top_ref[...] = top
    sea = mask_ref[...].astype(F32) * top
    sea_ref[...] = sea
    back_ref[...] = select_rows(arrive_ref[...].astype(BF16), jnp.concatenate([sea] * n_tables), 3)


def surface_kernel(came_ref, back_ref, tables_ref, sea_ref, out_ref):
    sec, tile, atmos = place()
    rows, width = sea_ref.shape
    picked = select_rows(back_ref[...], came_ref[...], 2)
    seen = jnp.zeros((rows, width), F32)
    for k in range(tables_ref.shape[0]):
        lines = picked[k * 128 : (k + 1) * 128]
        lines = sum(lines[i : i + rows] for i in range(0, 128, rows))
        seen += product(lines, tables_ref[k], mm_t)
    out_ref[...] = jnp.where(atmos, seen, sea_ref[...])


def call(kernel, n_in, outs, flops=0, scratch=(), space=pltpu.VMEM, vmem=32):
    shapes = [jax.ShapeDtypeStruct(s, d) for s, d in outs]
    return pl.pallas_call(
        kernel,
        out_shape=shapes,
        in_specs=[pl.BlockSpec(memory_space=space)] * n_in,
        out_specs=[VMEM] * len(shapes),
        scratch_shapes=scratch,
        compiler_params=pltpu.CompilerParams(vmem_limit_bytes=vmem * 1024 * 1024),
        cost_estimate=pl.CostEstimate(flops=flops, bytes_accessed=1 << 20, transcendentals=0),
    )


def swap_stage(bit, arrays, chunks, after=None):
    n_tile = lax.axis_size("tile")
    going = [m for m in range(n_tile) if m & bit]
    if after is not None:
        arrays, after = lax.optimization_barrier((arrays, after))
    if bit == 1:
        give = arrays.pop()
    else:
        give = jnp.stack([arrays[chunks[m][0]][chunks[m][1]] for m in going])
    came = lax.ppermute(give, "tile", [(t, t ^ bit) for t in range(n_tile)])
    chunks = chunks | {m: (len(arrays), i) for i, m in enumerate(going)}
    return arrays + [came], chunks, after


def local(fields, coefficients, owner_tile, dest_block, table_index, tables, land_mask):
    n_sec, n_tile = lax.axis_size("sec"), lax.axis_size("tile")
    levels, rows, width = fields.shape[1:]
    fan = owner_tile.shape[1]
    n_tables = tables.shape[0]
    cap = 2 * fan * rows // n_tile
    slots, lines = n_tile * cap, n_tables * rows
    up8 = lambda n: -(-n // 8) * 8
    chunk, side = up8(cap + N_COEF + 8), up8(cap + 4 * (levels - 2))
    owner, dest, table = owner_tile.T, dest_block.T, table_index.T
    exchange = lambda x, axis: lax.all_to_all(x, axis, split_axis=0, concat_axis=0, tiled=True)
    plane = ((rows, width), F32)

    send, stepped = call(
        functools.partial(send_kernel, cap),
        3,
        [((n_tile, chunk, width), F32), ((levels, rows, width), F32)],
        scratch=[
            pltpu.VMEM(fields.shape, F32),
            pltpu.VMEM(coefficients.shape, F32),
            pltpu.VMEM(owner.shape, I32),
            pltpu.SemaphoreType.DMA((3,)),
        ],
        space=pltpu.HBM,
        vmem=60,
    )(fields, coefficients, owner)
    got = exchange(send, "tile")
    keep, give = call(
        functools.partial(swap_kernel, cap),
        4,
        [((n_tile // 2, side, width), F32)] * 2,
        scratch=[pltpu.VMEM((n_tile, cap, width), F32)],
    )(fields, coefficients, owner, stepped)
    arrays, chunks, _ = swap_stage(1, [keep, give], {m: (0, m // 2) for m in range(0, n_tile, 2)})
    arrays, chunks, _ = swap_stage(2, arrays, chunks)
    arrive, collect, edge, back_hot = call(
        functools.partial(index_kernel, cap, rows, n_tables),
        3,
        [((slots, lines), F32), ((lines, slots), BF16), ((lines, 128), BF16), ((n_tables * 128, slots), BF16)],
        flops=1 << 28,
    )(owner, dest, table)
    part, whole = call(functools.partial(flux_kernel, cap), 6, [((n_sec, rows, width), F32), plane])(
        got, collect, edge, tables, stepped, land_mask
    )
    parts = exchange(part, "sec")
    bit = 4
    while bit < n_tile:
        arrays, chunks, part = swap_stage(bit, arrays, chunks, part)
        bit *= 2
    sources = [chunks[m] for m in range(n_tile)]
    top, sea, back = call(functools.partial(sea_kernel, n_tables), 3, [plane, plane, ((slots, width), F32)])(
        parts, land_mask, arrive
    )
    came = exchange(back.reshape(n_tile, cap, width), "tile").reshape(slots, width)
    arrays, _ = lax.optimization_barrier((arrays, back))
    second, others = call(
        functools.partial(second_kernel, cap, sources),
        6 + len(arrays),
        [plane, ((levels - 1, rows, width), F32)],
        scratch=[pltpu.VMEM((n_tile, side, width), F32)],
        flops=1 << 34,
    )(got, collect, edge, tables, stepped, land_mask, *arrays)
    seconds = [lax.ppermute(second, "sec", [(s, n_sec - 1)]) for s in range(n_sec - 1)]
    (surface,) = call(surface_kernel, 4, [plane])(came, back_hot, tables, sea)
    seconds, surface = lax.optimization_barrier((seconds, surface))
    ocean_here = lax.axis_index("sec") == n_sec - 1
    ended0 = jnp.where(ocean_here, top, whole)
    ended1 = jnp.where(ocean_here, others[0] + sum(seconds), others[0])
    return jnp.concatenate([ended0[None], ended1[None], others[1:]])[None], surface[None]


def solution(mesh):
    placed = (P("sec", None, "tile", None), P("sec", None, "tile", None), P(), P(), P(), P(), P("tile", None))
    return jax.shard_map(
        local,
        mesh=mesh,
        in_specs=placed,
        out_specs=(P("sec", None, "tile", None), P("sec", "tile", None)),
        check_vma=False,
    )
```

```python
import functools

import jax
import jax.numpy as jnp
from jax import lax
from jax.experimental import pallas as pl
from jax.experimental.pallas import tpu as pltpu
from jax.sharding import PartitionSpec as P

FORCING = 0.5
F32, BF16, I32 = jnp.float32, jnp.bfloat16, jnp.int32
N_COEF = 6
PLAN_COLLECT, PLAN_EDGE, PLAN_BACK, PLAN_WATER, PLAN_WAYS = 0, 1, 2, 3, 4


def iota(shape, axis):
    return lax.broadcasted_iota(I32, shape, axis)


def roll(x, shift, axis):
    return pltpu.roll(x, shift % x.shape[axis], axis)


def split(x, parts):
    out = []
    for _ in range(parts):
        out.append(x.astype(BF16))
        x = x - out[-1].astype(F32)
    return out


def mm(a, b):
    return lax.dot_general(a, b, (((1,), (0,)), ((), ())), preferred_element_type=F32)


def mm_0(a, b):
    return lax.dot_general(a, b, (((0,), (0,)), ((), ())), preferred_element_type=F32)


def mm_t(a, b):
    return lax.dot_general(a, b, (((1,), (1,)), ((), ())), preferred_element_type=F32)


def select_rows(hot, x, parts, dot=mm):
    return sum(dot(hot, p) for p in split(x, parts))


def product(a, b1, b2, dot=mm):
    a1, a2 = split(a, 2)
    rows = a.shape[0]
    both = dot(jnp.concatenate([a1, a2]), b1)
    return both[:rows] + both[rows:] + dot(a1, b2)


def sideways(x, kappa):
    return x + kappa * (roll(x, 1, x.ndim - 1) + roll(x, -1, x.ndim - 1) - 4.0 * x)


def substep(u, kappa, speed):
    rows = u.shape[1]
    row = iota(u.shape, 1)
    upper = jnp.where(row == 0, 0.0, roll(u, 1, 1))
    lower = jnp.where(row == rows - 1, 0.0, roll(u, -1, 1))
    laplace = upper + lower + roll(u, 1, 2) + roll(u, -1, 2) - 4.0 * u
    return u + kappa * laplace - 0.5 * speed * (lower - upper)


def place():
    sec, tile = lax.axis_index("sec"), lax.axis_index("tile")
    return sec, tile, sec < lax.axis_size("sec") - 1


def own_slots(owner_ref, rows, cap):
    sec, tile, atmos = place()
    n_sec, n_tile = lax.axis_size("sec"), lax.axis_size("tile")
    block = (jnp.minimum(sec, n_sec - 2) * n_tile + tile) * rows
    first = pl.multiple_of(block // 128 * 128, 128)
    half = block - first
    shape = (n_tile * cap, 128)
    lane = iota((1, 128), 1)
    inside = (lane >= half) & (lane < half + rows) & atmos
    owner = jnp.where(inside, owner_ref[:, pl.ds(first, 128)], -1)
    slot = iota(shape, 0)
    hot = [(owner[r : r + 1] == slot // cap).astype(F32) for r in range(owner.shape[0])]
    both = sum(hot)
    before = (iota((128, 128), 0) < iota((128, 128), 1)).astype(BF16)
    rank = mm(both.astype(BF16), before)
    placed = rank == (slot % cap).astype(F32)
    return first, [jnp.where(placed, h, 0.0) for h in hot]


def edge_rows(u, kappa, a, b):
    top, bot = slice(0, 1), slice(u.shape[0] - 1, u.shape[0])
    q_top = sideways(u[top], kappa[top]) + b[top] * u[1:2]
    q_bot = sideways(u[bot], kappa[bot]) + a[bot] * u[-2:-1]
    return [u[top], q_top, u[bot], q_bot]


def padded(lines, count, width):
    if count > len(lines):
        lines = lines + [jnp.zeros((count - len(lines), width), F32)]
    return jnp.concatenate(lines)


def placed_rows(placed, payload):
    return select_rows(sum(placed).astype(BF16), jnp.concatenate([payload] * (128 // payload.shape[0])), 3)


def send_kernel(cap, fields_hbm, coef_hbm, owner_hbm, send_ref, fields_ref, coef_ref, owner_ref, sems):
    pairs = ((owner_hbm, owner_ref), (coef_hbm.at[0], coef_ref), (fields_hbm.at[0, pl.ds(0, 2)], fields_ref))
    copies = [pltpu.make_async_copy(src, dst, sems.at[i]) for i, (src, dst) in enumerate(pairs)]
    for copy in copies:
        copy.start()
    copies[0].wait()
    _, rows, width = fields_ref.shape
    _, placed = own_slots(owner_ref, rows, cap)
    copies[1].wait()
    copies[2].wait()
    u = fields_ref[...]
    kappa, speed = coef_ref[0], coef_ref[1]
    stepped = substep(substep(u[:1], kappa, speed), kappa, speed)[0]
    n_tile = send_ref.shape[0]
    send_ref[:, :cap] = placed_rows(placed, stepped).reshape(n_tile, cap, width)
    a = kappa + 0.5 * speed
    b = kappa - 0.5 * speed
    bot = slice(rows - 1, rows)
    extra = [a[0:1], a[0:1] * a[1:2], kappa[0:1], b[bot], b[bot] * b[rows - 2 : rows - 1], kappa[bot]]
    extra += edge_rows(u[0], kappa, a, b) + edge_rows(u[1], kappa, a, b)
    extra = padded(extra, send_ref.shape[1] - cap, width)
    send_ref[:, cap:] = jnp.broadcast_to(extra[None], (n_tile,) + extra.shape)


def swap_kernel(cap, fields_ref, coef_ref, owner_ref, keep_ref, give_ref, slots_ref):
    _, tile, _ = place()
    levels, rows, width = fields_ref.shape[1:]
    _, placed = own_slots(owner_ref, rows, cap)
    kappa, speed = coef_ref[0, 0], coef_ref[0, 1]
    stepped = substep(substep(fields_ref[0, :2], kappa, speed), kappa, speed)
    count, side = slots_ref.shape[0], keep_ref.shape[1]
    for i in range(0, rows, side):
        keep_ref[count // 2 + i // side, : min(side, rows - i)] = stepped[0, i : i + side]
    slots_ref[...] = placed_rows(placed, stepped[0] - stepped[1]).reshape(count, cap, width)
    a = kappa + 0.5 * speed
    b = kappa - 0.5 * speed
    extra = sum([edge_rows(fields_ref[0, l], kappa, a, b) for l in range(2, levels)], [])
    extra = padded(extra, keep_ref.shape[1] - cap, width)
    for m in range(count):
        ref = (keep_ref, give_ref)[m % 2]
        ref[m // 2, :cap] = slots_ref[tile ^ m]
        ref[m // 2, cap:] = extra


def stack_kernel(picks, *refs):
    out_ref = refs[-1]
    for to, (i, j) in enumerate(picks):
        out_ref[to] = refs[i][j]


def index_kernel(
    cap, rows, owner_ref, dest_ref, table_ref, tables_ref, mask_ref, plan_ref, arrive_sum
):
    n_tables = tables_ref.shape[0]
    plan_ref[PLAN_WATER, :rows] = mask_ref[...].astype(F32).astype(BF16)
    for k in range(n_tables):
        at = PLAN_WAYS + 2 * k
        plan_ref[at], plan_ref[at + 1] = split(tables_ref[k], 2)
    sec, tile, atmos = place()
    n_sec, n_tile = lax.axis_size("sec"), lax.axis_size("tile")
    span = n_tile * rows
    start = jnp.minimum(sec, n_sec - 2) * span
    fan = owner_ref.shape[0]
    lines = n_tables * rows
    per = 128 // rows
    g, h = iota((128, 128), 0), iota((128, 128), 1)
    before = ((g < h) & (g // rows == h // rows)).astype(BF16)
    line = iota((lines, 128), 0)
    seat = iota((per * cap, 128), 0)
    lane = iota((per * cap, 128), 1)
    edges = jnp.zeros((lines, 128), F32)
    for group in range(span // 128):
        at = pl.ds(pl.multiple_of(start + group * 128, 128), 128)
        mine = [(owner_ref[r : r + 1, at] == tile) & atmos for r in range(fan)]
        key = jnp.full((1, 128), -1, I32)
        for r in range(fan):
            key = jnp.where(mine[r], table_ref[r : r + 1, at] * rows + dest_ref[r : r + 1, at], key)
        held = (key >= 0).astype(F32)
        rank = mm(jnp.broadcast_to(held, (16, 128)).astype(BF16), before)[:1]
        sits = (rank == (seat % cap).astype(F32)) & (lane // rows == seat // cap) & (held > 0)
        hit = (line == key).astype(BF16)
        arrive = mm_t(sits.astype(BF16), hit)
        arrive_sum[group * per * cap : (group + 1) * per * cap] = arrive
        block, within = group * per + g // rows, g % rows
        column = sum(jnp.where(within == w, i, 0) for i, w in enumerate((0, 1, rows - 2, rows - 1)))
        is_edge = (within < 2) | (within >= rows - 2)
        edges += mm(hit, (is_edge & (h == column * n_tile + block)).astype(BF16))
    arrive = arrive_sum[...]
    plan_ref[PLAN_COLLECT] = arrive.T.astype(BF16)
    plan_ref[PLAN_EDGE, :, :128] = edges.astype(BF16)
    plan_ref[PLAN_EDGE, :, 128:] = jnp.zeros((lines, plan_ref.shape[2] - 128), BF16)
    first, placed = own_slots(owner_ref, rows, cap)
    table = table_ref[:, pl.ds(first, 128)]
    for k in range(n_tables):
        here = sum(jnp.where(table[r : r + 1] == k, placed[r], 0.0) for r in range(fan))
        here = here.T
        plan_ref[PLAN_BACK, k * rows : (k + 1) * rows] = sum(here[i : i + rows] for i in range(0, 128, rows)).astype(BF16)


def shifted(x, by):
    row = iota(x.shape, 0)
    return jnp.where(row == (0 if by > 0 else x.shape[0] - 1), 0.0, roll(x, by, 0))


def corrections(coef, edges):
    a0, aa, k0, b1, bb, k1 = coef
    u0, q0, u1, q1 = edges
    b_prev, a_next = shifted(b1, 1), shifted(a0, -1)
    u_prev, q_prev, u_next, q_next = shifted(u1, 1), shifted(q1, 1), shifted(u0, -1), shifted(q0, -1)
    return [
        sideways(a0 * u_prev, k0) + a0 * (q_prev + b_prev * u0),
        aa * u_prev,
        bb * u_next,
        sideways(b1 * u_next, k1) + b1 * (q_next + a_next * u1),
    ]


def whole_level(plane, correction):
    _, tile, _ = place()
    rows = plane.shape[0]
    here = iota(correction[0].shape, 0) == tile
    own = [jnp.sum(jnp.where(here, c, 0.0), axis=0, keepdims=True) for c in correction]
    return jnp.concatenate(
        [plane[:2] + jnp.concatenate(own[:2]), plane[2 : rows - 2], plane[rows - 2 :] + jnp.concatenate(own[2:])]
    )


def water(plan_ref, rows):
    return plan_ref[PLAN_WATER, :rows].astype(F32)


def flux_of(slots, correction, plan_ref, n_tables, rows):
    width = slots.shape[1]
    if correction.shape[0] < 128:
        correction = jnp.concatenate([correction, jnp.zeros((128 - correction.shape[0], width), F32)])
    grouped = select_rows(plan_ref[PLAN_COLLECT], slots, 2) + select_rows(plan_ref[PLAN_EDGE, :, :128], correction, 2)
    flux = jnp.zeros((rows, width), F32)
    for k in range(n_tables):
        at = PLAN_WAYS + 2 * k
        flux += product(grouped[k * rows : (k + 1) * rows], plan_ref[at], plan_ref[at + 1])
    return flux


def lines_of(ref, first, count):
    return [ref[:, first + i, :] for i in range(count)]


def flux_kernel(cap, n_tables, got_ref, plan_ref, keep_ref, part_ref, whole_ref):
    _, _, atmos = place()
    n_tile, _, width = got_ref.shape
    rows, side = whole_ref.shape[0], keep_ref.shape[1]
    stepped = jnp.concatenate([keep_ref[n_tile // 2 + i // side, : min(side, rows - i)] for i in range(0, rows, side)])
    correction = corrections(lines_of(got_ref, cap, N_COEF), lines_of(got_ref, cap + N_COEF, 4))
    whole = whole_level(stepped, correction)
    whole_ref[...] = whole
    slots = got_ref[:, :cap, :].reshape(n_tile * cap, width)
    flux = flux_of(slots, jnp.concatenate(correction), plan_ref, n_tables, rows)
    part = jnp.where(atmos, FORCING * water(plan_ref, rows) * flux, whole)
    for s in range(part_ref.shape[0]):
        part_ref[s] = part


def second_kernel(cap, n_tables, sources, got_ref, plan_ref, fields_ref, coef_ref, *refs):
    swapped, (part_ref, whole_ref, came_ref) = refs[:-3], refs[-3:]
    _, tile, _ = place()
    n_tile, _, width = got_ref.shape
    levels, rows, _ = fields_ref.shape[1:]
    kappa, speed = coef_ref[0, 0], coef_ref[0, 1]
    stepped = substep(substep(fields_ref[0, 1:], kappa, speed), kappa, speed)
    for m, (i, j) in enumerate(sources):
        came_ref[tile ^ m] = swapped[i][j]
    coef = lines_of(got_ref, cap, N_COEF)
    first, second = [corrections(coef, lines_of(got_ref, cap + N_COEF + 4 * l, 4)) for l in range(2)]
    whole_ref[0] = whole_level(stepped[0], second)
    for l in range(2, levels):
        whole_ref[l - 1] = whole_level(stepped[l - 1], corrections(coef, lines_of(came_ref, cap + 4 * (l - 2), 4)))
    slots = came_ref[:, :cap, :].reshape(n_tile * cap, width)
    correction = jnp.concatenate([x - y for x, y in zip(first, second)])
    flux = flux_of(slots, correction, plan_ref, n_tables, rows)
    part_ref[...] = FORCING * water(plan_ref, rows) * flux


def sea_kernel(n_tables, plan_ref, parts_ref, whole_ref, first_ref, back_ref):
    _, _, atmos = place()
    top = sum(parts_ref[s] for s in range(parts_ref.shape[0]))
    first_ref[...] = jnp.where(atmos, whole_ref[...], top)
    sea = water(plan_ref, top.shape[0]) * top
    back_ref[...] = select_rows(plan_ref[PLAN_COLLECT], jnp.concatenate([sea] * n_tables), 3, mm_0)


def end_kernel(n_tables, came_ref, plan_ref, first_ref, others_ref, *refs):
    seconds, (fields_hbm, surface_hbm, second_ref, surface_ref, sems) = refs[:-5], refs[-5:]
    _, _, atmos = place()
    rows, width = first_ref.shape
    second_ref[...] = jnp.where(atmos, others_ref[0], others_ref[0] + sum(x[...] for x in seconds))
    levels = others_ref.shape[0] + 1
    copies = [
        pltpu.make_async_copy(first_ref, fields_hbm.at[0, 0], sems.at[0]),
        pltpu.make_async_copy(second_ref, fields_hbm.at[0, 1], sems.at[1]),
        pltpu.make_async_copy(others_ref.at[pl.ds(1, levels - 2)], fields_hbm.at[0, pl.ds(2, levels - 2)], sems.at[2]),
        pltpu.make_async_copy(surface_ref, surface_hbm.at[0], sems.at[3]),
    ]
    for copy in copies[:3]:
        copy.start()
    picked = select_rows(plan_ref[PLAN_BACK], came_ref[...], 2)
    seen = jnp.zeros((rows, width), F32)
    for k in range(n_tables):
        at = PLAN_WAYS + 2 * k
        seen += product(picked[k * rows : (k + 1) * rows], plan_ref[at], plan_ref[at + 1], mm_t)
    surface_ref[...] = jnp.where(atmos, seen, water(plan_ref, rows) * first_ref[...])
    copies[3].start()
    for copy in copies:
        copy.wait()


def call(kernel, n_in, outs, flops=0, scratch=(), space=pltpu.VMEM, out_space=pltpu.VMEM, vmem=12):
    shapes = [jax.ShapeDtypeStruct(s, d) for s, d in outs]
    return pl.pallas_call(
        kernel,
        out_shape=shapes,
        in_specs=[pl.BlockSpec(memory_space=space)] * n_in,
        out_specs=[pl.BlockSpec(memory_space=out_space)] * len(shapes),
        scratch_shapes=scratch,
        compiler_params=pltpu.CompilerParams(vmem_limit_bytes=vmem * 1024 * 1024),
        cost_estimate=pl.CostEstimate(flops=flops, bytes_accessed=1 << 10, transcendentals=0),
    )


def swap_stage(bit, arrays, chunks, after=None, flops=0):
    n_tile = lax.axis_size("tile")
    going = [m for m in range(n_tile) if m & bit]
    keep_shape = arrays[0].shape[1:]
    if after is not None:
        arrays, after = lax.optimization_barrier((arrays, after))
    if bit == 1:
        give = arrays.pop()
    else:
        picks = [chunks[m] for m in going]
        used = sorted({i for i, _ in picks})
        picks = [(used.index(i), j) for i, j in picks]
        taken = [arrays[i] for i in used]
        (give,) = call(functools.partial(stack_kernel, picks), len(used), [((len(going),) + keep_shape, F32)], flops=flops)(*taken)
    came = lax.ppermute(give, "tile", [(t, t ^ bit) for t in range(n_tile)])
    chunks = chunks | {m: (len(arrays), i) for i, m in enumerate(going)}
    return arrays + [came], chunks, after


def local(fields, coefficients, owner_tile, dest_block, table_index, tables, land_mask):
    n_sec, n_tile = lax.axis_size("sec"), lax.axis_size("tile")
    levels, rows, width = fields.shape[1:]
    fan = owner_tile.shape[1]
    n_tables = tables.shape[0]
    cap = 2 * fan * rows // n_tile
    slots, lines = n_tile * cap, n_tables * rows
    up8 = lambda n: -(-n // 8) * 8
    chunk, side = up8(cap + N_COEF + 8), up8(cap + 4 * (levels - 2))
    owner, dest, table = owner_tile.T, dest_block.T, table_index.T
    exchange = lambda x, axis: lax.all_to_all(x, axis, split_axis=0, concat_axis=0, tiled=True)
    plane = ((rows, width), F32)

    (send,) = call(
        functools.partial(send_kernel, cap),
        3,
        [((n_tile, chunk, width), F32)],
        scratch=[
            pltpu.VMEM((2, rows, width), F32),
            pltpu.VMEM((2, rows, width), F32),
            pltpu.VMEM(owner.shape, I32),
            pltpu.SemaphoreType.DMA((3,)),
        ],
        space=pltpu.HBM,
        vmem=60,
    )(fields, coefficients, owner)
    got = exchange(send, "tile")
    keep, give = call(
        functools.partial(swap_kernel, cap),
        3,
        [((n_tile // 2 - -rows // side, side, width), F32), ((n_tile // 2, side, width), F32)],
        scratch=[pltpu.VMEM((n_tile, cap, width), F32)],
    )(fields, coefficients, owner)
    arrays, chunks, _ = swap_stage(1, [keep, give], {m: (0, m // 2) for m in range(0, n_tile, 2)})
    (plan,) = call(
        functools.partial(index_kernel, cap, rows),
        5,
        [((PLAN_WAYS + 2 * n_tables, lines, width), BF16)],
        scratch=[pltpu.VMEM((slots, lines), F32)],
    )(owner, dest, table, tables, land_mask)
    arrays, chunks, plan = swap_stage(2, arrays, chunks, plan)
    part, whole = call(functools.partial(flux_kernel, cap, n_tables), 3, [((n_sec, rows, width), F32), plane])(got, plan, keep)
    parts = exchange(part, "sec")
    bit = 4
    while bit < n_tile:
        arrays, chunks, part = swap_stage(bit, arrays, chunks, part)
        bit *= 2
    sources = [chunks[m] for m in range(n_tile)]
    first, back = call(functools.partial(sea_kernel, n_tables), 3, [plane, ((slots, width), F32)])(plan, parts, whole)
    came = exchange(back.reshape(n_tile, cap, width), "tile").reshape(slots, width)
    second, others = call(
        functools.partial(second_kernel, cap, n_tables, sources),
        4 + len(arrays),
        [plane, ((levels - 1, rows, width), F32)],
        scratch=[pltpu.VMEM((n_tile, side, width), F32)],
        flops=1 << 34,
    )(got, plan, fields, coefficients, *arrays)
    seconds = [lax.ppermute(second, "sec", [(s, n_sec - 1)]) for s in range(n_sec - 1)]
    return call(
        functools.partial(end_kernel, n_tables),
        4 + len(seconds),
        [(fields.shape, F32), ((1, rows, width), F32)],
        scratch=[pltpu.VMEM((rows, width), F32)] * 2 + [pltpu.SemaphoreType.DMA((4,))],
        out_space=pltpu.HBM,
    )(came, plan, first, others, *seconds)


def solution(mesh):
    placed = (P("sec", None, "tile", None), P("sec", None, "tile", None), P(), P(), P(), P(), P("tile", None))
    return jax.shard_map(
        local,
        mesh=mesh,
        in_specs=placed,
        out_specs=(P("sec", None, "tile", None), P("sec", "tile", None)),
        check_vma=False,
    )
```

```python
import functools

import jax
import jax.numpy as jnp
from jax import lax
from jax.experimental import pallas as pl
from jax.experimental.pallas import tpu as pltpu
from jax.sharding import PartitionSpec as P

FORCING = 0.5
F32, BF16, I32 = jnp.float32, jnp.bfloat16, jnp.int32
N_COEF = 6
PLAN_COLLECT, PLAN_EDGE, PLAN_BACK, PLAN_WATER, PLAN_WAYS = 0, 1, 2, 3, 4


def iota(shape, axis):
    return lax.broadcasted_iota(I32, shape, axis)


def roll(x, shift, axis):
    return pltpu.roll(x, shift % x.shape[axis], axis)


def split(x, parts):
    out = []
    for _ in range(parts):
        out.append(x.astype(BF16))
        x = x - out[-1].astype(F32)
    return out


def mm(a, b):
    return lax.dot_general(a, b, (((1,), (0,)), ((), ())), preferred_element_type=F32)


def mm_0(a, b):
    return lax.dot_general(a, b, (((0,), (0,)), ((), ())), preferred_element_type=F32)


def mm_t(a, b):
    return lax.dot_general(a, b, (((1,), (1,)), ((), ())), preferred_element_type=F32)


def select_rows(hot, x, parts, dot=mm):
    return sum(dot(hot, p) for p in split(x, parts))


def product(a, b1, b2, dot=mm):
    a1, a2 = split(a, 2)
    rows = a.shape[0]
    both = dot(jnp.concatenate([a1, a2]), b1)
    return both[:rows] + both[rows:] + dot(a1, b2)


def sideways(x, kappa):
    return x + kappa * (roll(x, 1, x.ndim - 1) + roll(x, -1, x.ndim - 1) - 4.0 * x)


def substep(u, kappa, speed):
    rows = u.shape[1]
    row = iota(u.shape, 1)
    upper = jnp.where(row == 0, 0.0, roll(u, 1, 1))
    lower = jnp.where(row == rows - 1, 0.0, roll(u, -1, 1))
    laplace = upper + lower + roll(u, 1, 2) + roll(u, -1, 2) - 4.0 * u
    return u + kappa * laplace - 0.5 * speed * (lower - upper)


def place():
    sec, tile = lax.axis_index("sec"), lax.axis_index("tile")
    return sec, tile, sec < lax.axis_size("sec") - 1


def own_slots(owner_ref, rows, cap):
    sec, tile, atmos = place()
    n_sec, n_tile = lax.axis_size("sec"), lax.axis_size("tile")
    block = (jnp.minimum(sec, n_sec - 2) * n_tile + tile) * rows
    first = pl.multiple_of(block // 128 * 128, 128)
    half = block - first
    shape = (n_tile * cap, 128)
    lane = iota((1, 128), 1)
    inside = (lane >= half) & (lane < half + rows) & atmos
    owner = jnp.where(inside, owner_ref[:, pl.ds(first, 128)], -1)
    slot = iota(shape, 0)
    hot = [(owner[r : r + 1] == slot // cap).astype(F32) for r in range(owner.shape[0])]
    both = sum(hot)
    before = (iota((128, 128), 0) < iota((128, 128), 1)).astype(BF16)
    rank = mm(both.astype(BF16), before)
    placed = rank == (slot % cap).astype(F32)
    return first, [jnp.where(placed, h, 0.0) for h in hot]


def edge_rows(u, kappa, a, b):
    top, bot = slice(0, 1), slice(u.shape[0] - 1, u.shape[0])
    q_top = sideways(u[top], kappa[top]) + b[top] * u[1:2]
    q_bot = sideways(u[bot], kappa[bot]) + a[bot] * u[-2:-1]
    return [u[top], q_top, u[bot], q_bot]


def padded(lines, count, width):
    if count > len(lines):
        lines = lines + [jnp.zeros((count - len(lines), width), F32)]
    return jnp.concatenate(lines)


def placed_rows(placed, payload):
    return select_rows(sum(placed).astype(BF16), jnp.concatenate([payload] * (128 // payload.shape[0])), 3)


def send_kernel(cap, fields_hbm, coef_hbm, owner_hbm, send_ref, fields_ref, coef_ref, owner_ref, sems):
    pairs = ((owner_hbm, owner_ref), (coef_hbm.at[0], coef_ref), (fields_hbm.at[0, pl.ds(0, 2)], fields_ref))
    copies = [pltpu.make_async_copy(src, dst, sems.at[i]) for i, (src, dst) in enumerate(pairs)]
    for copy in copies:
        copy.start()
    copies[0].wait()
    _, rows, width = fields_ref.shape
    _, placed = own_slots(owner_ref, rows, cap)
    copies[1].wait()
    copies[2].wait()
    u = fields_ref[...]
    kappa, speed = coef_ref[0], coef_ref[1]
    stepped = substep(substep(u[:1], kappa, speed), kappa, speed)[0]
    n_tile = send_ref.shape[0]
    send_ref[:, :cap] = placed_rows(placed, stepped).reshape(n_tile, cap, width)
    a = kappa + 0.5 * speed
    b = kappa - 0.5 * speed
    bot = slice(rows - 1, rows)
    extra = [a[0:1], a[0:1] * a[1:2], kappa[0:1], b[bot], b[bot] * b[rows - 2 : rows - 1], kappa[bot]]
    extra += edge_rows(u[0], kappa, a, b) + edge_rows(u[1], kappa, a, b)
    extra = padded(extra, send_ref.shape[1] - cap, width)
    send_ref[:, cap:] = jnp.broadcast_to(extra[None], (n_tile,) + extra.shape)


def swap_kernel(cap, fields_ref, coef_ref, owner_ref, keep_ref, give_ref, slots_ref):
    _, tile, _ = place()
    levels, rows, width = fields_ref.shape[1:]
    _, placed = own_slots(owner_ref, rows, cap)
    kappa, speed = coef_ref[0, 0], coef_ref[0, 1]
    stepped = substep(substep(fields_ref[0, :2], kappa, speed), kappa, speed)
    count, side = slots_ref.shape[0], keep_ref.shape[1]
    for i in range(0, rows, side):
        keep_ref[count // 2 + i // side, : min(side, rows - i)] = stepped[0, i : i + side]
    slots_ref[...] = placed_rows(placed, stepped[0] - stepped[1]).reshape(count, cap, width)
    a = kappa + 0.5 * speed
    b = kappa - 0.5 * speed
    extra = sum([edge_rows(fields_ref[0, l], kappa, a, b) for l in range(2, levels)], [])
    extra = padded(extra, keep_ref.shape[1] - cap, width)
    for m in range(count):
        ref = (keep_ref, give_ref)[m % 2]
        ref[m // 2, :cap] = slots_ref[tile ^ m]
        ref[m // 2, cap:] = extra


def stack_kernel(picks, *refs):
    out_ref = refs[-1]
    for to, (i, j) in enumerate(picks):
        out_ref[to] = refs[i][j]


def index_kernel(
    cap, rows, owner_ref, dest_ref, table_ref, tables_ref, mask_ref, plan_ref, arrive_sum
):
    n_tables = tables_ref.shape[0]
    plan_ref[PLAN_WATER, :rows] = mask_ref[...].astype(F32).astype(BF16)
    for k in range(n_tables):
        at = PLAN_WAYS + 2 * k
        plan_ref[at], plan_ref[at + 1] = split(tables_ref[k], 2)
    sec, tile, atmos = place()
    n_sec, n_tile = lax.axis_size("sec"), lax.axis_size("tile")
    span = n_tile * rows
    start = jnp.minimum(sec, n_sec - 2) * span
    fan = owner_ref.shape[0]
    lines = n_tables * rows
    per = 128 // rows
    g, h = iota((128, 128), 0), iota((128, 128), 1)
    before = ((g < h) & (g // rows == h // rows)).astype(BF16)
    line = iota((lines, 128), 0)
    seat = iota((per * cap, 128), 0)
    lane = iota((per * cap, 128), 1)
    edges = jnp.zeros((lines, 128), F32)
    for group in range(span // 128):
        at = pl.ds(pl.multiple_of(start + group * 128, 128), 128)
        mine = [(owner_ref[r : r + 1, at] == tile) & atmos for r in range(fan)]
        key = jnp.full((1, 128), -1, I32)
        for r in range(fan):
            key = jnp.where(mine[r], table_ref[r : r + 1, at] * rows + dest_ref[r : r + 1, at], key)
        held = (key >= 0).astype(F32)
        rank = mm(jnp.broadcast_to(held, (16, 128)).astype(BF16), before)[:1]
        sits = (rank == (seat % cap).astype(F32)) & (lane // rows == seat // cap) & (held > 0)
        hit = (line == key).astype(BF16)
        arrive = mm_t(sits.astype(BF16), hit)
        arrive_sum[group * per * cap : (group + 1) * per * cap] = arrive
        block, within = group * per + g // rows, g % rows
        column = sum(jnp.where(within == w, i, 0) for i, w in enumerate((0, 1, rows - 2, rows - 1)))
        is_edge = (within < 2) | (within >= rows - 2)
        edges += mm(hit, (is_edge & (h == column * n_tile + block)).astype(BF16))
    arrive = arrive_sum[...]
    plan_ref[PLAN_COLLECT] = arrive.T.astype(BF16)
    plan_ref[PLAN_EDGE, :, :128] = edges.astype(BF16)
    plan_ref[PLAN_EDGE, :, 128:] = jnp.zeros((lines, plan_ref.shape[2] - 128), BF16)
    first, placed = own_slots(owner_ref, rows, cap)
    table = table_ref[:, pl.ds(first, 128)]
    for k in range(n_tables):
        here = sum(jnp.where(table[r : r + 1] == k, placed[r], 0.0) for r in range(fan))
        here = here.T
        plan_ref[PLAN_BACK, k * rows : (k + 1) * rows] = sum(here[i : i + rows] for i in range(0, 128, rows)).astype(BF16)


def shifted(x, by):
    row = iota(x.shape, 0)
    return jnp.where(row == (0 if by > 0 else x.shape[0] - 1), 0.0, roll(x, by, 0))


def corrections(coef, edges):
    a0, aa, k0, b1, bb, k1 = coef
    u0, q0, u1, q1 = edges
    b_prev, a_next = shifted(b1, 1), shifted(a0, -1)
    u_prev, q_prev, u_next, q_next = shifted(u1, 1), shifted(q1, 1), shifted(u0, -1), shifted(q0, -1)
    return [
        sideways(a0 * u_prev, k0) + a0 * (q_prev + b_prev * u0),
        aa * u_prev,
        bb * u_next,
        sideways(b1 * u_next, k1) + b1 * (q_next + a_next * u1),
    ]


def whole_level(plane, correction):
    _, tile, _ = place()
    rows = plane.shape[0]
    here = iota(correction[0].shape, 0) == tile
    own = [jnp.sum(jnp.where(here, c, 0.0), axis=0, keepdims=True) for c in correction]
    return jnp.concatenate(
        [plane[:2] + jnp.concatenate(own[:2]), plane[2 : rows - 2], plane[rows - 2 :] + jnp.concatenate(own[2:])]
    )


def water(plan_ref, rows):
    return plan_ref[PLAN_WATER, :rows].astype(F32)


def grouped_edges(correction, plan_ref):
    short = 128 - correction.shape[0]
    if short:
        correction = jnp.concatenate([correction, jnp.zeros((short, correction.shape[1]), F32)])
    return select_rows(plan_ref[PLAN_EDGE, :, :128], correction, 2)


def flux_of(slots, edges, plan_ref, n_tables, rows):
    grouped = select_rows(plan_ref[PLAN_COLLECT], slots, 2) + edges
    flux = jnp.zeros((rows, slots.shape[1]), F32)
    for k in range(n_tables):
        at = PLAN_WAYS + 2 * k
        flux += product(grouped[k * rows : (k + 1) * rows], plan_ref[at], plan_ref[at + 1])
    return flux


def lines_of(ref, first, count):
    return [ref[:, first + i, :] for i in range(count)]


def flux_kernel(cap, n_tables, got_ref, plan_ref, keep_ref, *refs):
    part_ref = refs[-1]
    _, _, atmos = place()
    n_tile, _, width = got_ref.shape
    rows, side = part_ref.shape[1], keep_ref.shape[1]
    stepped = jnp.concatenate([keep_ref[n_tile // 2 + i // side, : min(side, rows - i)] for i in range(0, rows, side)])
    correction = corrections(lines_of(got_ref, cap, N_COEF), lines_of(got_ref, cap + N_COEF, 4))
    whole = whole_level(stepped, correction)
    slots = got_ref[:, :cap, :].reshape(n_tile * cap, width)
    flux = flux_of(slots, grouped_edges(jnp.concatenate(correction), plan_ref), plan_ref, n_tables, rows)
    part = jnp.where(atmos, FORCING * water(plan_ref, rows) * flux, whole)
    for s in range(part_ref.shape[0]):
        part_ref[s] = part


def levels_kernel(cap, got_ref, fields_ref, coef_ref, level_ref):
    kappa, speed = coef_ref[0, 0], coef_ref[0, 1]
    levels, rows, width = fields_ref.shape[1:]
    stepped = substep(substep(fields_ref[0], kappa, speed), kappa, speed)
    coef = lines_of(got_ref, cap, N_COEF)
    first, second = [corrections(coef, lines_of(got_ref, cap + N_COEF + 4 * l, 4)) for l in range(2)]
    level_ref[:rows] = whole_level(stepped[0], first)
    level_ref[rows : 2 * rows] = whole_level(stepped[1], second)
    level_ref[2 * rows : levels * rows] = stepped[2:].reshape((levels - 2) * rows, width)
    level_ref[levels * rows :] = jnp.concatenate([x - y for x, y in zip(first, second)])


def second_kernel(cap, n_tables, sources, plan_ref, level_ref, *refs):
    swapped, (part_ref, came_ref) = refs[:-2], refs[-2:]
    _, tile, atmos = place()
    n_tile, _, width = came_ref.shape
    rows = part_ref.shape[0]
    edges = level_ref[level_ref.shape[0] - 4 * n_tile :]
    for m, (i, j) in enumerate(sources):
        came_ref[tile ^ m] = swapped[i][j, :cap]
    flux = flux_of(came_ref[...].reshape(n_tile * cap, width), grouped_edges(edges, plan_ref), plan_ref, n_tables, rows)
    part_ref[...] = jnp.where(atmos, FORCING * water(plan_ref, rows) * flux, 0.0)


def finish_kernel(cap, sources, got_ref, level_ref, *refs):
    swapped, (whole_ref, came_ref) = refs[:-2], refs[-2:]
    _, tile, _ = place()
    for m, (i, j) in enumerate(sources):
        came_ref[tile ^ m] = swapped[i][j, cap:]
    coef = lines_of(got_ref, cap, N_COEF)
    levels, rows, _ = whole_ref.shape
    for l in range(levels):
        plane = level_ref[l * rows : (l + 1) * rows]
        if l > 1:
            plane = whole_level(plane, corrections(coef, lines_of(came_ref, 4 * (l - 2), 4)))
        whole_ref[l] = plane


def sea_kernel(n_tables, plan_ref, parts_ref, top_ref, back_ref):
    top = sum(parts_ref[s] for s in range(parts_ref.shape[0]))
    top_ref[...] = top
    sea = water(plan_ref, top.shape[0]) * top
    back_ref[...] = select_rows(plan_ref[PLAN_COLLECT], jnp.concatenate([sea] * n_tables), 3, mm_0)


def end_kernel(n_tables, came_ref, plan_ref, top_ref, whole_ref, total_ref, fields_hbm, surface_hbm, forced_ref, surface_ref, sems):
    _, _, atmos = place()
    levels, rows, _ = whole_ref.shape
    forced_ref[0] = jnp.where(atmos, whole_ref[0], top_ref[...])
    forced_ref[1] = jnp.where(atmos, whole_ref[1], whole_ref[1] + total_ref[...])
    copies = [
        pltpu.make_async_copy(whole_ref.at[pl.ds(2, levels - 2)], fields_hbm.at[0, pl.ds(2, levels - 2)], sems.at[0]),
        pltpu.make_async_copy(forced_ref, fields_hbm.at[0, pl.ds(0, 2)], sems.at[1]),
        pltpu.make_async_copy(surface_ref, surface_hbm.at[0], sems.at[2]),
    ]
    for copy in copies[:2]:
        copy.start()
    picked = select_rows(plan_ref[PLAN_BACK], came_ref[...], 2)
    seen = jnp.zeros(surface_ref.shape, F32)
    for k in range(n_tables):
        at = PLAN_WAYS + 2 * k
        seen += product(picked[k * rows : (k + 1) * rows], plan_ref[at], plan_ref[at + 1], mm_t)
    surface_ref[...] = jnp.where(atmos, seen, water(plan_ref, rows) * top_ref[...])
    copies[2].start()
    for copy in copies:
        copy.wait()


def call(kernel, n_in, outs, flops=0, scratch=(), space=pltpu.VMEM, out_space=pltpu.VMEM, vmem=12):
    shapes = [jax.ShapeDtypeStruct(s, d) for s, d in outs]
    return pl.pallas_call(
        kernel,
        out_shape=shapes,
        in_specs=[pl.BlockSpec(memory_space=space)] * n_in,
        out_specs=[pl.BlockSpec(memory_space=out_space)] * len(shapes),
        scratch_shapes=scratch,
        compiler_params=pltpu.CompilerParams(vmem_limit_bytes=vmem * 1024 * 1024),
        cost_estimate=pl.CostEstimate(flops=flops, bytes_accessed=1 << 10, transcendentals=0),
    )


def swap_stage(bit, arrays, chunks, after=None, flops=0):
    n_tile = lax.axis_size("tile")
    going = [m for m in range(n_tile) if m & bit]
    keep_shape = arrays[0].shape[1:]
    if after is not None:
        arrays, after = lax.optimization_barrier((arrays, after))
    if bit == 1:
        give = arrays.pop()
    else:
        picks = [chunks[m] for m in going]
        used = sorted({i for i, _ in picks})
        picks = [(used.index(i), j) for i, j in picks]
        taken = [arrays[i] for i in used]
        (give,) = call(functools.partial(stack_kernel, picks), len(used), [((len(going),) + keep_shape, F32)], flops=flops)(*taken)
    came = lax.ppermute(give, "tile", [(t, t ^ bit) for t in range(n_tile)])
    chunks = chunks | {m: (len(arrays), i) for i, m in enumerate(going)}
    return arrays + [came], chunks, after


def local(fields, coefficients, owner_tile, dest_block, table_index, tables, land_mask):
    n_sec, n_tile = lax.axis_size("sec"), lax.axis_size("tile")
    levels, rows, width = fields.shape[1:]
    fan = owner_tile.shape[1]
    n_tables = tables.shape[0]
    cap = 2 * fan * rows // n_tile
    slots, lines = n_tile * cap, n_tables * rows
    up8 = lambda n: -(-n // 8) * 8
    chunk, side = up8(cap + N_COEF + 8), up8(cap + 4 * (levels - 2))
    owner, dest, table = owner_tile.T, dest_block.T, table_index.T
    exchange = lambda x, axis: lax.all_to_all(x, axis, split_axis=0, concat_axis=0, tiled=True)
    plane = ((rows, width), F32)

    (send,) = call(
        functools.partial(send_kernel, cap),
        3,
        [((n_tile, chunk, width), F32)],
        scratch=[
            pltpu.VMEM((2, rows, width), F32),
            pltpu.VMEM((2, rows, width), F32),
            pltpu.VMEM(owner.shape, I32),
            pltpu.SemaphoreType.DMA((3,)),
        ],
        space=pltpu.HBM,
        vmem=60,
    )(fields, coefficients, owner)
    got = exchange(send, "tile")
    keep, give = call(
        functools.partial(swap_kernel, cap),
        3,
        [((n_tile // 2 - -rows // side, side, width), F32), ((n_tile // 2, side, width), F32)],
        scratch=[pltpu.VMEM((n_tile, cap, width), F32)],
    )(fields, coefficients, owner)
    arrays, chunks, _ = swap_stage(1, [keep, give], {m: (0, m // 2) for m in range(0, n_tile, 2)})
    (plan,) = call(
        functools.partial(index_kernel, cap, rows),
        5,
        [((PLAN_WAYS + 2 * n_tables, lines, width), BF16)],
        scratch=[pltpu.VMEM((slots, lines), F32)],
    )(owner, dest, table, tables, land_mask)
    arrays, chunks, plan = swap_stage(2, arrays, chunks, plan)
    (part,) = call(functools.partial(flux_kernel, cap, n_tables), 1 + len(arrays), [((n_sec, rows, width), F32)])(
        got, plan, *arrays[:-1]
    )
    parts = exchange(part, "sec")
    bit = 4
    while bit < n_tile:
        arrays, chunks, part = swap_stage(bit, arrays, chunks, part)
        bit *= 2
    sources = [chunks[m] for m in range(n_tile)]
    (level,) = call(functools.partial(levels_kernel, cap), 3, [((levels * rows + 4 * n_tile, width), F32)], flops=1 << 32)(
        got, fields, coefficients
    )
    top, back = call(functools.partial(sea_kernel, n_tables), 2, [plane, ((slots, width), F32)])(plan, parts)
    level, back = lax.optimization_barrier((level, back))
    came = exchange(back.reshape(n_tile, cap, width), "tile").reshape(slots, width)
    (total,) = call(
        functools.partial(second_kernel, cap, n_tables, sources),
        2 + len(arrays),
        [plane],
        scratch=[pltpu.VMEM((n_tile, cap, width), F32)],
        flops=1 << 34,
    )(plan, level, *arrays)
    bit = 1
    while bit < n_sec:
        pairs = [(s, s | bit) for s in range(n_sec) if (s & (2 * bit - 1)) == bit - 1]
        total = total + lax.ppermute(total, "sec", pairs)
        bit *= 2
    (whole,) = call(
        functools.partial(finish_kernel, cap, sources),
        2 + len(arrays),
        [((levels, rows, width), F32)],
        scratch=[pltpu.VMEM((n_tile, side - cap, width), F32)],
        flops=1 << 28,
    )(got, level, *arrays)
    return call(
        functools.partial(end_kernel, n_tables),
        5,
        [(fields.shape, F32), ((1, rows, width), F32)],
        scratch=[pltpu.VMEM((2, rows, width), F32), pltpu.VMEM((rows, width), F32), pltpu.SemaphoreType.DMA((3,))],
        out_space=pltpu.HBM,
    )(came, plan, top, whole, total)


def solution(mesh):
    placed = (P("sec", None, "tile", None), P("sec", None, "tile", None), P(), P(), P(), P(), P("tile", None))
    return jax.shard_map(
        local,
        mesh=mesh,
        in_specs=placed,
        out_specs=(P("sec", None, "tile", None), P("sec", "tile", None)),
        check_vma=False,
    )
```

```python
import functools

import jax
import jax.numpy as jnp
from jax import lax
from jax.experimental import pallas as pl
from jax.experimental.pallas import tpu as pltpu
from jax.sharding import PartitionSpec as P

FORCING = 0.5
F32, BF16, I32 = jnp.float32, jnp.bfloat16, jnp.int32
N_COEF = 6
PLAN_COLLECT, PLAN_EDGE, PLAN_BACK, PLAN_WATER, PLAN_WAYS = 0, 1, 2, 3, 4


def iota(shape, axis):
    return lax.broadcasted_iota(I32, shape, axis)


def roll(x, shift, axis):
    return pltpu.roll(x, shift % x.shape[axis], axis)


def split(x, parts):
    out = []
    for _ in range(parts):
        out.append(x.astype(BF16))
        x = x - out[-1].astype(F32)
    return out


def mm(a, b):
    return lax.dot_general(a, b, (((1,), (0,)), ((), ())), preferred_element_type=F32)


def mm_0(a, b):
    return lax.dot_general(a, b, (((0,), (0,)), ((), ())), preferred_element_type=F32)


def mm_t(a, b):
    return lax.dot_general(a, b, (((1,), (1,)), ((), ())), preferred_element_type=F32)


def select_rows(hot, x, parts, dot=mm):
    return sum(dot(hot, p) for p in split(x, parts))


def product(a, b1, b2, dot=mm):
    a1, a2 = split(a, 2)
    rows = a.shape[0]
    both = dot(jnp.concatenate([a1, a2]), b1)
    return both[:rows] + both[rows:] + dot(a1, b2)


def sideways(x, kappa):
    return x + kappa * (roll(x, 1, x.ndim - 1) + roll(x, -1, x.ndim - 1) - 4.0 * x)


def substep(u, kappa, speed):
    rows = u.shape[1]
    row = iota(u.shape, 1)
    upper = jnp.where(row == 0, 0.0, roll(u, 1, 1))
    lower = jnp.where(row == rows - 1, 0.0, roll(u, -1, 1))
    laplace = upper + lower + roll(u, 1, 2) + roll(u, -1, 2) - 4.0 * u
    return u + kappa * laplace - 0.5 * speed * (lower - upper)


def place():
    sec, tile = lax.axis_index("sec"), lax.axis_index("tile")
    return sec, tile, sec < lax.axis_size("sec") - 1


def own_slots(owner_ref, rows, cap):
    sec, tile, atmos = place()
    n_sec, n_tile = lax.axis_size("sec"), lax.axis_size("tile")
    block = (jnp.minimum(sec, n_sec - 2) * n_tile + tile) * rows
    first = pl.multiple_of(block // 128 * 128, 128)
    half = block - first
    shape = (n_tile * cap, 128)
    lane = iota((1, 128), 1)
    inside = (lane >= half) & (lane < half + rows) & atmos
    owner = jnp.where(inside, owner_ref[:, pl.ds(first, 128)], -1)
    slot = iota(shape, 0)
    hot = [(owner[r : r + 1] == slot // cap).astype(F32) for r in range(owner.shape[0])]
    both = sum(hot)
    before = (iota((128, 128), 0) < iota((128, 128), 1)).astype(BF16)
    rank = mm(both.astype(BF16), before)
    placed = rank == (slot % cap).astype(F32)
    return first, [jnp.where(placed, h, 0.0) for h in hot]


def edge_rows(u, kappa, a, b):
    top, bot = slice(0, 1), slice(u.shape[0] - 1, u.shape[0])
    q_top = sideways(u[top], kappa[top]) + b[top] * u[1:2]
    q_bot = sideways(u[bot], kappa[bot]) + a[bot] * u[-2:-1]
    return [u[top], q_top, u[bot], q_bot]


def padded(lines, count, width):
    if count > len(lines):
        lines = lines + [jnp.zeros((count - len(lines), width), F32)]
    return jnp.concatenate(lines)


def placed_rows(placed, payload):
    return select_rows(sum(placed).astype(BF16), jnp.concatenate([payload] * (128 // payload.shape[0])), 3)


def send_kernel(cap, fields_hbm, coef_hbm, owner_hbm, send_ref, fields_ref, coef_ref, owner_ref, sems):
    pairs = ((owner_hbm, owner_ref), (coef_hbm.at[0], coef_ref), (fields_hbm.at[0, pl.ds(0, 2)], fields_ref))
    copies = [pltpu.make_async_copy(src, dst, sems.at[i]) for i, (src, dst) in enumerate(pairs)]
    for copy in copies:
        copy.start()
    copies[0].wait()
    _, rows, width = fields_ref.shape
    _, placed = own_slots(owner_ref, rows, cap)
    copies[1].wait()
    copies[2].wait()
    u = fields_ref[...]
    kappa, speed = coef_ref[0], coef_ref[1]
    stepped = substep(substep(u[:1], kappa, speed), kappa, speed)[0]
    n_tile = send_ref.shape[0]
    send_ref[:, :cap] = placed_rows(placed, stepped).reshape(n_tile, cap, width)
    a = kappa + 0.5 * speed
    b = kappa - 0.5 * speed
    bot = slice(rows - 1, rows)
    extra = [a[0:1], a[0:1] * a[1:2], kappa[0:1], b[bot], b[bot] * b[rows - 2 : rows - 1], kappa[bot]]
    extra += edge_rows(u[0], kappa, a, b) + edge_rows(u[1], kappa, a, b)
    extra = padded(extra, send_ref.shape[1] - cap, width)
    send_ref[:, cap:] = jnp.broadcast_to(extra[None], (n_tile,) + extra.shape)


def swap_kernel(cap, fields_ref, coef_ref, owner_ref, keep_ref, give_ref, slots_ref):
    _, tile, _ = place()
    levels, rows, width = fields_ref.shape[1:]
    _, placed = own_slots(owner_ref, rows, cap)
    kappa, speed = coef_ref[0, 0], coef_ref[0, 1]
    stepped = substep(substep(fields_ref[0, :2], kappa, speed), kappa, speed)
    count = slots_ref.shape[0]
    slots_ref[...] = placed_rows(placed, stepped[0] - stepped[1]).reshape(count, cap, width)
    for m in range(count):
        ref = (keep_ref, give_ref)[m % 2]
        ref[m // 2 * cap : (m // 2 + 1) * cap] = slots_ref[tile ^ m]
    a = kappa + 0.5 * speed
    b = kappa - 0.5 * speed
    extra = sum([edge_rows(fields_ref[0, l], kappa, a, b) for l in range(2, levels)], [])
    held = count // 2 * cap
    give_ref[held:] = padded(extra, give_ref.shape[0] - held, width)
    keep_ref[held:] = stepped[0]


def stack_kernel(picks, cap, *refs):
    out_ref = refs[-1]
    for to, (i, j) in enumerate(picks):
        out_ref[to * cap : (to + 1) * cap] = refs[i][j * cap : (j + 1) * cap]
    held = len(picks) * cap
    out_ref[held:] = refs[-2][held:]


def index_kernel(
    cap, rows, owner_ref, dest_ref, table_ref, tables_ref, mask_ref, plan_ref, arrive_sum
):
    n_tables = tables_ref.shape[0]
    plan_ref[PLAN_WATER, :rows] = mask_ref[...].astype(F32).astype(BF16)
    for k in range(n_tables):
        at = PLAN_WAYS + 2 * k
        plan_ref[at], plan_ref[at + 1] = split(tables_ref[k], 2)
    sec, tile, atmos = place()
    n_sec, n_tile = lax.axis_size("sec"), lax.axis_size("tile")
    span = n_tile * rows
    start = jnp.minimum(sec, n_sec - 2) * span
    fan = owner_ref.shape[0]
    lines = n_tables * rows
    per = 128 // rows
    g, h = iota((128, 128), 0), iota((128, 128), 1)
    before = ((g < h) & (g // rows == h // rows)).astype(BF16)
    line = iota((lines, 128), 0)
    seat = iota((per * cap, 128), 0)
    lane = iota((per * cap, 128), 1)
    edges = jnp.zeros((lines, 128), F32)
    for group in range(span // 128):
        at = pl.ds(pl.multiple_of(start + group * 128, 128), 128)
        mine = [(owner_ref[r : r + 1, at] == tile) & atmos for r in range(fan)]
        key = jnp.full((1, 128), -1, I32)
        for r in range(fan):
            key = jnp.where(mine[r], table_ref[r : r + 1, at] * rows + dest_ref[r : r + 1, at], key)
        held = (key >= 0).astype(F32)
        rank = mm(jnp.broadcast_to(held, (16, 128)).astype(BF16), before)[:1]
        sits = (rank == (seat % cap).astype(F32)) & (lane // rows == seat // cap) & (held > 0)
        hit = (line == key).astype(BF16)
        arrive = mm_t(sits.astype(BF16), hit)
        arrive_sum[group * per * cap : (group + 1) * per * cap] = arrive
        block, within = group * per + g // rows, g % rows
        column = sum(jnp.where(within == w, i, 0) for i, w in enumerate((0, 1, rows - 2, rows - 1)))
        is_edge = (within < 2) | (within >= rows - 2)
        edges += mm(hit, (is_edge & (h == column * n_tile + block)).astype(BF16))
    arrive = arrive_sum[...]
    plan_ref[PLAN_COLLECT] = arrive.T.astype(BF16)
    plan_ref[PLAN_EDGE, :, :128] = edges.astype(BF16)
    plan_ref[PLAN_EDGE, :, 128:] = jnp.zeros((lines, plan_ref.shape[2] - 128), BF16)
    first, placed = own_slots(owner_ref, rows, cap)
    table = table_ref[:, pl.ds(first, 128)]
    for k in range(n_tables):
        here = sum(jnp.where(table[r : r + 1] == k, placed[r], 0.0) for r in range(fan))
        here = here.T
        plan_ref[PLAN_BACK, k * rows : (k + 1) * rows] = sum(here[i : i + rows] for i in range(0, 128, rows)).astype(BF16)


def shifted(x, by):
    row = iota(x.shape, 0)
    return jnp.where(row == (0 if by > 0 else x.shape[0] - 1), 0.0, roll(x, by, 0))


def corrections(coef, edges):
    a0, aa, k0, b1, bb, k1 = coef
    u0, q0, u1, q1 = edges
    b_prev, a_next = shifted(b1, 1), shifted(a0, -1)
    u_prev, q_prev, u_next, q_next = shifted(u1, 1), shifted(q1, 1), shifted(u0, -1), shifted(q0, -1)
    return [
        sideways(a0 * u_prev, k0) + a0 * (q_prev + b_prev * u0),
        aa * u_prev,
        bb * u_next,
        sideways(b1 * u_next, k1) + b1 * (q_next + a_next * u1),
    ]


def whole_level(plane, correction):
    _, tile, _ = place()
    rows = plane.shape[0]
    here = iota(correction[0].shape, 0) == tile
    own = [jnp.sum(jnp.where(here, c, 0.0), axis=0, keepdims=True) for c in correction]
    return jnp.concatenate(
        [plane[:2] + jnp.concatenate(own[:2]), plane[2 : rows - 2], plane[rows - 2 :] + jnp.concatenate(own[2:])]
    )


def water(plan_ref, rows):
    return plan_ref[PLAN_WATER, :rows].astype(F32)


def grouped_edges(correction, plan_ref):
    short = 128 - correction.shape[0]
    if short:
        correction = jnp.concatenate([correction, jnp.zeros((short, correction.shape[1]), F32)])
    return select_rows(plan_ref[PLAN_EDGE, :, :128], correction, 2)


def flux_of(slots, edges, plan_ref, n_tables, rows):
    grouped = select_rows(plan_ref[PLAN_COLLECT], slots, 2) + edges
    flux = jnp.zeros((rows, slots.shape[1]), F32)
    for k in range(n_tables):
        at = PLAN_WAYS + 2 * k
        flux += product(grouped[k * rows : (k + 1) * rows], plan_ref[at], plan_ref[at + 1])
    return flux


def lines_of(ref, first, count):
    return [ref[:, first + i, :] for i in range(count)]


def flux_kernel(cap, n_tables, got_ref, plan_ref, keep_ref, *refs):
    part_ref = refs[-1]
    _, _, atmos = place()
    n_tile, _, width = got_ref.shape
    rows = part_ref.shape[0]
    stepped = keep_ref[keep_ref.shape[0] - rows :]
    correction = corrections(lines_of(got_ref, cap, N_COEF), lines_of(got_ref, cap + N_COEF, 4))
    whole = whole_level(stepped, correction)
    slots = got_ref[:, :cap, :].reshape(n_tile * cap, width)
    flux = flux_of(slots, grouped_edges(jnp.concatenate(correction), plan_ref), plan_ref, n_tables, rows)
    part_ref[...] = jnp.where(atmos, FORCING * water(plan_ref, rows) * flux, whole)


def levels_kernel(cap, got_ref, fields_ref, coef_ref, level_ref):
    kappa, speed = coef_ref[0, 0], coef_ref[0, 1]
    levels, rows, width = fields_ref.shape[1:]
    n_tile = got_ref.shape[0]
    stepped = substep(substep(fields_ref[0], kappa, speed), kappa, speed)
    coef = lines_of(got_ref, cap, N_COEF)
    first, second = [corrections(coef, lines_of(got_ref, cap + N_COEF + 4 * l, 4)) for l in range(2)]
    level_ref[:rows] = whole_level(stepped[0], first)
    level_ref[rows : 2 * rows] = whole_level(stepped[1], second)
    level_ref[2 * rows : levels * rows] = stepped[2:].reshape((levels - 2) * rows, width)
    at = levels * rows + 4 * n_tile
    level_ref[levels * rows : at] = jnp.concatenate([x - y for x, y in zip(first, second)])
    level_ref[at:] = padded(
        sum([[u[:1], u[:1], u[rows - 1 :], u[rows - 1 :]] for u in [fields_ref[0, l] for l in range(2, levels)]], []),
        level_ref.shape[0] - at,
        width,
    )


def second_kernel(cap, n_tables, levels, sources, plan_ref, level_ref, *refs):
    swapped, (part_ref, came_ref) = refs[:-2], refs[-2:]
    _, tile, atmos = place()
    n_tile, _, width = came_ref.shape
    rows = part_ref.shape[0]
    edges = level_ref[levels * rows : levels * rows + 4 * n_tile]
    for m, (i, j) in enumerate(sources):
        came_ref[tile ^ m] = swapped[i][j * cap : (j + 1) * cap]
    flux = flux_of(came_ref[...].reshape(n_tile * cap, width), grouped_edges(edges, plan_ref), plan_ref, n_tables, rows)
    part_ref[...] = jnp.where(atmos, FORCING * water(plan_ref, rows) * flux, 0.0)


def finish_kernel(cap, got_ref, level_ref, *refs):
    swapped, whole_ref = refs[:-1], refs[-1]
    _, tile, _ = place()
    levels, rows, width = whole_ref.shape
    n_tile = got_ref.shape[0]
    whole_ref[...] = level_ref[: levels * rows].reshape(levels, rows, width)
    count = 4 * (levels - 2)
    held = n_tile // 2 * cap
    prev = jnp.zeros((count, width), F32)
    after = prev
    for i, ref in enumerate(swapped):
        other = tile ^ (2 ** (i + 1) - 1)
        came = ref[held : held + count]
        prev = jnp.where(other == tile - 1, came, prev)
        after = jnp.where(other == tile + 1, came, after)
    own = got_ref[tile, cap : cap + 8]
    a0, aa, k0, b1, bb, k1 = [own[i : i + 1] for i in range(N_COEF)]
    b_prev = jnp.where(tile > 0, got_ref[jnp.maximum(tile - 1, 0), cap : cap + 8][3:4], 0.0)
    a_next = jnp.where(tile < n_tile - 1, got_ref[jnp.minimum(tile + 1, n_tile - 1), cap : cap + 8][0:1], 0.0)
    for l in range(2, levels):
        u0, _, u1, _ = [level_ref[levels * rows + 4 * n_tile + 4 * (l - 2) + i : levels * rows + 4 * n_tile + 4 * (l - 2) + i + 1] for i in range(4)]
        u_prev, q_prev = [prev[4 * (l - 2) + i : 4 * (l - 2) + i + 1] for i in (2, 3)]
        u_next, q_next = [after[4 * (l - 2) + i : 4 * (l - 2) + i + 1] for i in (0, 1)]
        whole_ref[l, :2] += jnp.concatenate([sideways(a0 * u_prev, k0) + a0 * (q_prev + b_prev * u0), aa * u_prev])
        whole_ref[l, rows - 2 :] += jnp.concatenate([bb * u_next, sideways(b1 * u_next, k1) + b1 * (q_next + a_next * u1)])


def sea_kernel(n_tables, plan_ref, *refs):
    parts, (top_ref, back_ref) = refs[:-2], refs[-2:]
    top = sum(part[...] for part in parts)
    top_ref[...] = top
    sea = water(plan_ref, top.shape[0]) * top
    back_ref[...] = select_rows(plan_ref[PLAN_COLLECT], jnp.concatenate([sea] * n_tables), 3, mm_0)


def surface_kernel(n_tables, came_ref, plan_ref, top_ref, surface_ref):
    _, _, atmos = place()
    rows, width = top_ref.shape
    picked = select_rows(plan_ref[PLAN_BACK], came_ref[...], 2)
    seen = jnp.zeros((rows, width), F32)
    for k in range(n_tables):
        at = PLAN_WAYS + 2 * k
        seen += product(picked[k * rows : (k + 1) * rows], plan_ref[at], plan_ref[at + 1], mm_t)
    surface_ref[0] = jnp.where(atmos, seen, water(plan_ref, rows) * top_ref[...])


def fields_kernel(top_ref, whole_ref, total_ref, came_ref, fields_ref):
    _, _, atmos = place()
    fields_ref[0, 0] = jnp.where(atmos, whole_ref[0], top_ref[...])
    fields_ref[0, 1] = jnp.where(atmos, whole_ref[1], whole_ref[1] + total_ref[...] + came_ref[...])
    fields_ref[0, 2:] = whole_ref[2:]


def call(kernel, n_in, outs, flops=0, scratch=(), space=pltpu.VMEM, out_space=pltpu.VMEM, vmem=12):
    shapes = [jax.ShapeDtypeStruct(s, d) for s, d in outs]
    return pl.pallas_call(
        kernel,
        out_shape=shapes,
        in_specs=[pl.BlockSpec(memory_space=space)] * n_in,
        out_specs=[pl.BlockSpec(memory_space=out_space)] * len(shapes),
        scratch_shapes=scratch,
        compiler_params=pltpu.CompilerParams(vmem_limit_bytes=vmem * 1024 * 1024),
        cost_estimate=pl.CostEstimate(flops=flops, bytes_accessed=1 << 10, transcendentals=0),
    )


def swap_stage(bit, cap, arrays, chunks, after=None):
    n_tile = lax.axis_size("tile")
    going = [m for m in range(n_tile) if m & bit]
    if after is not None:
        arrays, after = lax.optimization_barrier((arrays, after))
    if bit == 1:
        give = arrays.pop()
    else:
        picks = [chunks[m] for m in going]
        used = sorted({i for i, _ in picks})
        picks = [(used.index(i), j) for i, j in picks]
        taken = [arrays[i] for i in used]
        if used[-1] != len(arrays) - 1:
            taken.append(arrays[-1])
        kernel = functools.partial(stack_kernel, picks, cap)
        (give,) = call(kernel, len(taken), [(arrays[-1].shape, F32)])(*taken)
    came = lax.ppermute(give, "tile", [(t, t ^ bit) for t in range(n_tile)])
    chunks = chunks | {m: (len(arrays), i) for i, m in enumerate(going)}
    return arrays + [came], chunks, after


def local(fields, coefficients, owner_tile, dest_block, table_index, tables, land_mask):
    n_sec, n_tile = lax.axis_size("sec"), lax.axis_size("tile")
    levels, rows, width = fields.shape[1:]
    fan = owner_tile.shape[1]
    n_tables = tables.shape[0]
    cap = 2 * fan * rows // n_tile
    slots, lines = n_tile * cap, n_tables * rows
    up8 = lambda n: -(-n // 8) * 8
    chunk, side = up8(cap + N_COEF + 8), up8(4 * (levels - 2))
    owner, dest, table = owner_tile.T, dest_block.T, table_index.T
    exchange = lambda x, axis: lax.all_to_all(x, axis, split_axis=0, concat_axis=0, tiled=True)
    plane = ((rows, width), F32)

    (send,) = call(
        functools.partial(send_kernel, cap),
        3,
        [((n_tile, chunk, width), F32)],
        scratch=[
            pltpu.VMEM((2, rows, width), F32),
            pltpu.VMEM((2, rows, width), F32),
            pltpu.VMEM(owner.shape, I32),
            pltpu.SemaphoreType.DMA((3,)),
        ],
        space=pltpu.HBM,
        vmem=60,
    )(fields, coefficients, owner)
    got = exchange(send, "tile")
    half = n_tile // 2 * cap
    keep, give = call(
        functools.partial(swap_kernel, cap),
        3,
        [((half + rows, width), F32), ((half + side, width), F32)],
        scratch=[pltpu.VMEM((n_tile, cap, width), F32)],
    )(fields, coefficients, owner)
    arrays, chunks, _ = swap_stage(1, cap, [keep, give], {m: (0, m // 2) for m in range(0, n_tile, 2)})
    (plan,) = call(
        functools.partial(index_kernel, cap, rows),
        5,
        [((PLAN_WAYS + 2 * n_tables, lines, width), BF16)],
        scratch=[pltpu.VMEM((slots, lines), F32)],
    )(owner, dest, table, tables, land_mask)
    arrays, chunks, plan = swap_stage(2, cap, arrays, chunks, plan)
    (part,) = call(functools.partial(flux_kernel, cap, n_tables), 1 + len(arrays), [plane])(got, plan, *arrays[:-1])
    others = [lax.ppermute(part, "sec", [(s, s ^ other) for s in range(n_sec)]) for other in range(n_sec - 1, 0, -1)]
    bit = 4
    while bit < n_tile:
        arrays, chunks, part = swap_stage(bit, cap, arrays, chunks, part)
        bit *= 2
    sources = [chunks[m] for m in range(n_tile)]
    top, back = call(functools.partial(sea_kernel, n_tables), 1 + n_sec, [plane, ((slots, width), F32)])(plan, part, *others)
    got, back = lax.optimization_barrier((got, back))
    (level,) = call(
        functools.partial(levels_kernel, cap), 3, [((levels * rows + 4 * n_tile + side, width), F32)], flops=1 << 32
    )(got, fields, coefficients)
    came = exchange(back.reshape(n_tile, cap, width), "tile").reshape(slots, width)
    (total,) = call(
        functools.partial(second_kernel, cap, n_tables, levels, sources),
        2 + len(arrays),
        [plane],
        scratch=[pltpu.VMEM((n_tile, cap, width), F32)],
        flops=1 << 34,
    )(plan, level, *arrays)
    came_total = 0.0
    bit = 1
    while bit < n_sec:
        pairs = [(s, s | bit) for s in range(n_sec) if (s & (2 * bit - 1)) == bit - 1]
        total = total + came_total
        came_total = lax.ppermute(total, "sec", pairs)
        bit *= 2
    (whole,) = call(
        functools.partial(finish_kernel, cap), 1 + len(arrays), [((levels, rows, width), F32)], flops=1 << 28
    )(got, level, *arrays[1:])
    (surface,) = call(functools.partial(surface_kernel, n_tables), 3, [((1, rows, width), F32)])(came, plan, top)
    came_total, surface = lax.optimization_barrier((came_total, surface))
    (ended,) = call(fields_kernel, 4, [(fields.shape, F32)])(top, whole, total, came_total)
    return ended, surface


def solution(mesh):
    placed = (P("sec", None, "tile", None), P("sec", None, "tile", None), P(), P(), P(), P(), P("tile", None))
    return jax.shard_map(
        local,
        mesh=mesh,
        in_specs=placed,
        out_specs=(P("sec", None, "tile", None), P("sec", "tile", None)),
        check_vma=False,
    )
```

```python
import functools

import jax
import jax.numpy as jnp
from jax import lax
from jax.experimental import pallas as pl
from jax.experimental.pallas import tpu as pltpu
from jax.sharding import PartitionSpec as P

FORCING = 0.5
F32, BF16, I32 = jnp.float32, jnp.bfloat16, jnp.int32
N_COEF = 6
PLAN_COLLECT, PLAN_ARRIVE, PLAN_EDGE, PLAN_BACK, PLAN_WAYS = 0, 1, 2, 3, 4


def iota(shape, axis):
    return lax.broadcasted_iota(I32, shape, axis)


def roll(x, shift, axis):
    return pltpu.roll(x, shift % x.shape[axis], axis)


def split(x, parts):
    out = []
    for _ in range(parts):
        out.append(x.astype(BF16))
        x = x - out[-1].astype(F32)
    return out


def mm(a, b):
    return lax.dot_general(a, b, (((1,), (0,)), ((), ())), preferred_element_type=F32)


def mm_t(a, b):
    return lax.dot_general(a, b, (((1,), (1,)), ((), ())), preferred_element_type=F32)


def select_rows(hot, x, parts):
    return sum(mm(hot, p) for p in split(x, parts))


def product(a, b1, b2, dot=mm):
    a1, a2 = split(a, 2)
    rows = a.shape[0]
    both = dot(jnp.concatenate([a1, a2]), b1)
    return both[:rows] + both[rows:] + dot(a1, b2)


def sideways(x, kappa):
    return x + kappa * (roll(x, 1, x.ndim - 1) + roll(x, -1, x.ndim - 1) - 4.0 * x)


def substep(u, kappa, speed):
    rows = u.shape[1]
    row = iota(u.shape, 1)
    upper = jnp.where(row == 0, 0.0, roll(u, 1, 1))
    lower = jnp.where(row == rows - 1, 0.0, roll(u, -1, 1))
    laplace = upper + lower + roll(u, 1, 2) + roll(u, -1, 2) - 4.0 * u
    return u + kappa * laplace - 0.5 * speed * (lower - upper)


def place():
    sec, tile = lax.axis_index("sec"), lax.axis_index("tile")
    return sec, tile, sec < lax.axis_size("sec") - 1


def own_slots(owner_ref, rows, cap):
    sec, tile, atmos = place()
    n_sec, n_tile = lax.axis_size("sec"), lax.axis_size("tile")
    block = (jnp.minimum(sec, n_sec - 2) * n_tile + tile) * rows
    first = pl.multiple_of(block // 128 * 128, 128)
    half = block - first
    shape = (n_tile * cap, 128)
    lane = iota((1, 128), 1)
    inside = (lane >= half) & (lane < half + rows) & atmos
    owner = jnp.where(inside, owner_ref[:, pl.ds(first, 128)], -1)
    slot = iota(shape, 0)
    hot = [(owner[r : r + 1] == slot // cap).astype(F32) for r in range(owner.shape[0])]
    both = sum(hot)
    before = (iota((128, 128), 0) < iota((128, 128), 1)).astype(BF16)
    rank = mm(both.astype(BF16), before)
    placed = rank == (slot % cap).astype(F32)
    return first, [jnp.where(placed, h, 0.0) for h in hot]


def edge_rows(u, kappa, a, b):
    top, bot = slice(0, 1), slice(u.shape[0] - 1, u.shape[0])
    q_top = sideways(u[top], kappa[top]) + b[top] * u[1:2]
    q_bot = sideways(u[bot], kappa[bot]) + a[bot] * u[-2:-1]
    return [u[top], q_top, u[bot], q_bot]


def padded(lines, count, width):
    if count > len(lines):
        lines = lines + [jnp.zeros((count - len(lines), width), F32)]
    return jnp.concatenate(lines)


def placed_rows(placed, payload):
    return select_rows(sum(placed).astype(BF16), jnp.concatenate([payload] * (128 // payload.shape[0])), 2)


def send_kernel(cap, fields_hbm, coef_hbm, owner_hbm, send_ref, fields_ref, coef_ref, owner_ref, sems):
    pairs = ((owner_hbm, owner_ref), (coef_hbm.at[0], coef_ref), (fields_hbm.at[0, pl.ds(0, 2)], fields_ref))
    copies = [pltpu.make_async_copy(src, dst, sems.at[i]) for i, (src, dst) in enumerate(pairs)]
    for copy in copies:
        copy.start()
    copies[0].wait()
    _, rows, width = fields_ref.shape
    _, placed = own_slots(owner_ref, rows, cap)
    copies[1].wait()
    copies[2].wait()
    u = fields_ref[...]
    kappa, speed = coef_ref[0], coef_ref[1]
    stepped = substep(substep(u[:1], kappa, speed), kappa, speed)[0]
    n_tile = send_ref.shape[0]
    send_ref[:, :cap] = placed_rows(placed, stepped).reshape(n_tile, cap, width)
    a = kappa + 0.5 * speed
    b = kappa - 0.5 * speed
    bot = slice(rows - 1, rows)
    extra = [a[0:1], a[0:1] * a[1:2], kappa[0:1], b[bot], b[bot] * b[rows - 2 : rows - 1], kappa[bot]]
    extra += edge_rows(u[0], kappa, a, b) + edge_rows(u[1], kappa, a, b)
    extra = padded(extra, send_ref.shape[1] - cap, width)
    send_ref[:, cap:] = jnp.broadcast_to(extra[None], (n_tile,) + extra.shape)


def swap_kernel(cap, fields_ref, coef_ref, owner_ref, keep_ref, give_ref, slots_ref):
    _, tile, _ = place()
    levels, rows, width = fields_ref.shape[1:]
    _, placed = own_slots(owner_ref, rows, cap)
    kappa, speed = coef_ref[0, 0], coef_ref[0, 1]
    stepped = substep(substep(fields_ref[0, :2], kappa, speed), kappa, speed)
    count = slots_ref.shape[0]
    slots_ref[...] = placed_rows(placed, stepped[0] - stepped[1]).reshape(count, cap, width)
    for m in range(count):
        ref = (keep_ref, give_ref)[m % 2]
        ref[m // 2 * cap : (m // 2 + 1) * cap] = slots_ref[tile ^ m]
    a = kappa + 0.5 * speed
    b = kappa - 0.5 * speed
    extra = sum([edge_rows(fields_ref[0, l], kappa, a, b) for l in range(2, levels)], [])
    held = count // 2 * cap
    give_ref[held:] = padded(extra, give_ref.shape[0] - held, width)
    keep_ref[held:] = stepped[0]


def stack_kernel(picks, cap, *refs):
    out_ref = refs[-1]
    for to, (i, j) in enumerate(picks):
        out_ref[to * cap : (to + 1) * cap] = refs[i][j * cap : (j + 1) * cap]
    held = len(picks) * cap
    out_ref[held:] = refs[-2][held:]


def index_kernel(
    cap, rows, owner_ref, dest_ref, table_ref, tables_ref, mask_ref, plan_ref, arrive_sum
):
    n_tables = tables_ref.shape[0]
    for k in range(n_tables):
        at = PLAN_WAYS + 2 * k
        plan_ref[at], plan_ref[at + 1] = split(tables_ref[k], 2)
    sec, tile, atmos = place()
    n_sec, n_tile = lax.axis_size("sec"), lax.axis_size("tile")
    span = n_tile * rows
    start = jnp.minimum(sec, n_sec - 2) * span
    fan = owner_ref.shape[0]
    lines = n_tables * rows
    per = 128 // rows
    g, h = iota((128, 128), 0), iota((128, 128), 1)
    before = ((g < h) & (g // rows == h // rows)).astype(BF16)
    line = iota((lines, 128), 0)
    seat = iota((per * cap, 128), 0)
    lane = iota((per * cap, 128), 1)
    edges = jnp.zeros((lines, 128), F32)
    for group in range(span // 128):
        at = pl.ds(pl.multiple_of(start + group * 128, 128), 128)
        mine = [(owner_ref[r : r + 1, at] == tile) & atmos for r in range(fan)]
        key = jnp.full((1, 128), -1, I32)
        for r in range(fan):
            key = jnp.where(mine[r], table_ref[r : r + 1, at] * rows + dest_ref[r : r + 1, at], key)
        held = (key >= 0).astype(F32)
        rank = mm(jnp.broadcast_to(held, (16, 128)).astype(BF16), before)[:1]
        sits = (rank == (seat % cap).astype(F32)) & (lane // rows == seat // cap) & (held > 0)
        hit = (line == key).astype(BF16)
        arrive = mm_t(sits.astype(BF16), hit)
        arrive_sum[group * per * cap : (group + 1) * per * cap] = arrive
        block, within = group * per + g // rows, g % rows
        column = sum(jnp.where(within == w, i, 0) for i, w in enumerate((0, 1, rows - 2, rows - 1)))
        is_edge = (within < 2) | (within >= rows - 2)
        edges += mm(hit, (is_edge & (h == column * n_tile + block)).astype(BF16))
    arrive = arrive_sum[...]
    plan_ref[PLAN_ARRIVE] = arrive.astype(BF16)
    plan_ref[PLAN_COLLECT] = arrive.T.astype(BF16)
    plan_ref[PLAN_EDGE, :, :128] = edges.astype(BF16)
    for i in range(mask_ref.shape[1] // 128):
        plan_ref[PLAN_EDGE, i * rows : (i + 1) * rows, 128:] = mask_ref[:, i * 128 : (i + 1) * 128].astype(F32).astype(BF16)
    first, placed = own_slots(owner_ref, rows, cap)
    table = table_ref[:, pl.ds(first, 128)]
    for k in range(n_tables):
        here = sum(jnp.where(table[r : r + 1] == k, placed[r], 0.0) for r in range(fan))
        here = here.T
        plan_ref[PLAN_BACK, k * rows : (k + 1) * rows] = sum(here[i : i + rows] for i in range(0, 128, rows)).astype(BF16)


def shifted(x, by):
    row = iota(x.shape, 0)
    return jnp.where(row == (0 if by > 0 else x.shape[0] - 1), 0.0, roll(x, by, 0))


def corrections(coef, edges):
    a0, aa, k0, b1, bb, k1 = coef
    u0, q0, u1, q1 = edges
    b_prev, a_next = shifted(b1, 1), shifted(a0, -1)
    u_prev, q_prev, u_next, q_next = shifted(u1, 1), shifted(q1, 1), shifted(u0, -1), shifted(q0, -1)
    return [
        sideways(a0 * u_prev, k0) + a0 * (q_prev + b_prev * u0),
        aa * u_prev,
        bb * u_next,
        sideways(b1 * u_next, k1) + b1 * (q_next + a_next * u1),
    ]


def whole_level(plane, correction):
    _, tile, _ = place()
    rows = plane.shape[0]
    here = iota(correction[0].shape, 0) == tile
    own = [jnp.sum(jnp.where(here, c, 0.0), axis=0, keepdims=True) for c in correction]
    return jnp.concatenate(
        [plane[:2] + jnp.concatenate(own[:2]), plane[2 : rows - 2], plane[rows - 2 :] + jnp.concatenate(own[2:])]
    )


def water(plan_ref, rows):
    parts = plan_ref.shape[2] // 128
    return jnp.concatenate([plan_ref[PLAN_EDGE, i * rows : (i + 1) * rows, 128:] for i in range(parts)], axis=1).astype(F32)


def grouped_edges(correction, plan_ref):
    short = 128 - correction.shape[0]
    if short:
        correction = jnp.concatenate([correction, jnp.zeros((short, correction.shape[1]), F32)])
    return select_rows(plan_ref[PLAN_EDGE, :, :128], correction, 2)


def flux_of(slots, edges, plan_ref, n_tables, rows):
    grouped = select_rows(plan_ref[PLAN_COLLECT], slots, 2) + edges
    flux = jnp.zeros((rows, slots.shape[1]), F32)
    for k in range(n_tables):
        at = PLAN_WAYS + 2 * k
        flux += product(grouped[k * rows : (k + 1) * rows], plan_ref[at], plan_ref[at + 1])
    return flux


def lines_of(ref, first, count):
    return [ref[:, first + i, :] for i in range(count)]


def flux_kernel(cap, n_tables, got_ref, plan_ref, keep_ref, *refs):
    part_ref = refs[-1]
    _, _, atmos = place()
    n_tile, _, width = got_ref.shape
    rows = part_ref.shape[0]
    stepped = keep_ref[keep_ref.shape[0] - rows :]
    correction = corrections(lines_of(got_ref, cap, N_COEF), lines_of(got_ref, cap + N_COEF, 4))
    whole = whole_level(stepped, correction)
    slots = got_ref[:, :cap, :].reshape(n_tile * cap, width)
    flux = flux_of(slots, grouped_edges(jnp.concatenate(correction), plan_ref), plan_ref, n_tables, rows)
    part_ref[...] = jnp.where(atmos, FORCING * water(plan_ref, rows) * flux, whole)


def levels_kernel(cap, got_ref, fields_ref, coef_ref, top_ref, level_ref):
    _, _, atmos = place()
    kappa, speed = coef_ref[0, 0], coef_ref[0, 1]
    levels, rows, width = fields_ref.shape[1:]
    n_tile = got_ref.shape[0]
    stepped = substep(substep(fields_ref[0], kappa, speed), kappa, speed)
    coef = lines_of(got_ref, cap, N_COEF)
    first, second = [corrections(coef, lines_of(got_ref, cap + N_COEF + 4 * l, 4)) for l in range(2)]
    level_ref[:rows] = jnp.where(atmos, whole_level(stepped[0], first), top_ref[...])
    level_ref[rows : 2 * rows] = whole_level(stepped[1], second)
    level_ref[2 * rows : levels * rows] = stepped[2:].reshape((levels - 2) * rows, width)
    at = levels * rows + 4 * n_tile
    level_ref[levels * rows : at] = jnp.concatenate([x - y for x, y in zip(first, second)])
    level_ref[at:] = padded(
        sum([[u[:1], u[:1], u[rows - 1 :], u[rows - 1 :]] for u in [fields_ref[0, l] for l in range(2, levels)]], []),
        level_ref.shape[0] - at,
        width,
    )


def second_kernel(cap, n_tables, levels, sources, plan_ref, level_ref, *refs):
    swapped, (part_ref, came_ref) = refs[:-2], refs[-2:]
    _, tile, atmos = place()
    n_tile, _, width = came_ref.shape
    rows = part_ref.shape[0]
    edges = level_ref[levels * rows : levels * rows + 4 * n_tile]
    for m, (i, j) in enumerate(sources):
        came_ref[tile ^ m] = swapped[i][j * cap : (j + 1) * cap]
    flux = flux_of(came_ref[...].reshape(n_tile * cap, width), grouped_edges(edges, plan_ref), plan_ref, n_tables, rows)
    part_ref[...] = jnp.where(atmos, FORCING * water(plan_ref, rows) * flux, 0.0)


def finish_kernel(cap, got_ref, level_ref, *refs):
    swapped, whole_ref = refs[:-1], refs[-1]
    _, tile, _ = place()
    levels, rows, width = whole_ref.shape
    n_tile = got_ref.shape[0]
    whole_ref[...] = level_ref[: levels * rows].reshape(levels, rows, width)
    count = 4 * (levels - 2)
    held = n_tile // 2 * cap
    prev = jnp.zeros((count, width), F32)
    after = prev
    for i, ref in enumerate(swapped):
        other = tile ^ (2 ** (i + 1) - 1)
        came = ref[held : held + count]
        prev = jnp.where(other == tile - 1, came, prev)
        after = jnp.where(other == tile + 1, came, after)
    own = got_ref[tile, cap : cap + 8]
    a0, aa, k0, b1, bb, k1 = [own[i : i + 1] for i in range(N_COEF)]
    b_prev = jnp.where(tile > 0, got_ref[jnp.maximum(tile - 1, 0), cap : cap + 8][3:4], 0.0)
    a_next = jnp.where(tile < n_tile - 1, got_ref[jnp.minimum(tile + 1, n_tile - 1), cap : cap + 8][0:1], 0.0)
    for l in range(2, levels):
        u0, _, u1, _ = [level_ref[levels * rows + 4 * n_tile + 4 * (l - 2) + i : levels * rows + 4 * n_tile + 4 * (l - 2) + i + 1] for i in range(4)]
        u_prev, q_prev = [prev[4 * (l - 2) + i : 4 * (l - 2) + i + 1] for i in (2, 3)]
        u_next, q_next = [after[4 * (l - 2) + i : 4 * (l - 2) + i + 1] for i in (0, 1)]
        whole_ref[l, :2] += jnp.concatenate([sideways(a0 * u_prev, k0) + a0 * (q_prev + b_prev * u0), aa * u_prev])
        whole_ref[l, rows - 2 :] += jnp.concatenate([bb * u_next, sideways(b1 * u_next, k1) + b1 * (q_next + a_next * u1)])


def sea_kernel(n_tables, plan_ref, *refs):
    parts, (top_ref, back_ref) = refs[:-2], refs[-2:]
    top = sum(part[...] for part in parts)
    top_ref[...] = top
    sea = water(plan_ref, top.shape[0]) * top
    back_ref[...] = select_rows(plan_ref[PLAN_ARRIVE], jnp.concatenate([sea] * n_tables), 2)


def end_kernel(
    n_tables, came_ref, plan_ref, whole_ref, total_ref, last_ref, fields_hbm, surface_hbm, forced_ref, surface_ref, sems
):
    _, _, atmos = place()
    levels, rows, width = whole_ref.shape
    forced_ref[...] = jnp.where(atmos, whole_ref[1], whole_ref[1] + total_ref[...] + last_ref[...])
    copies = [
        pltpu.make_async_copy(whole_ref.at[pl.ds(2, levels - 2)], fields_hbm.at[0, pl.ds(2, levels - 2)], sems.at[0]),
        pltpu.make_async_copy(whole_ref.at[0], fields_hbm.at[0, 0], sems.at[1]),
        pltpu.make_async_copy(forced_ref, fields_hbm.at[0, 1], sems.at[2]),
        pltpu.make_async_copy(surface_ref, surface_hbm.at[0], sems.at[3]),
    ]
    for copy in copies[:3]:
        copy.start()
    picked = select_rows(plan_ref[PLAN_BACK], came_ref[...], 2)
    seen = jnp.zeros((rows, width), F32)
    for k in range(n_tables):
        at = PLAN_WAYS + 2 * k
        seen += product(picked[k * rows : (k + 1) * rows], plan_ref[at], plan_ref[at + 1], mm_t)
    surface_ref[...] = jnp.where(atmos, seen, water(plan_ref, rows) * whole_ref[0])
    copies[3].start()
    for copy in copies:
        copy.wait()


def call(kernel, n_in, outs, flops=0, scratch=(), space=pltpu.VMEM, out_space=pltpu.VMEM, vmem=12):
    shapes = [jax.ShapeDtypeStruct(s, d) for s, d in outs]
    return pl.pallas_call(
        kernel,
        out_shape=shapes,
        in_specs=[pl.BlockSpec(memory_space=space)] * n_in,
        out_specs=[pl.BlockSpec(memory_space=out_space)] * len(shapes),
        scratch_shapes=scratch,
        compiler_params=pltpu.CompilerParams(vmem_limit_bytes=vmem * 1024 * 1024),
        cost_estimate=pl.CostEstimate(flops=flops, bytes_accessed=1 << 10, transcendentals=0),
    )


def swap_stage(bit, cap, arrays, chunks, after=None):
    n_tile = lax.axis_size("tile")
    going = [m for m in range(n_tile) if m & bit]
    if after is not None:
        arrays, after = lax.optimization_barrier((arrays, after))
    if bit == 1:
        give = arrays.pop()
    else:
        picks = [chunks[m] for m in going]
        used = sorted({i for i, _ in picks})
        picks = [(used.index(i), j) for i, j in picks]
        taken = [arrays[i] for i in used]
        if used[-1] != len(arrays) - 1:
            taken.append(arrays[-1])
        kernel = functools.partial(stack_kernel, picks, cap)
        (give,) = call(kernel, len(taken), [(arrays[-1].shape, F32)])(*taken)
    came = lax.ppermute(give, "tile", [(t, t ^ bit) for t in range(n_tile)])
    chunks = chunks | {m: (len(arrays), i) for i, m in enumerate(going)}
    return arrays + [came], chunks, after


def local(fields, coefficients, owner_tile, dest_block, table_index, tables, land_mask):
    n_sec, n_tile = lax.axis_size("sec"), lax.axis_size("tile")
    levels, rows, width = fields.shape[1:]
    fan = owner_tile.shape[1]
    n_tables = tables.shape[0]
    cap = 2 * fan * rows // n_tile
    slots, lines = n_tile * cap, n_tables * rows
    up8 = lambda n: -(-n // 8) * 8
    chunk, side = up8(cap + N_COEF + 8), up8(4 * (levels - 2))
    owner, dest, table = owner_tile.T, dest_block.T, table_index.T
    exchange = lambda x, axis: lax.all_to_all(x, axis, split_axis=0, concat_axis=0, tiled=True)
    plane = ((rows, width), F32)

    (send,) = call(
        functools.partial(send_kernel, cap),
        3,
        [((n_tile, chunk, width), F32)],
        scratch=[
            pltpu.VMEM((2, rows, width), F32),
            pltpu.VMEM((2, rows, width), F32),
            pltpu.VMEM(owner.shape, I32),
            pltpu.SemaphoreType.DMA((3,)),
        ],
        space=pltpu.HBM,
        vmem=60,
    )(fields, coefficients, owner)
    got = exchange(send, "tile")
    half = n_tile // 2 * cap
    keep, give = call(
        functools.partial(swap_kernel, cap),
        3,
        [((half + rows, width), F32), ((half + side, width), F32)],
        scratch=[pltpu.VMEM((n_tile, cap, width), F32)],
    )(fields, coefficients, owner)
    arrays, chunks, _ = swap_stage(1, cap, [keep, give], {m: (0, m // 2) for m in range(0, n_tile, 2)})
    (plan,) = call(
        functools.partial(index_kernel, cap, rows),
        5,
        [((PLAN_WAYS + 2 * n_tables, lines, width), BF16)],
        scratch=[pltpu.VMEM((slots, lines), F32)],
    )(owner, dest, table, tables, land_mask)
    arrays, chunks, plan = swap_stage(2, cap, arrays, chunks, plan)
    (part,) = call(functools.partial(flux_kernel, cap, n_tables), 1 + len(arrays), [plane])(got, plan, *arrays[:-1])
    others = [lax.ppermute(part, "sec", [(s, s ^ other) for s in range(n_sec)]) for other in range(n_sec - 1, 0, -1)]
    bit = 4
    while bit < n_tile:
        arrays, chunks, part = swap_stage(bit, cap, arrays, chunks, part)
        bit *= 2
    sources = [chunks[m] for m in range(n_tile)]
    top, back = call(functools.partial(sea_kernel, n_tables), 1 + n_sec, [plane, ((slots, width), F32)])(plan, part, *others)
    got, back = lax.optimization_barrier((got, back))
    (level,) = call(
        functools.partial(levels_kernel, cap), 4, [((levels * rows + 4 * n_tile + side, width), F32)], flops=1 << 32
    )(got, fields, coefficients, top)
    came = exchange(back.reshape(n_tile, cap, width), "tile").reshape(slots, width)
    (total,) = call(
        functools.partial(second_kernel, cap, n_tables, levels, sources),
        2 + len(arrays),
        [plane],
        scratch=[pltpu.VMEM((n_tile, cap, width), F32)],
        flops=1 << 34,
    )(plan, level, *arrays)
    came_total = 0.0
    bit = 1
    while bit < n_sec:
        pairs = [(s, s | bit) for s in range(n_sec) if (s & (2 * bit - 1)) == bit - 1]
        total = total + came_total
        came_total = lax.ppermute(total, "sec", pairs)
        bit *= 2
    (whole,) = call(
        functools.partial(finish_kernel, cap), 1 + len(arrays), [((levels, rows, width), F32)], flops=1 << 28
    )(got, level, *arrays[1:])
    return call(
        functools.partial(end_kernel, n_tables),
        5,
        [(fields.shape, F32), ((1, rows, width), F32)],
        scratch=[pltpu.VMEM((rows, width), F32)] * 2 + [pltpu.SemaphoreType.DMA((4,))],
        out_space=pltpu.HBM,
    )(came, plan, whole, total, came_total)


def solution(mesh):
    placed = (P("sec", None, "tile", None), P("sec", None, "tile", None), P(), P(), P(), P(), P("tile", None))
    return jax.shard_map(
        local,
        mesh=mesh,
        in_specs=placed,
        out_specs=(P("sec", None, "tile", None), P("sec", "tile", None)),
        check_vma=False,
    )
```

```python
import functools

import jax
import jax.numpy as jnp
from jax import lax
from jax.experimental import pallas as pl
from jax.experimental.pallas import tpu as pltpu
from jax.sharding import PartitionSpec as P

FORCING = 0.5
F32, BF16, I32 = jnp.float32, jnp.bfloat16, jnp.int32
N_COEF = 6
EDGES = 16
PLAN_COLLECT, PLAN_ARRIVE, PLAN_EDGE, PLAN_BACK, PLAN_WAYS = 0, 1, 2, 3, 4


def iota(shape, axis):
    return lax.broadcasted_iota(I32, shape, axis)


def roll(x, shift, axis):
    return pltpu.roll(x, shift % x.shape[axis], axis)


def split(x, parts):
    out = []
    for _ in range(parts):
        out.append(x.astype(BF16))
        x = x - out[-1].astype(F32)
    return out


def mm(a, b):
    return lax.dot_general(a, b, (((1,), (0,)), ((), ())), preferred_element_type=F32)


def mm_t(a, b):
    return lax.dot_general(a, b, (((1,), (1,)), ((), ())), preferred_element_type=F32)


def select_rows(hot, x, parts):
    return sum(mm(hot, p) for p in split(x, parts))


def product(a, b1, b2, dot=mm):
    a1, a2 = split(a, 2)
    rows = a.shape[0]
    both = dot(jnp.concatenate([a1, a2]), b1)
    return both[:rows] + both[rows:] + dot(a1, b2)


def sideways(x, kappa):
    return x + kappa * (roll(x, 1, x.ndim - 1) + roll(x, -1, x.ndim - 1) - 4.0 * x)


def substep(u, kappa, speed):
    rows = u.shape[1]
    row = iota(u.shape, 1)
    upper = jnp.where(row == 0, 0.0, roll(u, 1, 1))
    lower = jnp.where(row == rows - 1, 0.0, roll(u, -1, 1))
    laplace = upper + lower + roll(u, 1, 2) + roll(u, -1, 2) - 4.0 * u
    return u + kappa * laplace - 0.5 * speed * (lower - upper)


def place():
    sec, tile = lax.axis_index("sec"), lax.axis_index("tile")
    return sec, tile, sec < lax.axis_size("sec") - 1


def own_slots(owner_ref, rows, cap):
    sec, tile, atmos = place()
    n_sec, n_tile = lax.axis_size("sec"), lax.axis_size("tile")
    block = (jnp.minimum(sec, n_sec - 2) * n_tile + tile) * rows
    first = pl.multiple_of(block // 128 * 128, 128)
    half = block - first
    shape = (n_tile * cap, 128)
    lane = iota((1, 128), 1)
    inside = (lane >= half) & (lane < half + rows) & atmos
    owner = jnp.where(inside, owner_ref[:, pl.ds(first, 128)], -1)
    slot = iota(shape, 0)
    hot = [(owner[r : r + 1] == slot // cap).astype(F32) for r in range(owner.shape[0])]
    both = sum(hot)
    before = (iota((128, 128), 0) < iota((128, 128), 1)).astype(BF16)
    rank = mm(both.astype(BF16), before)
    placed = rank == (slot % cap).astype(F32)
    return first, [jnp.where(placed, h, 0.0) for h in hot]


def edge_rows(u, kappa, a, b):
    top, bot = slice(0, 1), slice(u.shape[0] - 1, u.shape[0])
    q_top = sideways(u[top], kappa[top]) + b[top] * u[1:2]
    q_bot = sideways(u[bot], kappa[bot]) + a[bot] * u[-2:-1]
    return [u[top], q_top, u[bot], q_bot]


def padded(lines, count, width):
    if count > len(lines):
        lines = lines + [jnp.zeros((count - len(lines), width), F32)]
    return jnp.concatenate(lines)


def placed_rows(placed, payload):
    return select_rows(sum(placed).astype(BF16), jnp.concatenate([payload] * (128 // payload.shape[0])), 2)


def send_kernel(cap, fields_hbm, coef_hbm, owner_hbm, *refs):
    outs, (fields_ref, coef_ref, owner_ref, slots_ref, sems) = refs[:-5], refs[-5:]
    pairs = ((owner_hbm, owner_ref), (coef_hbm.at[0], coef_ref), (fields_hbm.at[0], fields_ref))
    copies = [pltpu.make_async_copy(src, dst, sems.at[i]) for i, (src, dst) in enumerate(pairs)]
    for copy in copies:
        copy.start()
    copies[0].wait()
    _, tile, _ = place()
    levels, rows, width = fields_ref.shape
    _, placed = own_slots(owner_ref, rows, cap)
    copies[1].wait()
    copies[2].wait()
    u = fields_ref[...]
    kappa, speed = coef_ref[0], coef_ref[1]
    stepped = substep(substep(u[:2], kappa, speed), kappa, speed)
    both = placed_rows(placed, jnp.concatenate([stepped[0], stepped[0] - stepped[1]], axis=1))
    n_tile = slots_ref.shape[0]
    slots_ref[:, :cap] = both[:, :width].reshape(n_tile, cap, width)
    slots_ref[:, cap:] = both[:, width:].reshape(n_tile, cap, width)
    a = kappa + 0.5 * speed
    b = kappa - 0.5 * speed
    bot = slice(rows - 1, rows)
    extra = [a[0:1], a[0:1] * a[1:2], kappa[0:1], b[bot], b[bot] * b[rows - 2 : rows - 1], kappa[bot]]
    extra += edge_rows(u[0], kappa, a, b) + edge_rows(u[1], kappa, a, b)
    extra = padded(extra, EDGES, width)
    near = sum([edge_rows(u[l], kappa, a, b) for l in range(2, levels)], [])
    near = padded(near, outs[0].shape[0] - 2 * cap - EDGES, width)
    for m, out_ref in enumerate(outs):
        out_ref[: 2 * cap] = slots_ref[tile ^ m]
        out_ref[2 * cap : 2 * cap + EDGES] = extra
        if m & (m + 1) == 0:
            out_ref[2 * cap + EDGES :] = near


def index_kernel(
    cap, rows, owner_ref, dest_ref, table_ref, tables_ref, mask_ref, plan_ref, arrive_sum
):
    n_tables = tables_ref.shape[0]
    for k in range(n_tables):
        at = PLAN_WAYS + 2 * k
        plan_ref[at], plan_ref[at + 1] = split(tables_ref[k], 2)
    sec, tile, atmos = place()
    n_sec, n_tile = lax.axis_size("sec"), lax.axis_size("tile")
    span = n_tile * rows
    start = jnp.minimum(sec, n_sec - 2) * span
    fan = owner_ref.shape[0]
    lines = n_tables * rows
    per = 128 // rows
    g, h = iota((128, 128), 0), iota((128, 128), 1)
    before = ((g < h) & (g // rows == h // rows)).astype(BF16)
    line = iota((lines, 128), 0)
    seat = iota((per * cap, 128), 0)
    lane = iota((per * cap, 128), 1)
    edges = jnp.zeros((lines, 128), F32)
    for group in range(span // 128):
        at = pl.ds(pl.multiple_of(start + group * 128, 128), 128)
        mine = [(owner_ref[r : r + 1, at] == tile) & atmos for r in range(fan)]
        key = jnp.full((1, 128), -1, I32)
        for r in range(fan):
            key = jnp.where(mine[r], table_ref[r : r + 1, at] * rows + dest_ref[r : r + 1, at], key)
        held = (key >= 0).astype(F32)
        rank = mm(jnp.broadcast_to(held, (16, 128)).astype(BF16), before)[:1]
        sits = (rank == (seat % cap).astype(F32)) & (lane // rows == seat // cap) & (held > 0)
        hit = (line == key).astype(BF16)
        arrive = mm_t(sits.astype(BF16), hit)
        arrive_sum[group * per * cap : (group + 1) * per * cap] = arrive
        block, within = group * per + g // rows, g % rows
        column = sum(jnp.where(within == w, i, 0) for i, w in enumerate((0, 1, rows - 2, rows - 1)))
        is_edge = (within < 2) | (within >= rows - 2)
        edges += mm(hit, (is_edge & (h == column * n_tile + block)).astype(BF16))
    arrive = arrive_sum[...]
    plan_ref[PLAN_ARRIVE] = arrive.astype(BF16)
    plan_ref[PLAN_COLLECT] = arrive.T.astype(BF16)
    plan_ref[PLAN_EDGE, :, :128] = edges.astype(BF16)
    for i in range(mask_ref.shape[1] // 128):
        plan_ref[PLAN_EDGE, i * rows : (i + 1) * rows, 128:] = mask_ref[:, i * 128 : (i + 1) * 128].astype(F32).astype(BF16)
    first, placed = own_slots(owner_ref, rows, cap)
    table = table_ref[:, pl.ds(first, 128)]
    for k in range(n_tables):
        here = sum(jnp.where(table[r : r + 1] == k, placed[r], 0.0) for r in range(fan))
        here = here.T
        plan_ref[PLAN_BACK, k * rows : (k + 1) * rows] = sum(here[i : i + rows] for i in range(0, 128, rows)).astype(BF16)


def shifted(x, by):
    row = iota(x.shape, 0)
    return jnp.where(row == (0 if by > 0 else x.shape[0] - 1), 0.0, roll(x, by, 0))


def corrections(coef, edges):
    a0, aa, k0, b1, bb, k1 = coef
    u0, q0, u1, q1 = edges
    b_prev, a_next = shifted(b1, 1), shifted(a0, -1)
    u_prev, q_prev, u_next, q_next = shifted(u1, 1), shifted(q1, 1), shifted(u0, -1), shifted(q0, -1)
    return [
        sideways(a0 * u_prev, k0) + a0 * (q_prev + b_prev * u0),
        aa * u_prev,
        bb * u_next,
        sideways(b1 * u_next, k1) + b1 * (q_next + a_next * u1),
    ]


def whole_level(plane, correction):
    _, tile, _ = place()
    rows = plane.shape[0]
    here = iota(correction[0].shape, 0) == tile
    own = [jnp.sum(jnp.where(here, c, 0.0), axis=0, keepdims=True) for c in correction]
    return jnp.concatenate(
        [plane[:2] + jnp.concatenate(own[:2]), plane[2 : rows - 2], plane[rows - 2 :] + jnp.concatenate(own[2:])]
    )


def water(plan_ref, rows):
    parts = plan_ref.shape[2] // 128
    return jnp.concatenate([plan_ref[PLAN_EDGE, i * rows : (i + 1) * rows, 128:] for i in range(parts)], axis=1).astype(F32)


def grouped_edges(correction, plan_ref):
    short = 128 - correction.shape[0]
    if short:
        correction = jnp.concatenate([correction, jnp.zeros((short, correction.shape[1]), F32)])
    return select_rows(plan_ref[PLAN_EDGE, :, :128], correction, 2)


def lines_of(ref, first, count):
    return [ref[:, first + i, :] for i in range(count)]


def flux_kernel(cap, n_tables, plan_ref, coef_ref, fields_ref, *refs):
    came, (first_ref, second_ref, edge_ref, slots_ref) = refs[:-4], refs[-4:]
    _, tile, atmos = place()
    n_tile, _, width = slots_ref.shape
    rows = first_ref.shape[0]
    for m, ref in enumerate(came):
        slots_ref[tile ^ m] = ref[: 2 * cap]
        edge_ref[tile ^ m, : ref.shape[0] - 2 * cap] = ref[2 * cap :]
    coef = lines_of(edge_ref, 0, N_COEF)
    added = [corrections(coef, lines_of(edge_ref, N_COEF + 4 * l, 4)) for l in range(2)]
    first, second = [jnp.concatenate(x) for x in added]
    edges = grouped_edges(jnp.concatenate([first, first - second], axis=1), plan_ref)
    slots = jnp.concatenate([slots_ref[:, :cap], slots_ref[:, cap:]], axis=2).reshape(n_tile * cap, 2 * width)
    grouped = select_rows(plan_ref[PLAN_COLLECT], slots, 2) + edges
    flux = jnp.zeros((2 * rows, width), F32)
    for k in range(n_tables):
        at = PLAN_WAYS + 2 * k
        lines = grouped[k * rows : (k + 1) * rows]
        flux += product(jnp.concatenate([lines[:, :width], lines[:, width:]]), plan_ref[at], plan_ref[at + 1])
    half = FORCING * water(plan_ref, rows)
    kappa, speed = coef_ref[0, 0], coef_ref[0, 1]
    stepped = substep(substep(fields_ref[0, :1], kappa, speed), kappa, speed)[0]
    first_ref[...] = jnp.where(atmos, half * flux[:rows], whole_level(stepped, added[0]))
    second_ref[...] = jnp.where(atmos, half * flux[rows:], 0.0)


def levels_kernel(edge_ref, fields_ref, coef_ref, top_ref, whole_ref):
    _, tile, atmos = place()
    kappa, speed = coef_ref[0, 0], coef_ref[0, 1]
    levels, rows, width = fields_ref.shape[1:]
    n_tile = edge_ref.shape[0]
    stepped = substep(substep(fields_ref[0], kappa, speed), kappa, speed)
    before, after = jnp.maximum(tile - 1, 0), jnp.minimum(tile + 1, n_tile - 1)
    own = edge_ref[tile, :8]
    a0, aa, k0, b1, bb, k1 = [own[i : i + 1] for i in range(N_COEF)]
    b_prev = jnp.where(tile > 0, edge_ref[before, :8][3:4], 0.0)
    a_next = jnp.where(tile < n_tile - 1, edge_ref[after, :8][0:1], 0.0)
    for l in range(levels):
        at = N_COEF + 4 * l if l < 2 else EDGES + 4 * (l - 2)
        base, off = at // 8 * 8, at % 8
        prev = jnp.where(tile > 0, edge_ref[before, base : base + 8], 0.0)
        next_ = jnp.where(tile < n_tile - 1, edge_ref[after, base : base + 8], 0.0)
        if off > 4:
            prev = jnp.concatenate([prev, jnp.where(tile > 0, edge_ref[before, base + 8 : base + 16], 0.0)])
            next_ = jnp.concatenate([next_, jnp.where(tile < n_tile - 1, edge_ref[after, base + 8 : base + 16], 0.0)])
        u_prev, q_prev = prev[off + 2 : off + 3], prev[off + 3 : off + 4]
        u_next, q_next = next_[off : off + 1], next_[off + 1 : off + 2]
        u0, u1 = fields_ref[0, l, :1], fields_ref[0, l, rows - 1 :]
        top = jnp.concatenate([sideways(a0 * u_prev, k0) + a0 * (q_prev + b_prev * u0), aa * u_prev])
        bottom = jnp.concatenate([bb * u_next, sideways(b1 * u_next, k1) + b1 * (q_next + a_next * u1)])
        plane = jnp.concatenate([stepped[l, :2] + top, stepped[l, 2 : rows - 2], stepped[l, rows - 2 :] + bottom])
        whole_ref[l] = jnp.where(atmos, plane, top_ref[...]) if l == 0 else plane


def sea_kernel(n_parts, n_tables, plan_ref, *refs):
    parts, top_ref, outs, slots_ref = refs[:n_parts], refs[n_parts], refs[n_parts + 1 : -1], refs[-1]
    _, tile, _ = place()
    top = sum(part[...] for part in parts)
    top_ref[...] = top
    sea = water(plan_ref, top.shape[0]) * top
    slots_ref[...] = select_rows(plan_ref[PLAN_ARRIVE], jnp.concatenate([sea] * n_tables), 2).reshape(slots_ref.shape)
    for m, out_ref in enumerate(outs):
        out_ref[...] = slots_ref[tile ^ m]


def end_kernel(n_tables, plan_ref, whole_ref, total_ref, last_ref, *refs):
    came, (fields_hbm, surface_hbm, forced_ref, surface_ref, slots_ref, sems) = refs[:-6], refs[-6:]
    _, tile, atmos = place()
    levels, rows, width = whole_ref.shape
    forced_ref[...] = jnp.where(atmos, whole_ref[1], whole_ref[1] + total_ref[...] + last_ref[...])
    copies = [
        pltpu.make_async_copy(whole_ref.at[pl.ds(2, levels - 2)], fields_hbm.at[0, pl.ds(2, levels - 2)], sems.at[0]),
        pltpu.make_async_copy(whole_ref.at[0], fields_hbm.at[0, 0], sems.at[1]),
        pltpu.make_async_copy(forced_ref, fields_hbm.at[0, 1], sems.at[2]),
        pltpu.make_async_copy(surface_ref, surface_hbm.at[0], sems.at[3]),
    ]
    for copy in copies[:3]:
        copy.start()
    for m, ref in enumerate(came):
        slots_ref[tile ^ m] = ref[...]
    picked = select_rows(plan_ref[PLAN_BACK], slots_ref[...].reshape(-1, width), 2)
    seen = jnp.zeros((rows, width), F32)
    for k in range(n_tables):
        at = PLAN_WAYS + 2 * k
        seen += product(picked[k * rows : (k + 1) * rows], plan_ref[at], plan_ref[at + 1], mm_t)
    surface_ref[...] = jnp.where(atmos, seen, water(plan_ref, rows) * whole_ref[0])
    copies[3].start()
    for copy in copies:
        copy.wait()


def call(kernel, n_in, outs, flops=0, scratch=(), space=pltpu.VMEM, out_space=pltpu.VMEM, vmem=12):
    shapes = [jax.ShapeDtypeStruct(s, d) for s, d in outs]
    return pl.pallas_call(
        kernel,
        out_shape=shapes,
        in_specs=[pl.BlockSpec(memory_space=space)] * n_in,
        out_specs=[pl.BlockSpec(memory_space=out_space)] * len(shapes),
        scratch_shapes=scratch,
        compiler_params=pltpu.CompilerParams(vmem_limit_bytes=vmem * 1024 * 1024),
        cost_estimate=pl.CostEstimate(flops=flops, bytes_accessed=1 << 10, transcendentals=0),
    )


def to_all(arrays):
    n_tile = len(arrays)
    came = {m: lax.ppermute(arrays[m], "tile", [(t, t ^ m) for t in range(n_tile)]) for m in range(n_tile - 1, 0, -1)}
    return [arrays[0]] + [came[m] for m in range(1, n_tile)]


def local(fields, coefficients, owner_tile, dest_block, table_index, tables, land_mask):
    n_sec, n_tile = lax.axis_size("sec"), lax.axis_size("tile")
    levels, rows, width = fields.shape[1:]
    fan = owner_tile.shape[1]
    n_tables = tables.shape[0]
    cap = 2 * fan * rows // n_tile
    slots, lines = n_tile * cap, n_tables * rows
    owner, dest, table = owner_tile.T, dest_block.T, table_index.T
    plane = ((rows, width), F32)
    near = -(-4 * (levels - 2) // 8) * 8

    sent = call(
        functools.partial(send_kernel, cap),
        3,
        [((2 * cap + EDGES + (near if m & (m + 1) == 0 else 0), width), F32) for m in range(n_tile)],
        scratch=[
            pltpu.VMEM((levels, rows, width), F32),
            pltpu.VMEM((2, rows, width), F32),
            pltpu.VMEM(owner.shape, I32),
            pltpu.VMEM((n_tile, 2 * cap, width), F32),
            pltpu.SemaphoreType.DMA((3,)),
        ],
        space=pltpu.HBM,
        vmem=60,
    )(fields, coefficients, owner)
    got = to_all(sent)
    (plan,) = call(
        functools.partial(index_kernel, cap, rows),
        5,
        [((PLAN_WAYS + 2 * n_tables, lines, width), BF16)],
        scratch=[pltpu.VMEM((slots, lines), F32)],
    )(owner, dest, table, tables, land_mask)
    first, second, edge = call(
        functools.partial(flux_kernel, cap, n_tables),
        3 + n_tile,
        [plane, plane, ((n_tile, EDGES + near, width), F32)],
        scratch=[pltpu.VMEM((n_tile, 2 * cap, width), F32)],
    )(plan, coefficients, fields, *got)
    others = [lax.ppermute(first, "sec", [(s, s ^ other) for s in range(n_sec)]) for other in range(n_sec - 1, 0, -1)]
    top, *back = call(
        functools.partial(sea_kernel, n_sec, n_tables),
        1 + n_sec,
        [plane] + [((cap, width), F32)] * n_tile,
        scratch=[pltpu.VMEM((n_tile, cap, width), F32)],
    )(plan, first, *others)
    came = to_all(back)
    total, top = lax.optimization_barrier((second, top))
    last = 0.0
    bit = 1
    while bit < n_sec:
        pairs = [(s, s | bit) for s in range(n_sec) if (s & (2 * bit - 1)) == bit - 1]
        total = total + last
        last = lax.ppermute(total, "sec", pairs)
        bit *= 2
    (whole,) = call(levels_kernel, 4, [((levels, rows, width), F32)])(edge, fields, coefficients, top)
    return call(
        functools.partial(end_kernel, n_tables),
        4 + n_tile,
        [(fields.shape, F32), ((1, rows, width), F32)],
        scratch=[
            pltpu.VMEM((rows, width), F32),
            pltpu.VMEM((rows, width), F32),
            pltpu.VMEM((n_tile, cap, width), F32),
            pltpu.SemaphoreType.DMA((4,)),
        ],
        out_space=pltpu.HBM,
    )(plan, whole, total, last, *came)


def solution(mesh):
    placed = (P("sec", None, "tile", None), P("sec", None, "tile", None), P(), P(), P(), P(), P("tile", None))
    return jax.shard_map(
        local,
        mesh=mesh,
        in_specs=placed,
        out_specs=(P("sec", None, "tile", None), P("sec", "tile", None)),
        check_vma=False,
    )
```

```python
import functools

import jax
import jax.numpy as jnp
from jax import lax
from jax.experimental import pallas as pl
from jax.experimental.pallas import tpu as pltpu
from jax.sharding import PartitionSpec as P

FORCING = 0.5
F32, BF16, I32 = jnp.float32, jnp.bfloat16, jnp.int32
N_COEF = 6
PLAN_COLLECT, PLAN_ARRIVE, PLAN_EDGE, PLAN_BACK, PLAN_WAYS = 0, 1, 2, 3, 4


def iota(shape, axis):
    return lax.broadcasted_iota(I32, shape, axis)


def roll(x, shift, axis):
    return pltpu.roll(x, shift % x.shape[axis], axis)


def split(x, parts):
    out = []
    for _ in range(parts):
        out.append(x.astype(BF16))
        x = x - out[-1].astype(F32)
    return out


def mm(a, b):
    return lax.dot_general(a, b, (((1,), (0,)), ((), ())), preferred_element_type=F32)


def mm_t(a, b):
    return lax.dot_general(a, b, (((1,), (1,)), ((), ())), preferred_element_type=F32)


def select_rows(hot, x, parts):
    return sum(mm(hot, p) for p in split(x, parts))


def product(a, b1, b2, dot=mm):
    a1, a2 = split(a, 2)
    rows = a.shape[0]
    both = dot(jnp.concatenate([a1, a2]), b1)
    return both[:rows] + both[rows:] + dot(a1, b2)


def sideways(x, kappa):
    return x + kappa * (roll(x, 1, x.ndim - 1) + roll(x, -1, x.ndim - 1) - 4.0 * x)


def substep(u, kappa, speed):
    rows = u.shape[1]
    row = iota(u.shape, 1)
    upper = jnp.where(row == 0, 0.0, roll(u, 1, 1))
    lower = jnp.where(row == rows - 1, 0.0, roll(u, -1, 1))
    laplace = upper + lower + roll(u, 1, 2) + roll(u, -1, 2) - 4.0 * u
    return u + kappa * laplace - 0.5 * speed * (lower - upper)


def place():
    sec, tile = lax.axis_index("sec"), lax.axis_index("tile")
    return sec, tile, sec < lax.axis_size("sec") - 1


def own_slots(owner_ref, rows, cap):
    sec, tile, atmos = place()
    n_sec, n_tile = lax.axis_size("sec"), lax.axis_size("tile")
    block = (jnp.minimum(sec, n_sec - 2) * n_tile + tile) * rows
    first = pl.multiple_of(block // 128 * 128, 128)
    half = block - first
    shape = (n_tile * cap, 128)
    lane = iota((1, 128), 1)
    inside = (lane >= half) & (lane < half + rows) & atmos
    owner = jnp.where(inside, owner_ref[:, pl.ds(first, 128)], -1)
    slot = iota(shape, 0)
    hot = [(owner[r : r + 1] == n_tile - 1 - slot // cap).astype(F32) for r in range(owner.shape[0])]
    both = sum(hot)
    before = (iota((128, 128), 0) < iota((128, 128), 1)).astype(BF16)
    rank = mm(both.astype(BF16), before)
    placed = rank == (slot % cap).astype(F32)
    return first, [jnp.where(placed, h, 0.0) for h in hot]


def edge_rows(u, kappa, a, b):
    top, bot = slice(0, 1), slice(u.shape[0] - 1, u.shape[0])
    q_top = sideways(u[top], kappa[top]) + b[top] * u[1:2]
    q_bot = sideways(u[bot], kappa[bot]) + a[bot] * u[-2:-1]
    return [u[top], q_top, u[bot], q_bot]


def padded(lines, count, width):
    if count > len(lines):
        lines = lines + [jnp.zeros((count - len(lines), width), F32)]
    return jnp.concatenate(lines)


def placed_rows(placed, payload):
    return select_rows(sum(placed).astype(BF16), jnp.concatenate([payload] * (128 // payload.shape[0])), 2)


def send_kernel(cap, fields_hbm, coef_hbm, owner_hbm, send_ref, fields_ref, coef_ref, owner_ref, sems):
    pairs = ((owner_hbm, owner_ref), (coef_hbm.at[0], coef_ref), (fields_hbm.at[0, pl.ds(0, 2)], fields_ref))
    copies = [pltpu.make_async_copy(src, dst, sems.at[i]) for i, (src, dst) in enumerate(pairs)]
    for copy in copies:
        copy.start()
    copies[0].wait()
    _, rows, width = fields_ref.shape
    _, placed = own_slots(owner_ref, rows, cap)
    copies[1].wait()
    copies[2].wait()
    u = fields_ref[...]
    kappa, speed = coef_ref[0], coef_ref[1]
    stepped = substep(substep(u[:1], kappa, speed), kappa, speed)[0]
    n_tile = send_ref.shape[0]
    send_ref[:, :cap] = placed_rows(placed, stepped).reshape(n_tile, cap, width)
    a = kappa + 0.5 * speed
    b = kappa - 0.5 * speed
    bot = slice(rows - 1, rows)
    extra = [a[0:1], a[0:1] * a[1:2], kappa[0:1], b[bot], b[bot] * b[rows - 2 : rows - 1], kappa[bot]]
    extra += edge_rows(u[0], kappa, a, b) + edge_rows(u[1], kappa, a, b)
    extra = padded(extra, send_ref.shape[1] - cap, width)
    send_ref[:, cap:] = jnp.broadcast_to(extra[None], (n_tile,) + extra.shape)


def swap_kernel(cap, fields_ref, coef_ref, owner_ref, keep_ref, give_ref, slots_ref):
    _, tile, _ = place()
    levels, rows, width = fields_ref.shape[1:]
    _, placed = own_slots(owner_ref, rows, cap)
    kappa, speed = coef_ref[0, 0], coef_ref[0, 1]
    stepped = substep(substep(fields_ref[0, :2], kappa, speed), kappa, speed)
    count = slots_ref.shape[0]
    slots_ref[...] = placed_rows(placed, stepped[0] - stepped[1]).reshape(count, cap, width)
    for m in range(count):
        ref = (keep_ref, give_ref)[m % 2]
        ref[m // 2 * cap : (m // 2 + 1) * cap] = slots_ref[count - 1 - (tile ^ m)]
    a = kappa + 0.5 * speed
    b = kappa - 0.5 * speed
    extra = sum([edge_rows(fields_ref[0, l], kappa, a, b) for l in range(2, levels)], [])
    held = count // 2 * cap
    give_ref[held:] = padded(extra, give_ref.shape[0] - held, width)
    keep_ref[held:] = stepped[0]


def stack_kernel(picks, cap, *refs):
    out_ref = refs[-1]
    for to, (i, j) in enumerate(picks):
        out_ref[to * cap : (to + 1) * cap] = refs[i][j * cap : (j + 1) * cap]
    held = len(picks) * cap
    out_ref[held:] = refs[-2][held:]


def index_kernel(
    cap, rows, owner_ref, dest_ref, table_ref, tables_ref, mask_ref, plan_ref, arrive_sum
):
    n_tables = tables_ref.shape[0]
    for k in range(n_tables):
        at = PLAN_WAYS + 2 * k
        plan_ref[at], plan_ref[at + 1] = split(tables_ref[k], 2)
    sec, tile, atmos = place()
    n_sec, n_tile = lax.axis_size("sec"), lax.axis_size("tile")
    span = n_tile * rows
    start = jnp.minimum(sec, n_sec - 2) * span
    fan = owner_ref.shape[0]
    lines = n_tables * rows
    per = 128 // rows
    g, h = iota((128, 128), 0), iota((128, 128), 1)
    before = ((g < h) & (g // rows == h // rows)).astype(BF16)
    line = iota((lines, 128), 0)
    seat = iota((per * cap, 128), 0)
    lane = iota((per * cap, 128), 1)
    edges = jnp.zeros((lines, 128), F32)
    for group in range(span // 128):
        at = pl.ds(pl.multiple_of(start + group * 128, 128), 128)
        mine = [(owner_ref[r : r + 1, at] == tile) & atmos for r in range(fan)]
        key = jnp.full((1, 128), -1, I32)
        for r in range(fan):
            key = jnp.where(mine[r], table_ref[r : r + 1, at] * rows + dest_ref[r : r + 1, at], key)
        held = (key >= 0).astype(F32)
        rank = mm(jnp.broadcast_to(held, (16, 128)).astype(BF16), before)[:1]
        sits = (rank == (seat % cap).astype(F32)) & (lane // rows == per - 1 - seat // cap) & (held > 0)
        hit = (line == key).astype(BF16)
        arrive = mm_t(sits.astype(BF16), hit)
        last = (n_tile - group * per) * cap
        arrive_sum[last - per * cap : last] = arrive
        block, within = group * per + g // rows, g % rows
        column = sum(jnp.where(within == w, i, 0) for i, w in enumerate((0, 1, rows - 2, rows - 1)))
        is_edge = (within < 2) | (within >= rows - 2)
        edges += mm(hit, (is_edge & (h == column * n_tile + n_tile - 1 - block)).astype(BF16))
    arrive = arrive_sum[...]
    plan_ref[PLAN_ARRIVE] = arrive.astype(BF16)
    plan_ref[PLAN_COLLECT] = arrive.T.astype(BF16)
    plan_ref[PLAN_EDGE, :, :128] = edges.astype(BF16)
    for i in range(mask_ref.shape[1] // 128):
        plan_ref[PLAN_EDGE, i * rows : (i + 1) * rows, 128:] = mask_ref[:, i * 128 : (i + 1) * 128].astype(F32).astype(BF16)
    first, placed = own_slots(owner_ref, rows, cap)
    table = table_ref[:, pl.ds(first, 128)]
    for k in range(n_tables):
        here = sum(jnp.where(table[r : r + 1] == k, placed[r], 0.0) for r in range(fan))
        here = here.T
        plan_ref[PLAN_BACK, k * rows : (k + 1) * rows] = sum(here[i : i + rows] for i in range(0, 128, rows)).astype(BF16)


def shifted(x, by):
    row = iota(x.shape, 0)
    return jnp.where(row == (0 if by > 0 else x.shape[0] - 1), 0.0, roll(x, by, 0))


def corrections(coef, edges):
    a0, aa, k0, b1, bb, k1 = coef
    u0, q0, u1, q1 = edges
    b_prev, a_next = shifted(b1, -1), shifted(a0, 1)
    u_prev, q_prev, u_next, q_next = shifted(u1, -1), shifted(q1, -1), shifted(u0, 1), shifted(q0, 1)
    return [
        sideways(a0 * u_prev, k0) + a0 * (q_prev + b_prev * u0),
        aa * u_prev,
        bb * u_next,
        sideways(b1 * u_next, k1) + b1 * (q_next + a_next * u1),
    ]


def whole_level(plane, correction):
    _, tile, _ = place()
    rows = plane.shape[0]
    here = iota(correction[0].shape, 0) == correction[0].shape[0] - 1 - tile
    own = [jnp.sum(jnp.where(here, c, 0.0), axis=0, keepdims=True) for c in correction]
    return jnp.concatenate(
        [plane[:2] + jnp.concatenate(own[:2]), plane[2 : rows - 2], plane[rows - 2 :] + jnp.concatenate(own[2:])]
    )


def water(plan_ref, rows):
    parts = plan_ref.shape[2] // 128
    return jnp.concatenate([plan_ref[PLAN_EDGE, i * rows : (i + 1) * rows, 128:] for i in range(parts)], axis=1).astype(F32)


def grouped_edges(correction, plan_ref):
    short = 128 - correction.shape[0]
    if short:
        correction = jnp.concatenate([correction, jnp.zeros((short, correction.shape[1]), F32)])
    return select_rows(plan_ref[PLAN_EDGE, :, :128], correction, 2)


def flux_of(slots, edges, plan_ref, n_tables, rows):
    grouped = select_rows(plan_ref[PLAN_COLLECT], slots, 2) + edges
    flux = jnp.zeros((rows, slots.shape[1]), F32)
    for k in range(n_tables):
        at = PLAN_WAYS + 2 * k
        flux += product(grouped[k * rows : (k + 1) * rows], plan_ref[at], plan_ref[at + 1])
    return flux


def lines_of(ref, first, count):
    return [ref[:, first + i, :] for i in range(count)]


def flux_kernel(cap, n_tables, got_ref, plan_ref, keep_ref, *refs):
    part_ref = refs[-1]
    _, _, atmos = place()
    n_tile, _, width = got_ref.shape
    rows = part_ref.shape[0]
    stepped = keep_ref[keep_ref.shape[0] - rows :]
    correction = corrections(lines_of(got_ref, cap, N_COEF), lines_of(got_ref, cap + N_COEF, 4))
    whole = whole_level(stepped, correction)
    slots = got_ref[:, :cap, :].reshape(n_tile * cap, width)
    flux = flux_of(slots, grouped_edges(jnp.concatenate(correction), plan_ref), plan_ref, n_tables, rows)
    part_ref[...] = jnp.where(atmos, FORCING * water(plan_ref, rows) * flux, whole)


def levels_kernel(cap, got_ref, fields_ref, coef_ref, top_ref, level_ref):
    _, _, atmos = place()
    kappa, speed = coef_ref[0, 0], coef_ref[0, 1]
    levels, rows, width = fields_ref.shape[1:]
    n_tile = got_ref.shape[0]
    stepped = substep(substep(fields_ref[0], kappa, speed), kappa, speed)
    coef = lines_of(got_ref, cap, N_COEF)
    first, second = [corrections(coef, lines_of(got_ref, cap + N_COEF + 4 * l, 4)) for l in range(2)]
    level_ref[:rows] = jnp.where(atmos, whole_level(stepped[0], first), top_ref[...])
    level_ref[rows : 2 * rows] = whole_level(stepped[1], second)
    level_ref[2 * rows : levels * rows] = stepped[2:].reshape((levels - 2) * rows, width)
    at = levels * rows + 4 * n_tile
    level_ref[levels * rows : at] = jnp.concatenate([x - y for x, y in zip(first, second)])
    level_ref[at:] = padded(
        sum([[u[:1], u[:1], u[rows - 1 :], u[rows - 1 :]] for u in [fields_ref[0, l] for l in range(2, levels)]], []),
        level_ref.shape[0] - at,
        width,
    )


def second_kernel(cap, n_tables, levels, sources, plan_ref, level_ref, *refs):
    swapped, (part_ref, came_ref) = refs[:-2], refs[-2:]
    _, tile, atmos = place()
    n_tile, _, width = came_ref.shape
    rows = part_ref.shape[0]
    edges = level_ref[levels * rows : levels * rows + 4 * n_tile]
    for m, (i, j) in enumerate(sources):
        came_ref[n_tile - 1 - (tile ^ m)] = swapped[i][j * cap : (j + 1) * cap]
    flux = flux_of(came_ref[...].reshape(n_tile * cap, width), grouped_edges(edges, plan_ref), plan_ref, n_tables, rows)
    part_ref[...] = jnp.where(atmos, FORCING * water(plan_ref, rows) * flux, 0.0)


def finish_kernel(cap, got_ref, level_ref, *refs):
    swapped, whole_ref = refs[:-1], refs[-1]
    _, tile, _ = place()
    levels, rows, width = whole_ref.shape
    n_tile = got_ref.shape[0]
    whole_ref[...] = level_ref[: levels * rows].reshape(levels, rows, width)
    count = 4 * (levels - 2)
    held = n_tile // 2 * cap
    prev = jnp.zeros((count, width), F32)
    after = prev
    for i, ref in enumerate(swapped):
        other = tile ^ (2 ** (i + 1) - 1)
        came = ref[held : held + count]
        prev = jnp.where(other == tile - 1, came, prev)
        after = jnp.where(other == tile + 1, came, after)
    at = n_tile - 1 - tile
    own = got_ref[at, cap : cap + 8]
    a0, aa, k0, b1, bb, k1 = [own[i : i + 1] for i in range(N_COEF)]
    b_prev = jnp.where(tile > 0, got_ref[jnp.minimum(at + 1, n_tile - 1), cap : cap + 8][3:4], 0.0)
    a_next = jnp.where(tile < n_tile - 1, got_ref[jnp.maximum(at - 1, 0), cap : cap + 8][0:1], 0.0)
    for l in range(2, levels):
        u0, _, u1, _ = [level_ref[levels * rows + 4 * n_tile + 4 * (l - 2) + i : levels * rows + 4 * n_tile + 4 * (l - 2) + i + 1] for i in range(4)]
        u_prev, q_prev = [prev[4 * (l - 2) + i : 4 * (l - 2) + i + 1] for i in (2, 3)]
        u_next, q_next = [after[4 * (l - 2) + i : 4 * (l - 2) + i + 1] for i in (0, 1)]
        whole_ref[l, :2] += jnp.concatenate([sideways(a0 * u_prev, k0) + a0 * (q_prev + b_prev * u0), aa * u_prev])
        whole_ref[l, rows - 2 :] += jnp.concatenate([bb * u_next, sideways(b1 * u_next, k1) + b1 * (q_next + a_next * u1)])


def sea_kernel(n_tables, plan_ref, *refs):
    parts, (top_ref, back_ref) = refs[:-2], refs[-2:]
    top = sum(part[...] for part in parts)
    top_ref[...] = top
    sea = water(plan_ref, top.shape[0]) * top
    back_ref[...] = select_rows(plan_ref[PLAN_ARRIVE], jnp.concatenate([sea] * n_tables), 2)


def end_kernel(
    n_tables, came_ref, plan_ref, whole_ref, total_ref, last_ref, fields_hbm, surface_hbm, forced_ref, surface_ref, sems
):
    _, _, atmos = place()
    levels, rows, width = whole_ref.shape
    forced_ref[...] = jnp.where(atmos, whole_ref[1], whole_ref[1] + total_ref[...] + last_ref[...])
    copies = [
        pltpu.make_async_copy(whole_ref.at[pl.ds(2, levels - 2)], fields_hbm.at[0, pl.ds(2, levels - 2)], sems.at[0]),
        pltpu.make_async_copy(whole_ref.at[0], fields_hbm.at[0, 0], sems.at[1]),
        pltpu.make_async_copy(forced_ref, fields_hbm.at[0, 1], sems.at[2]),
        pltpu.make_async_copy(surface_ref, surface_hbm.at[0], sems.at[3]),
    ]
    for copy in copies[:3]:
        copy.start()
    picked = select_rows(plan_ref[PLAN_BACK], came_ref[...], 2)
    seen = jnp.zeros((rows, width), F32)
    for k in range(n_tables):
        at = PLAN_WAYS + 2 * k
        seen += product(picked[k * rows : (k + 1) * rows], plan_ref[at], plan_ref[at + 1], mm_t)
    surface_ref[...] = jnp.where(atmos, seen, water(plan_ref, rows) * whole_ref[0])
    copies[3].start()
    for copy in copies:
        copy.wait()


def call(kernel, n_in, outs, flops=0, scratch=(), space=pltpu.VMEM, out_space=pltpu.VMEM, vmem=12):
    shapes = [jax.ShapeDtypeStruct(s, d) for s, d in outs]
    return pl.pallas_call(
        kernel,
        out_shape=shapes,
        in_specs=[pl.BlockSpec(memory_space=space)] * n_in,
        out_specs=[pl.BlockSpec(memory_space=out_space)] * len(shapes),
        scratch_shapes=scratch,
        compiler_params=pltpu.CompilerParams(vmem_limit_bytes=vmem * 1024 * 1024),
        cost_estimate=pl.CostEstimate(flops=flops, bytes_accessed=1 << 10, transcendentals=0),
    )


def swap_stage(bit, cap, arrays, chunks, after=None):
    n_tile = lax.axis_size("tile")
    going = [m for m in range(n_tile) if m & bit]
    if after is not None:
        arrays, after = lax.optimization_barrier((arrays, after))
    if bit == 1:
        give = arrays.pop()
    else:
        picks = [chunks[m] for m in going]
        used = sorted({i for i, _ in picks})
        picks = [(used.index(i), j) for i, j in picks]
        taken = [arrays[i] for i in used]
        if used[-1] != len(arrays) - 1:
            taken.append(arrays[-1])
        kernel = functools.partial(stack_kernel, picks, cap)
        (give,) = call(kernel, len(taken), [(arrays[-1].shape, F32)])(*taken)
    came = lax.ppermute(give, "tile", [(t, t ^ bit) for t in range(n_tile)])
    chunks = chunks | {m: (len(arrays), i) for i, m in enumerate(going)}
    return arrays + [came], chunks, after


def local(fields, coefficients, owner_tile, dest_block, table_index, tables, land_mask):
    n_sec, n_tile = lax.axis_size("sec"), lax.axis_size("tile")
    levels, rows, width = fields.shape[1:]
    fan = owner_tile.shape[1]
    n_tables = tables.shape[0]
    cap = 2 * fan * rows // n_tile
    slots, lines = n_tile * cap, n_tables * rows
    up8 = lambda n: -(-n // 8) * 8
    chunk, side = up8(cap + N_COEF + 8), up8(4 * (levels - 2))
    owner, dest, table = owner_tile.T, dest_block.T, table_index.T
    turned = [list(range(n_tile - 1, -1, -1))]
    exchange = lambda x, axis: lax.all_to_all(x, axis, split_axis=0, concat_axis=0, axis_index_groups=turned, tiled=True)
    plane = ((rows, width), F32)

    (send,) = call(
        functools.partial(send_kernel, cap),
        3,
        [((n_tile, chunk, width), F32)],
        scratch=[
            pltpu.VMEM((2, rows, width), F32),
            pltpu.VMEM((2, rows, width), F32),
            pltpu.VMEM(owner.shape, I32),
            pltpu.SemaphoreType.DMA((3,)),
        ],
        space=pltpu.HBM,
        vmem=60,
    )(fields, coefficients, owner)
    got = exchange(send, "tile")
    half = n_tile // 2 * cap
    keep, give = call(
        functools.partial(swap_kernel, cap),
        3,
        [((half + rows, width), F32), ((half + side, width), F32)],
        scratch=[pltpu.VMEM((n_tile, cap, width), F32)],
    )(fields, coefficients, owner)
    arrays, chunks, _ = swap_stage(1, cap, [keep, give], {m: (0, m // 2) for m in range(0, n_tile, 2)})
    (plan,) = call(
        functools.partial(index_kernel, cap, rows),
        5,
        [((PLAN_WAYS + 2 * n_tables, lines, width), BF16)],
        scratch=[pltpu.VMEM((slots, lines), F32)],
    )(owner, dest, table, tables, land_mask)
    arrays, chunks, plan = swap_stage(2, cap, arrays, chunks, plan)
    (part,) = call(functools.partial(flux_kernel, cap, n_tables), 1 + len(arrays), [plane])(got, plan, *arrays[:-1])
    others = [lax.ppermute(part, "sec", [(s, s ^ other) for s in range(n_sec)]) for other in range(n_sec - 1, 0, -1)]
    bit = 4
    while bit < n_tile:
        arrays, chunks, part = swap_stage(bit, cap, arrays, chunks, part)
        bit *= 2
    sources = [chunks[m] for m in range(n_tile)]
    top, back = call(functools.partial(sea_kernel, n_tables), 1 + n_sec, [plane, ((slots, width), F32)])(plan, part, *others)
    got, back = lax.optimization_barrier((got, back))
    (level,) = call(
        functools.partial(levels_kernel, cap), 4, [((levels * rows + 4 * n_tile + side, width), F32)], flops=1 << 32
    )(got, fields, coefficients, top)
    came = exchange(back.reshape(n_tile, cap, width), "tile").reshape(slots, width)
    (total,) = call(
        functools.partial(second_kernel, cap, n_tables, levels, sources),
        2 + len(arrays),
        [plane],
        scratch=[pltpu.VMEM((n_tile, cap, width), F32)],
        flops=1 << 34,
    )(plan, level, *arrays)
    came_total = 0.0
    bit = 1
    while bit < n_sec:
        pairs = [(s, s | bit) for s in range(n_sec) if (s & (2 * bit - 1)) == bit - 1]
        total = total + came_total
        came_total = lax.ppermute(total, "sec", pairs)
        bit *= 2
    (whole,) = call(
        functools.partial(finish_kernel, cap), 1 + len(arrays), [((levels, rows, width), F32)], flops=1 << 28
    )(got, level, *arrays[1:])
    return call(
        functools.partial(end_kernel, n_tables),
        5,
        [(fields.shape, F32), ((1, rows, width), F32)],
        scratch=[pltpu.VMEM((rows, width), F32)] * 2 + [pltpu.SemaphoreType.DMA((4,))],
        out_space=pltpu.HBM,
    )(came, plan, whole, total, came_total)


def solution(mesh):
    placed = (P("sec", None, "tile", None), P("sec", None, "tile", None), P(), P(), P(), P(), P("tile", None))
    return jax.shard_map(
        local,
        mesh=mesh,
        in_specs=placed,
        out_specs=(P("sec", None, "tile", None), P("sec", "tile", None)),
        check_vma=False,
    )
```

```python
import functools

import jax
import jax.numpy as jnp
from jax import lax
from jax.experimental import pallas as pl
from jax.experimental.pallas import tpu as pltpu
from jax.sharding import PartitionSpec as P

FORCING = 0.5
F32, BF16, I32 = jnp.float32, jnp.bfloat16, jnp.int32
N_COEF = 6
PLAN_COLLECT, PLAN_ARRIVE, PLAN_EDGE, PLAN_BACK, PLAN_WAYS = 0, 1, 2, 3, 4


def iota(shape, axis):
    return lax.broadcasted_iota(I32, shape, axis)


def roll(x, shift, axis):
    return pltpu.roll(x, shift % x.shape[axis], axis)


def split(x, parts):
    out = []
    for _ in range(parts):
        out.append(x.astype(BF16))
        x = x - out[-1].astype(F32)
    return out


def mm(a, b):
    return lax.dot_general(a, b, (((1,), (0,)), ((), ())), preferred_element_type=F32)


def mm_t(a, b):
    return lax.dot_general(a, b, (((1,), (1,)), ((), ())), preferred_element_type=F32)


def select_rows(hot, x, parts):
    return sum(mm(hot, p) for p in split(x, parts))


def product(a, b1, b2, dot=mm):
    a1, a2 = split(a, 2)
    rows = a.shape[0]
    both = dot(jnp.concatenate([a1, a2]), b1)
    return both[:rows] + both[rows:] + dot(a1, b2)


def sideways(x, kappa):
    return x + kappa * (roll(x, 1, x.ndim - 1) + roll(x, -1, x.ndim - 1) - 4.0 * x)


def substep(u, kappa, speed):
    rows = u.shape[1]
    row = iota(u.shape, 1)
    upper = jnp.where(row == 0, 0.0, roll(u, 1, 1))
    lower = jnp.where(row == rows - 1, 0.0, roll(u, -1, 1))
    laplace = upper + lower + roll(u, 1, 2) + roll(u, -1, 2) - 4.0 * u
    return u + kappa * laplace - 0.5 * speed * (lower - upper)


def place():
    sec, tile = lax.axis_index("sec"), lax.axis_index("tile")
    return sec, tile, sec < lax.axis_size("sec") - 1


def own_slots(owner_ref, rows, cap):
    sec, tile, atmos = place()
    n_sec, n_tile = lax.axis_size("sec"), lax.axis_size("tile")
    block = (jnp.minimum(sec, n_sec - 2) * n_tile + tile) * rows
    first = pl.multiple_of(block // 128 * 128, 128)
    half = block - first
    shape = (n_tile * cap, 128)
    lane = iota((1, 128), 1)
    inside = (lane >= half) & (lane < half + rows) & atmos
    owner = jnp.where(inside, owner_ref[:, pl.ds(first, 128)], -1)
    slot = iota(shape, 0)
    hot = [(owner[r : r + 1] == slot // cap).astype(F32) for r in range(owner.shape[0])]
    both = sum(hot)
    before = (iota((128, 128), 0) < iota((128, 128), 1)).astype(BF16)
    rank = mm(both.astype(BF16), before)
    placed = rank == (slot % cap).astype(F32)
    return first, [jnp.where(placed, h, 0.0) for h in hot]


def edge_rows(u, kappa, a, b):
    top, bot = slice(0, 1), slice(u.shape[0] - 1, u.shape[0])
    q_top = sideways(u[top], kappa[top]) + b[top] * u[1:2]
    q_bot = sideways(u[bot], kappa[bot]) + a[bot] * u[-2:-1]
    return [u[top], q_top, u[bot], q_bot]


def padded(lines, count, width):
    if count > len(lines):
        lines = lines + [jnp.zeros((count - len(lines), width), F32)]
    return jnp.concatenate(lines)


def placed_rows(placed, payload):
    return select_rows(sum(placed).astype(BF16), jnp.concatenate([payload] * (128 // payload.shape[0])), 2)


def send_kernel(cap, fields_hbm, coef_hbm, owner_hbm, send_hbm, fields_ref, coef_ref, owner_ref, slots_ref, edge_ref, sems):
    pairs = ((owner_hbm, owner_ref), (coef_hbm.at[0], coef_ref), (fields_hbm.at[0, pl.ds(0, 2)], fields_ref))
    copies = [pltpu.make_async_copy(src, dst, sems.at[i]) for i, (src, dst) in enumerate(pairs)]
    for copy in copies:
        copy.start()
    copies[0].wait()
    _, rows, width = fields_ref.shape
    _, placed = own_slots(owner_ref, rows, cap)
    copies[1].wait()
    copies[2].wait()
    u = fields_ref[...]
    kappa, speed = coef_ref[0], coef_ref[1]
    a = kappa + 0.5 * speed
    b = kappa - 0.5 * speed
    bot = slice(rows - 1, rows)
    extra = [a[0:1], a[0:1] * a[1:2], kappa[0:1], b[bot], b[bot] * b[rows - 2 : rows - 1], kappa[bot]]
    extra += edge_rows(u[0], kappa, a, b) + edge_rows(u[1], kappa, a, b)
    n_tile, side = slots_ref.shape[0], edge_ref.shape[0]
    edge_ref[...] = padded(extra, side, width)
    going = [pltpu.make_async_copy(edge_ref, send_hbm.at[t, pl.ds(cap, side)], sems.at[3 + t]) for t in range(n_tile)]
    going.append(pltpu.make_async_copy(slots_ref, send_hbm.at[:, pl.ds(0, cap)], sems.at[3 + n_tile]))
    for copy in going[:-1]:
        copy.start()
    stepped = substep(substep(u[:1], kappa, speed), kappa, speed)[0]
    slots_ref[...] = placed_rows(placed, stepped).reshape(slots_ref.shape)
    going[-1].start()
    for copy in going:
        copy.wait()


def swap_kernel(cap, fields_ref, coef_ref, owner_ref, keep_ref, give_ref, slots_ref):
    _, tile, _ = place()
    levels, rows, width = fields_ref.shape[1:]
    _, placed = own_slots(owner_ref, rows, cap)
    kappa, speed = coef_ref[0, 0], coef_ref[0, 1]
    stepped = substep(substep(fields_ref[0, :2], kappa, speed), kappa, speed)
    count = slots_ref.shape[0]
    slots_ref[...] = placed_rows(placed, stepped[0] - stepped[1]).reshape(count, cap, width)
    for m in range(count):
        ref = (keep_ref, give_ref)[m % 2]
        ref[m // 2 * cap : (m // 2 + 1) * cap] = slots_ref[tile ^ m]
    a = kappa + 0.5 * speed
    b = kappa - 0.5 * speed
    extra = sum([edge_rows(fields_ref[0, l], kappa, a, b) for l in range(2, levels)], [])
    held = count // 2 * cap
    give_ref[held:] = padded(extra, give_ref.shape[0] - held, width)
    keep_ref[held:] = stepped[0]


def stack_kernel(picks, cap, *refs):
    out_ref = refs[-1]
    for to, (i, j) in enumerate(picks):
        out_ref[to * cap : (to + 1) * cap] = refs[i][j * cap : (j + 1) * cap]
    held = len(picks) * cap
    out_ref[held:] = refs[-2][held:]


def index_kernel(
    cap, rows, owner_ref, dest_ref, table_ref, tables_ref, mask_ref, plan_ref, arrive_sum
):
    n_tables = tables_ref.shape[0]
    for k in range(n_tables):
        at = PLAN_WAYS + 2 * k
        plan_ref[at], plan_ref[at + 1] = split(tables_ref[k], 2)
    sec, tile, atmos = place()
    n_sec, n_tile = lax.axis_size("sec"), lax.axis_size("tile")
    span = n_tile * rows
    start = jnp.minimum(sec, n_sec - 2) * span
    fan = owner_ref.shape[0]
    lines = n_tables * rows
    per = 128 // rows
    g, h = iota((128, 128), 0), iota((128, 128), 1)
    before = ((g < h) & (g // rows == h // rows)).astype(BF16)
    line = iota((lines, 128), 0)
    seat = iota((per * cap, 128), 0)
    lane = iota((per * cap, 128), 1)
    edges = jnp.zeros((lines, 128), F32)
    for group in range(span // 128):
        at = pl.ds(pl.multiple_of(start + group * 128, 128), 128)
        mine = [(owner_ref[r : r + 1, at] == tile) & atmos for r in range(fan)]
        key = jnp.full((1, 128), -1, I32)
        for r in range(fan):
            key = jnp.where(mine[r], table_ref[r : r + 1, at] * rows + dest_ref[r : r + 1, at], key)
        held = (key >= 0).astype(F32)
        rank = mm(jnp.broadcast_to(held, (16, 128)).astype(BF16), before)[:1]
        sits = (rank == (seat % cap).astype(F32)) & (lane // rows == seat // cap) & (held > 0)
        hit = (line == key).astype(BF16)
        arrive = mm_t(sits.astype(BF16), hit)
        arrive_sum[group * per * cap : (group + 1) * per * cap] = arrive
        block, within = group * per + g // rows, g % rows
        column = sum(jnp.where(within == w, i, 0) for i, w in enumerate((0, 1, rows - 2, rows - 1)))
        is_edge = (within < 2) | (within >= rows - 2)
        edges += mm(hit, (is_edge & (h == column * n_tile + block)).astype(BF16))
    arrive = arrive_sum[...]
    plan_ref[PLAN_ARRIVE] = arrive.astype(BF16)
    plan_ref[PLAN_COLLECT] = arrive.T.astype(BF16)
    plan_ref[PLAN_EDGE, :, :128] = edges.astype(BF16)
    for i in range(mask_ref.shape[1] // 128):
        plan_ref[PLAN_EDGE, i * rows : (i + 1) * rows, 128:] = mask_ref[:, i * 128 : (i + 1) * 128].astype(F32).astype(BF16)
    first, placed = own_slots(owner_ref, rows, cap)
    table = table_ref[:, pl.ds(first, 128)]
    for k in range(n_tables):
        here = sum(jnp.where(table[r : r + 1] == k, placed[r], 0.0) for r in range(fan))
        here = here.T
        plan_ref[PLAN_BACK, k * rows : (k + 1) * rows] = sum(here[i : i + rows] for i in range(0, 128, rows)).astype(BF16)


def shifted(x, by):
    row = iota(x.shape, 0)
    return jnp.where(row == (0 if by > 0 else x.shape[0] - 1), 0.0, roll(x, by, 0))


def corrections(coef, edges):
    a0, aa, k0, b1, bb, k1 = coef
    u0, q0, u1, q1 = edges
    b_prev, a_next = shifted(b1, 1), shifted(a0, -1)
    u_prev, q_prev, u_next, q_next = shifted(u1, 1), shifted(q1, 1), shifted(u0, -1), shifted(q0, -1)
    return [
        sideways(a0 * u_prev, k0) + a0 * (q_prev + b_prev * u0),
        aa * u_prev,
        bb * u_next,
        sideways(b1 * u_next, k1) + b1 * (q_next + a_next * u1),
    ]


def whole_level(plane, correction):
    _, tile, _ = place()
    rows = plane.shape[0]
    here = iota(correction[0].shape, 0) == tile
    own = [jnp.sum(jnp.where(here, c, 0.0), axis=0, keepdims=True) for c in correction]
    return jnp.concatenate(
        [plane[:2] + jnp.concatenate(own[:2]), plane[2 : rows - 2], plane[rows - 2 :] + jnp.concatenate(own[2:])]
    )


def water(plan_ref, rows):
    parts = plan_ref.shape[2] // 128
    return jnp.concatenate([plan_ref[PLAN_EDGE, i * rows : (i + 1) * rows, 128:] for i in range(parts)], axis=1).astype(F32)


def grouped_edges(correction, plan_ref):
    short = 128 - correction.shape[0]
    if short:
        correction = jnp.concatenate([correction, jnp.zeros((short, correction.shape[1]), F32)])
    return select_rows(plan_ref[PLAN_EDGE, :, :128], correction, 2)


def flux_of(slots, edges, plan_ref, n_tables, rows):
    grouped = select_rows(plan_ref[PLAN_COLLECT], slots, 2) + edges
    flux = jnp.zeros((rows, slots.shape[1]), F32)
    for k in range(n_tables):
        at = PLAN_WAYS + 2 * k
        flux += product(grouped[k * rows : (k + 1) * rows], plan_ref[at], plan_ref[at + 1])
    return flux


def lines_of(ref, first, count):
    return [ref[:, first + i, :] for i in range(count)]


def flux_kernel(cap, n_tables, got_ref, plan_ref, keep_ref, *refs):
    part_ref = refs[-1]
    _, _, atmos = place()
    n_tile, _, width = got_ref.shape
    rows = part_ref.shape[0]
    stepped = keep_ref[keep_ref.shape[0] - rows :]
    correction = corrections(lines_of(got_ref, cap, N_COEF), lines_of(got_ref, cap + N_COEF, 4))
    whole = whole_level(stepped, correction)
    slots = got_ref[:, :cap, :].reshape(n_tile * cap, width)
    flux = flux_of(slots, grouped_edges(jnp.concatenate(correction), plan_ref), plan_ref, n_tables, rows)
    part_ref[...] = jnp.where(atmos, FORCING * water(plan_ref, rows) * flux, whole)


def levels_kernel(cap, got_ref, fields_ref, coef_ref, top_ref, level_ref):
    _, _, atmos = place()
    kappa, speed = coef_ref[0, 0], coef_ref[0, 1]
    levels, rows, width = fields_ref.shape[1:]
    n_tile = got_ref.shape[0]
    stepped = substep(substep(fields_ref[0], kappa, speed), kappa, speed)
    coef = lines_of(got_ref, cap, N_COEF)
    first, second = [corrections(coef, lines_of(got_ref, cap + N_COEF + 4 * l, 4)) for l in range(2)]
    level_ref[:rows] = jnp.where(atmos, whole_level(stepped[0], first), top_ref[...])
    level_ref[rows : 2 * rows] = whole_level(stepped[1], second)
    level_ref[2 * rows : levels * rows] = stepped[2:].reshape((levels - 2) * rows, width)
    at = levels * rows + 4 * n_tile
    level_ref[levels * rows : at] = jnp.concatenate([x - y for x, y in zip(first, second)])
    level_ref[at:] = padded(
        sum([[u[:1], u[:1], u[rows - 1 :], u[rows - 1 :]] for u in [fields_ref[0, l] for l in range(2, levels)]], []),
        level_ref.shape[0] - at,
        width,
    )


def second_kernel(cap, n_tables, levels, sources, plan_ref, level_ref, *refs):
    swapped, (part_ref, came_ref) = refs[:-2], refs[-2:]
    _, tile, atmos = place()
    n_tile, _, width = came_ref.shape
    rows = part_ref.shape[0]
    edges = level_ref[levels * rows : levels * rows + 4 * n_tile]
    for m, (i, j) in enumerate(sources):
        came_ref[tile ^ m] = swapped[i][j * cap : (j + 1) * cap]
    flux = flux_of(came_ref[...].reshape(n_tile * cap, width), grouped_edges(edges, plan_ref), plan_ref, n_tables, rows)
    part_ref[...] = jnp.where(atmos, FORCING * water(plan_ref, rows) * flux, 0.0)


def finish_kernel(cap, got_ref, level_ref, *refs):
    swapped, whole_ref = refs[:-1], refs[-1]
    _, tile, _ = place()
    levels, rows, width = whole_ref.shape
    n_tile = got_ref.shape[0]
    whole_ref[...] = level_ref[: levels * rows].reshape(levels, rows, width)
    count = 4 * (levels - 2)
    held = n_tile // 2 * cap
    prev = jnp.zeros((count, width), F32)
    after = prev
    for i, ref in enumerate(swapped):
        other = tile ^ (2 ** (i + 1) - 1)
        came = ref[held : held + count]
        prev = jnp.where(other == tile - 1, came, prev)
        after = jnp.where(other == tile + 1, came, after)
    own = got_ref[tile, cap : cap + 8]
    a0, aa, k0, b1, bb, k1 = [own[i : i + 1] for i in range(N_COEF)]
    b_prev = jnp.where(tile > 0, got_ref[jnp.maximum(tile - 1, 0), cap : cap + 8][3:4], 0.0)
    a_next = jnp.where(tile < n_tile - 1, got_ref[jnp.minimum(tile + 1, n_tile - 1), cap : cap + 8][0:1], 0.0)
    for l in range(2, levels):
        u0, _, u1, _ = [level_ref[levels * rows + 4 * n_tile + 4 * (l - 2) + i : levels * rows + 4 * n_tile + 4 * (l - 2) + i + 1] for i in range(4)]
        u_prev, q_prev = [prev[4 * (l - 2) + i : 4 * (l - 2) + i + 1] for i in (2, 3)]
        u_next, q_next = [after[4 * (l - 2) + i : 4 * (l - 2) + i + 1] for i in (0, 1)]
        whole_ref[l, :2] += jnp.concatenate([sideways(a0 * u_prev, k0) + a0 * (q_prev + b_prev * u0), aa * u_prev])
        whole_ref[l, rows - 2 :] += jnp.concatenate([bb * u_next, sideways(b1 * u_next, k1) + b1 * (q_next + a_next * u1)])


def sea_kernel(n_tables, plan_ref, *refs):
    parts, (top_ref, back_ref) = refs[:-2], refs[-2:]
    top = sum(part[...] for part in parts)
    top_ref[...] = top
    sea = water(plan_ref, top.shape[0]) * top
    back_ref[...] = select_rows(plan_ref[PLAN_ARRIVE], jnp.concatenate([sea] * n_tables), 2)


def end_kernel(
    n_tables, came_ref, plan_ref, whole_ref, total_ref, last_ref, fields_hbm, surface_hbm, forced_ref, surface_ref, sems
):
    _, _, atmos = place()
    levels, rows, width = whole_ref.shape
    forced_ref[...] = jnp.where(atmos, whole_ref[1], whole_ref[1] + total_ref[...] + last_ref[...])
    copies = [
        pltpu.make_async_copy(whole_ref.at[pl.ds(2, levels - 2)], fields_hbm.at[0, pl.ds(2, levels - 2)], sems.at[0]),
        pltpu.make_async_copy(whole_ref.at[0], fields_hbm.at[0, 0], sems.at[1]),
        pltpu.make_async_copy(forced_ref, fields_hbm.at[0, 1], sems.at[2]),
        pltpu.make_async_copy(surface_ref, surface_hbm.at[0], sems.at[3]),
    ]
    for copy in copies[:3]:
        copy.start()
    picked = select_rows(plan_ref[PLAN_BACK], came_ref[...], 2)
    seen = jnp.zeros((rows, width), F32)
    for k in range(n_tables):
        at = PLAN_WAYS + 2 * k
        seen += product(picked[k * rows : (k + 1) * rows], plan_ref[at], plan_ref[at + 1], mm_t)
    surface_ref[...] = jnp.where(atmos, seen, water(plan_ref, rows) * whole_ref[0])
    copies[3].start()
    for copy in copies:
        copy.wait()


def call(kernel, n_in, outs, flops=0, scratch=(), space=pltpu.VMEM, out_space=pltpu.VMEM, vmem=12):
    shapes = [jax.ShapeDtypeStruct(s, d) for s, d in outs]
    return pl.pallas_call(
        kernel,
        out_shape=shapes,
        in_specs=[pl.BlockSpec(memory_space=space)] * n_in,
        out_specs=[pl.BlockSpec(memory_space=out_space)] * len(shapes),
        scratch_shapes=scratch,
        compiler_params=pltpu.CompilerParams(vmem_limit_bytes=vmem * 1024 * 1024),
        cost_estimate=pl.CostEstimate(flops=flops, bytes_accessed=1 << 10, transcendentals=0),
    )


def swap_stage(bit, cap, arrays, chunks, after=None):
    n_tile = lax.axis_size("tile")
    going = [m for m in range(n_tile) if m & bit]
    if after is not None:
        arrays, after = lax.optimization_barrier((arrays, after))
    if bit == 1:
        give = arrays.pop()
    else:
        picks = [chunks[m] for m in going]
        used = sorted({i for i, _ in picks})
        picks = [(used.index(i), j) for i, j in picks]
        taken = [arrays[i] for i in used]
        if used[-1] != len(arrays) - 1:
            taken.append(arrays[-1])
        kernel = functools.partial(stack_kernel, picks, cap)
        (give,) = call(kernel, len(taken), [(arrays[-1].shape, F32)])(*taken)
    came = lax.ppermute(give, "tile", [(t, t ^ bit) for t in range(n_tile)])
    chunks = chunks | {m: (len(arrays), i) for i, m in enumerate(going)}
    return arrays + [came], chunks, after


def local(fields, coefficients, owner_tile, dest_block, table_index, tables, land_mask):
    n_sec, n_tile = lax.axis_size("sec"), lax.axis_size("tile")
    levels, rows, width = fields.shape[1:]
    fan = owner_tile.shape[1]
    n_tables = tables.shape[0]
    cap = 2 * fan * rows // n_tile
    slots, lines = n_tile * cap, n_tables * rows
    up8 = lambda n: -(-n // 8) * 8
    chunk, side = up8(cap + N_COEF + 8), up8(4 * (levels - 2))
    owner, dest, table = owner_tile.T, dest_block.T, table_index.T
    exchange = lambda x, axis: lax.all_to_all(x, axis, split_axis=0, concat_axis=0, tiled=True)
    plane = ((rows, width), F32)

    (send,) = call(
        functools.partial(send_kernel, cap),
        3,
        [((n_tile, chunk, width), F32)],
        scratch=[
            pltpu.VMEM((2, rows, width), F32),
            pltpu.VMEM((2, rows, width), F32),
            pltpu.VMEM(owner.shape, I32),
            pltpu.VMEM((n_tile, cap, width), F32),
            pltpu.VMEM((chunk - cap, width), F32),
            pltpu.SemaphoreType.DMA((4 + n_tile,)),
        ],
        space=pltpu.HBM,
        out_space=pltpu.HBM,
        vmem=60,
    )(fields, coefficients, owner)
    got = exchange(send, "tile")
    half = n_tile // 2 * cap
    keep, give = call(
        functools.partial(swap_kernel, cap),
        3,
        [((half + rows, width), F32), ((half + side, width), F32)],
        scratch=[pltpu.VMEM((n_tile, cap, width), F32)],
    )(fields, coefficients, owner)
    arrays, chunks, _ = swap_stage(1, cap, [keep, give], {m: (0, m // 2) for m in range(0, n_tile, 2)})
    (plan,) = call(
        functools.partial(index_kernel, cap, rows),
        5,
        [((PLAN_WAYS + 2 * n_tables, lines, width), BF16)],
        scratch=[pltpu.VMEM((slots, lines), F32)],
    )(owner, dest, table, tables, land_mask)
    arrays, chunks, plan = swap_stage(2, cap, arrays, chunks, plan)
    (part,) = call(functools.partial(flux_kernel, cap, n_tables), 1 + len(arrays), [plane])(got, plan, *arrays[:-1])
    others = [lax.ppermute(part, "sec", [(s, s ^ other) for s in range(n_sec)]) for other in range(n_sec - 1, 0, -1)]
    bit = 4
    while bit < n_tile:
        arrays, chunks, part = swap_stage(bit, cap, arrays, chunks, part)
        bit *= 2
    sources = [chunks[m] for m in range(n_tile)]
    top, back = call(functools.partial(sea_kernel, n_tables), 1 + n_sec, [plane, ((slots, width), F32)])(plan, part, *others)
    got, back = lax.optimization_barrier((got, back))
    (level,) = call(
        functools.partial(levels_kernel, cap), 4, [((levels * rows + 4 * n_tile + side, width), F32)], flops=1 << 32
    )(got, fields, coefficients, top)
    came = exchange(back.reshape(n_tile, cap, width), "tile").reshape(slots, width)
    (total,) = call(
        functools.partial(second_kernel, cap, n_tables, levels, sources),
        2 + len(arrays),
        [plane],
        scratch=[pltpu.VMEM((n_tile, cap, width), F32)],
        flops=1 << 34,
    )(plan, level, *arrays)
    came_total = 0.0
    bit = n_sec // 2
    while bit:
        above = n_sec - 2 * bit
        pairs = [(s, s | bit) for s in range(n_sec) if s & above == above and not s & bit]
        total = total + came_total
        came_total = lax.ppermute(total, "sec", pairs)
        bit //= 2
    (whole,) = call(
        functools.partial(finish_kernel, cap), 1 + len(arrays), [((levels, rows, width), F32)], flops=1 << 28
    )(got, level, *arrays[1:])
    return call(
        functools.partial(end_kernel, n_tables),
        5,
        [(fields.shape, F32), ((1, rows, width), F32)],
        scratch=[pltpu.VMEM((rows, width), F32)] * 2 + [pltpu.SemaphoreType.DMA((4,))],
        out_space=pltpu.HBM,
    )(came, plan, whole, total, came_total)


def solution(mesh):
    placed = (P("sec", None, "tile", None), P("sec", None, "tile", None), P(), P(), P(), P(), P("tile", None))
    return jax.shard_map(
        local,
        mesh=mesh,
        in_specs=placed,
        out_specs=(P("sec", None, "tile", None), P("sec", "tile", None)),
        check_vma=False,
    )
```

```python
import functools

import jax
import jax.numpy as jnp
from jax import lax
from jax.experimental import pallas as pl
from jax.experimental.pallas import tpu as pltpu
from jax.sharding import PartitionSpec as P

FORCING = 0.5
F32, BF16, I32 = jnp.float32, jnp.bfloat16, jnp.int32
N_COEF = 6
PLAN_COLLECT, PLAN_ARRIVE, PLAN_EDGE, PLAN_BACK, PLAN_WAYS = 0, 1, 2, 3, 4


def iota(shape, axis):
    return lax.broadcasted_iota(I32, shape, axis)


def roll(x, shift, axis):
    return pltpu.roll(x, shift % x.shape[axis], axis)


def split(x, parts):
    out = []
    for _ in range(parts):
        out.append(x.astype(BF16))
        x = x - out[-1].astype(F32)
    return out


def mm(a, b):
    return lax.dot_general(a, b, (((1,), (0,)), ((), ())), preferred_element_type=F32)


def mm_t(a, b):
    return lax.dot_general(a, b, (((1,), (1,)), ((), ())), preferred_element_type=F32)


def select_rows(hot, x, parts):
    return sum(mm(hot, p) for p in split(x, parts))


def product(a, b1, b2, dot=mm):
    a1, a2 = split(a, 2)
    rows = a.shape[0]
    both = dot(jnp.concatenate([a1, a2]), b1)
    return both[:rows] + both[rows:] + dot(a1, b2)


def sideways(x, kappa):
    return x + kappa * (roll(x, 1, x.ndim - 1) + roll(x, -1, x.ndim - 1) - 4.0 * x)


def substep(u, kappa, speed):
    rows = u.shape[1]
    row = iota(u.shape, 1)
    upper = jnp.where(row == 0, 0.0, roll(u, 1, 1))
    lower = jnp.where(row == rows - 1, 0.0, roll(u, -1, 1))
    laplace = upper + lower + roll(u, 1, 2) + roll(u, -1, 2) - 4.0 * u
    return u + kappa * laplace - 0.5 * speed * (lower - upper)


def place():
    sec, tile = lax.axis_index("sec"), lax.axis_index("tile")
    return sec, tile, sec < lax.axis_size("sec") - 1


def own_slots(owner_ref, rows, cap):
    sec, tile, atmos = place()
    n_sec, n_tile = lax.axis_size("sec"), lax.axis_size("tile")
    block = (jnp.minimum(sec, n_sec - 2) * n_tile + tile) * rows
    first = pl.multiple_of(block // 128 * 128, 128)
    half = block - first
    shape = (n_tile * cap, 128)
    lane = iota((1, 128), 1)
    inside = (lane >= half) & (lane < half + rows) & atmos
    owner = jnp.where(inside, owner_ref[:, pl.ds(first, 128)], -1)
    slot = iota(shape, 0)
    hot = [(owner[r : r + 1] == slot // cap).astype(F32) for r in range(owner.shape[0])]
    both = sum(hot)
    before = (iota((128, 128), 0) < iota((128, 128), 1)).astype(BF16)
    rank = mm(both.astype(BF16), before)
    placed = rank == (slot % cap).astype(F32)
    return first, [jnp.where(placed, h, 0.0) for h in hot]


def edge_rows(u, kappa, a, b):
    top, bot = slice(0, 1), slice(u.shape[0] - 1, u.shape[0])
    q_top = sideways(u[top], kappa[top]) + b[top] * u[1:2]
    q_bot = sideways(u[bot], kappa[bot]) + a[bot] * u[-2:-1]
    return [u[top], q_top, u[bot], q_bot]


def padded(lines, count, width):
    if count > len(lines):
        lines = lines + [jnp.zeros((count - len(lines), width), F32)]
    return jnp.concatenate(lines)


def placed_rows(placed, payload):
    return select_rows(sum(placed).astype(BF16), jnp.concatenate([payload] * (128 // payload.shape[0])), 2)


def send_kernel(cap, fields_hbm, coef_hbm, owner_hbm, send_hbm, fields_ref, coef_ref, owner_ref, slots_ref, edge_ref, sems):
    pairs = ((owner_hbm, owner_ref), (coef_hbm.at[0], coef_ref), (fields_hbm.at[0, pl.ds(0, 2)], fields_ref))
    copies = [pltpu.make_async_copy(src, dst, sems.at[i]) for i, (src, dst) in enumerate(pairs)]
    for copy in copies:
        copy.start()
    copies[0].wait()
    _, rows, width = fields_ref.shape
    _, placed = own_slots(owner_ref, rows, cap)
    copies[1].wait()
    copies[2].wait()
    u = fields_ref[...]
    kappa, speed = coef_ref[0], coef_ref[1]
    a = kappa + 0.5 * speed
    b = kappa - 0.5 * speed
    bot = slice(rows - 1, rows)
    extra = [a[0:1], a[0:1] * a[1:2], kappa[0:1], b[bot], b[bot] * b[rows - 2 : rows - 1], kappa[bot]]
    extra += edge_rows(u[0], kappa, a, b) + edge_rows(u[1], kappa, a, b)
    n_tile, side = slots_ref.shape[0], edge_ref.shape[0]
    edge_ref[...] = padded(extra, side, width)
    going = [pltpu.make_async_copy(edge_ref, send_hbm.at[t, pl.ds(cap, side)], sems.at[3 + t]) for t in range(n_tile)]
    going.append(pltpu.make_async_copy(slots_ref, send_hbm.at[:, pl.ds(0, cap)], sems.at[3 + n_tile]))
    for copy in going[:-1]:
        copy.start()
    stepped = substep(substep(u[:1], kappa, speed), kappa, speed)[0]
    slots_ref[...] = placed_rows(placed, stepped).reshape(slots_ref.shape)
    going[-1].start()
    for copy in going:
        copy.wait()


def swap_kernel(cap, fields_ref, coef_ref, owner_ref, keep_ref, give_ref, slots_ref):
    _, tile, _ = place()
    levels, rows, width = fields_ref.shape[1:]
    _, placed = own_slots(owner_ref, rows, cap)
    kappa, speed = coef_ref[0, 0], coef_ref[0, 1]
    stepped = substep(substep(fields_ref[0, :2], kappa, speed), kappa, speed)
    count = slots_ref.shape[0]
    slots_ref[...] = placed_rows(placed, stepped[0] - stepped[1]).reshape(count, cap, width)
    for m in range(count):
        ref = (keep_ref, give_ref)[m % 2]
        ref[m // 2 * cap : (m // 2 + 1) * cap] = slots_ref[tile ^ m]
    a = kappa + 0.5 * speed
    b = kappa - 0.5 * speed
    extra = sum([edge_rows(fields_ref[0, l], kappa, a, b) for l in range(2, levels)], [])
    held = count // 2 * cap
    give_ref[held:] = padded(extra, give_ref.shape[0] - held, width)
    keep_ref[held:] = stepped[0]


def stack_kernel(picks, cap, *refs):
    out_ref = refs[-1]
    for to, (i, j) in enumerate(picks):
        out_ref[to * cap : (to + 1) * cap] = refs[i][j * cap : (j + 1) * cap]
    held = len(picks) * cap
    out_ref[held:] = refs[-2][held:]


def index_kernel(
    cap, rows, owner_ref, dest_ref, table_ref, tables_ref, mask_ref, plan_ref, arrive_sum
):
    n_tables = tables_ref.shape[0]
    for k in range(n_tables):
        at = PLAN_WAYS + 2 * k
        plan_ref[at], plan_ref[at + 1] = split(tables_ref[k], 2)
    sec, tile, atmos = place()
    n_sec, n_tile = lax.axis_size("sec"), lax.axis_size("tile")
    span = n_tile * rows
    start = jnp.minimum(sec, n_sec - 2) * span
    fan = owner_ref.shape[0]
    lines = n_tables * rows
    per = 128 // rows
    g, h = iota((128, 128), 0), iota((128, 128), 1)
    before = ((g < h) & (g // rows == h // rows)).astype(BF16)
    line = iota((lines, 128), 0)
    seat = iota((per * cap, 128), 0)
    lane = iota((per * cap, 128), 1)
    edges = jnp.zeros((lines, 128), F32)
    for group in range(span // 128):
        at = pl.ds(pl.multiple_of(start + group * 128, 128), 128)
        mine = [(owner_ref[r : r + 1, at] == tile) & atmos for r in range(fan)]
        key = jnp.full((1, 128), -1, I32)
        for r in range(fan):
            key = jnp.where(mine[r], table_ref[r : r + 1, at] * rows + dest_ref[r : r + 1, at], key)
        held = (key >= 0).astype(F32)
        rank = mm(jnp.broadcast_to(held, (16, 128)).astype(BF16), before)[:1]
        sits = (rank == (seat % cap).astype(F32)) & (lane // rows == seat // cap) & (held > 0)
        hit = (line == key).astype(BF16)
        arrive = mm_t(sits.astype(BF16), hit)
        arrive_sum[group * per * cap : (group + 1) * per * cap] = arrive
        block, within = group * per + g // rows, g % rows
        column = sum(jnp.where(within == w, i, 0) for i, w in enumerate((0, 1, rows - 2, rows - 1)))
        is_edge = (within < 2) | (within >= rows - 2)
        edges += mm(hit, (is_edge & (h == column * n_tile + block)).astype(BF16))
    arrive = arrive_sum[...]
    plan_ref[PLAN_ARRIVE] = arrive.astype(BF16)
    plan_ref[PLAN_COLLECT] = arrive.T.astype(BF16)
    plan_ref[PLAN_EDGE, :, :128] = edges.astype(BF16)
    for i in range(mask_ref.shape[1] // 128):
        plan_ref[PLAN_EDGE, i * rows : (i + 1) * rows, 128:] = mask_ref[:, i * 128 : (i + 1) * 128].astype(F32).astype(BF16)
    first, placed = own_slots(owner_ref, rows, cap)
    table = table_ref[:, pl.ds(first, 128)]
    for k in range(n_tables):
        here = sum(jnp.where(table[r : r + 1] == k, placed[r], 0.0) for r in range(fan))
        here = here.T
        plan_ref[PLAN_BACK, k * rows : (k + 1) * rows] = sum(here[i : i + rows] for i in range(0, 128, rows)).astype(BF16)


def shifted(x, by):
    row = iota(x.shape, 0)
    return jnp.where(row == (0 if by > 0 else x.shape[0] - 1), 0.0, roll(x, by, 0))


def corrections(coef, edges):
    a0, aa, k0, b1, bb, k1 = coef
    u0, q0, u1, q1 = edges
    b_prev, a_next = shifted(b1, 1), shifted(a0, -1)
    u_prev, q_prev, u_next, q_next = shifted(u1, 1), shifted(q1, 1), shifted(u0, -1), shifted(q0, -1)
    return [
        sideways(a0 * u_prev, k0) + a0 * (q_prev + b_prev * u0),
        aa * u_prev,
        bb * u_next,
        sideways(b1 * u_next, k1) + b1 * (q_next + a_next * u1),
    ]


def whole_level(plane, correction):
    _, tile, _ = place()
    rows = plane.shape[0]
    here = iota(correction[0].shape, 0) == tile
    own = [jnp.sum(jnp.where(here, c, 0.0), axis=0, keepdims=True) for c in correction]
    return jnp.concatenate(
        [plane[:2] + jnp.concatenate(own[:2]), plane[2 : rows - 2], plane[rows - 2 :] + jnp.concatenate(own[2:])]
    )


def water(plan_ref, rows):
    parts = plan_ref.shape[2] // 128
    return jnp.concatenate([plan_ref[PLAN_EDGE, i * rows : (i + 1) * rows, 128:] for i in range(parts)], axis=1).astype(F32)


def grouped_edges(correction, plan_ref):
    short = 128 - correction.shape[0]
    if short:
        correction = jnp.concatenate([correction, jnp.zeros((short, correction.shape[1]), F32)])
    return select_rows(plan_ref[PLAN_EDGE, :, :128], correction, 2)


def flux_of(slots, edges, plan_ref, n_tables, rows):
    grouped = select_rows(plan_ref[PLAN_COLLECT], slots, 2) + edges
    flux = jnp.zeros((rows, slots.shape[1]), F32)
    for k in range(n_tables):
        at = PLAN_WAYS + 2 * k
        flux += product(grouped[k * rows : (k + 1) * rows], plan_ref[at], plan_ref[at + 1])
    return flux


def lines_of(ref, first, count):
    return [ref[:, first + i, :] for i in range(count)]


def flux_kernel(cap, n_tables, got_ref, plan_ref, keep_ref, *refs):
    part_ref = refs[-1]
    _, _, atmos = place()
    n_tile, _, width = got_ref.shape
    rows = part_ref.shape[0]
    stepped = keep_ref[keep_ref.shape[0] - rows :]
    correction = corrections(lines_of(got_ref, cap, N_COEF), lines_of(got_ref, cap + N_COEF, 4))
    whole = whole_level(stepped, correction)
    slots = got_ref[:, :cap, :].reshape(n_tile * cap, width)
    flux = flux_of(slots, grouped_edges(jnp.concatenate(correction), plan_ref), plan_ref, n_tables, rows)
    part_ref[...] = jnp.where(atmos, FORCING * water(plan_ref, rows) * flux, whole)


def levels_kernel(cap, got_ref, fields_ref, coef_ref, top_ref, level_ref):
    _, _, atmos = place()
    kappa, speed = coef_ref[0, 0], coef_ref[0, 1]
    levels, rows, width = fields_ref.shape[1:]
    n_tile = got_ref.shape[0]
    stepped = substep(substep(fields_ref[0], kappa, speed), kappa, speed)
    coef = lines_of(got_ref, cap, N_COEF)
    first, second = [corrections(coef, lines_of(got_ref, cap + N_COEF + 4 * l, 4)) for l in range(2)]
    level_ref[:rows] = jnp.where(atmos, whole_level(stepped[0], first), top_ref[...])
    level_ref[rows : 2 * rows] = whole_level(stepped[1], second)
    level_ref[2 * rows : levels * rows] = stepped[2:].reshape((levels - 2) * rows, width)
    at = levels * rows + 4 * n_tile
    level_ref[levels * rows : at] = jnp.concatenate([x - y for x, y in zip(first, second)])
    level_ref[at:] = padded(
        sum([[u[:1], u[:1], u[rows - 1 :], u[rows - 1 :]] for u in [fields_ref[0, l] for l in range(2, levels)]], []),
        level_ref.shape[0] - at,
        width,
    )


def second_kernel(cap, n_tables, levels, sources, plan_ref, level_ref, *refs):
    swapped, (part_ref, came_ref) = refs[:-2], refs[-2:]
    _, tile, atmos = place()
    n_tile, _, width = came_ref.shape
    rows = part_ref.shape[0]
    edges = level_ref[levels * rows : levels * rows + 4 * n_tile]
    for m, (i, j) in enumerate(sources):
        came_ref[tile ^ m] = swapped[i][j * cap : (j + 1) * cap]
    flux = flux_of(came_ref[...].reshape(n_tile * cap, width), grouped_edges(edges, plan_ref), plan_ref, n_tables, rows)
    part_ref[...] = jnp.where(atmos, FORCING * water(plan_ref, rows) * flux, 0.0)


def finish_kernel(cap, got_ref, level_ref, *refs):
    swapped, whole_ref = refs[:-1], refs[-1]
    _, tile, _ = place()
    levels, rows, width = whole_ref.shape
    n_tile = got_ref.shape[0]
    whole_ref[...] = level_ref[: levels * rows].reshape(levels, rows, width)
    count = 4 * (levels - 2)
    held = n_tile // 2 * cap
    prev = jnp.zeros((count, width), F32)
    after = prev
    for i, ref in enumerate(swapped):
        other = tile ^ (2 ** (i + 1) - 1)
        came = ref[held : held + count]
        prev = jnp.where(other == tile - 1, came, prev)
        after = jnp.where(other == tile + 1, came, after)
    own = got_ref[tile, cap : cap + 8]
    a0, aa, k0, b1, bb, k1 = [own[i : i + 1] for i in range(N_COEF)]
    b_prev = jnp.where(tile > 0, got_ref[jnp.maximum(tile - 1, 0), cap : cap + 8][3:4], 0.0)
    a_next = jnp.where(tile < n_tile - 1, got_ref[jnp.minimum(tile + 1, n_tile - 1), cap : cap + 8][0:1], 0.0)
    for l in range(2, levels):
        u0, _, u1, _ = [level_ref[levels * rows + 4 * n_tile + 4 * (l - 2) + i : levels * rows + 4 * n_tile + 4 * (l - 2) + i + 1] for i in range(4)]
        u_prev, q_prev = [prev[4 * (l - 2) + i : 4 * (l - 2) + i + 1] for i in (2, 3)]
        u_next, q_next = [after[4 * (l - 2) + i : 4 * (l - 2) + i + 1] for i in (0, 1)]
        whole_ref[l, :2] += jnp.concatenate([sideways(a0 * u_prev, k0) + a0 * (q_prev + b_prev * u0), aa * u_prev])
        whole_ref[l, rows - 2 :] += jnp.concatenate([bb * u_next, sideways(b1 * u_next, k1) + b1 * (q_next + a_next * u1)])


def sea_kernel(n_tables, plan_ref, *refs):
    parts, (top_ref, back_ref) = refs[:-2], refs[-2:]
    top = sum(part[...] for part in parts)
    top_ref[...] = top
    sea = water(plan_ref, top.shape[0]) * top
    back_ref[...] = select_rows(plan_ref[PLAN_ARRIVE], jnp.concatenate([sea] * n_tables), 2)


def end_kernel(n_tables, came_ref, plan_ref, whole_ref, fields_hbm, surface_hbm, surface_ref, sems):
    _, _, atmos = place()
    _, rows, width = whole_ref.shape
    copies = [
        pltpu.make_async_copy(whole_ref, fields_hbm.at[0], sems.at[0]),
        pltpu.make_async_copy(surface_ref, surface_hbm.at[0], sems.at[1]),
    ]
    copies[0].start()
    picked = select_rows(plan_ref[PLAN_BACK], came_ref[...], 2)
    seen = jnp.zeros((rows, width), F32)
    for k in range(n_tables):
        at = PLAN_WAYS + 2 * k
        seen += product(picked[k * rows : (k + 1) * rows], plan_ref[at], plan_ref[at + 1], mm_t)
    surface_ref[...] = jnp.where(atmos, seen, water(plan_ref, rows) * whole_ref[0])
    copies[1].start()
    for copy in copies:
        copy.wait()


def forced_kernel(_, whole_ref, total_ref, last_ref, fields_hbm, plane_ref, sem):
    _, _, atmos = place()

    @pl.when(jnp.logical_not(atmos))
    def _():
        plane_ref[...] = whole_ref[1] + total_ref[...] + last_ref[...]
        copy = pltpu.make_async_copy(plane_ref, fields_hbm.at[0, 1], sem)
        copy.start()
        copy.wait()


def call(kernel, n_in, outs, flops=0, scratch=(), space=pltpu.VMEM, out_space=pltpu.VMEM, vmem=12):
    shapes = [jax.ShapeDtypeStruct(s, d) for s, d in outs]
    return pl.pallas_call(
        kernel,
        out_shape=shapes,
        in_specs=[pl.BlockSpec(memory_space=space)] * n_in,
        out_specs=[pl.BlockSpec(memory_space=out_space)] * len(shapes),
        scratch_shapes=scratch,
        compiler_params=pltpu.CompilerParams(vmem_limit_bytes=vmem * 1024 * 1024),
        cost_estimate=pl.CostEstimate(flops=flops, bytes_accessed=1 << 10, transcendentals=0),
    )


def swap_stage(bit, cap, arrays, chunks, after=None):
    n_tile = lax.axis_size("tile")
    going = [m for m in range(n_tile) if m & bit]
    if after is not None:
        arrays, after = lax.optimization_barrier((arrays, after))
    if bit == 1:
        give = arrays.pop()
    else:
        picks = [chunks[m] for m in going]
        used = sorted({i for i, _ in picks})
        picks = [(used.index(i), j) for i, j in picks]
        taken = [arrays[i] for i in used]
        if used[-1] != len(arrays) - 1:
            taken.append(arrays[-1])
        kernel = functools.partial(stack_kernel, picks, cap)
        (give,) = call(kernel, len(taken), [(arrays[-1].shape, F32)])(*taken)
    came = lax.ppermute(give, "tile", [(t, t ^ bit) for t in range(n_tile)])
    chunks = chunks | {m: (len(arrays), i) for i, m in enumerate(going)}
    return arrays + [came], chunks, after


def local(fields, coefficients, owner_tile, dest_block, table_index, tables, land_mask):
    n_sec, n_tile = lax.axis_size("sec"), lax.axis_size("tile")
    levels, rows, width = fields.shape[1:]
    fan = owner_tile.shape[1]
    n_tables = tables.shape[0]
    cap = 2 * fan * rows // n_tile
    slots, lines = n_tile * cap, n_tables * rows
    up8 = lambda n: -(-n // 8) * 8
    chunk, side = up8(cap + N_COEF + 8), up8(4 * (levels - 2))
    owner, dest, table = owner_tile.T, dest_block.T, table_index.T
    exchange = lambda x, axis: lax.all_to_all(x, axis, split_axis=0, concat_axis=0, tiled=True)
    plane = ((rows, width), F32)

    (send,) = call(
        functools.partial(send_kernel, cap),
        3,
        [((n_tile, chunk, width), F32)],
        scratch=[
            pltpu.VMEM((2, rows, width), F32),
            pltpu.VMEM((2, rows, width), F32),
            pltpu.VMEM(owner.shape, I32),
            pltpu.VMEM((n_tile, cap, width), F32),
            pltpu.VMEM((chunk - cap, width), F32),
            pltpu.SemaphoreType.DMA((4 + n_tile,)),
        ],
        space=pltpu.HBM,
        out_space=pltpu.HBM,
        vmem=60,
    )(fields, coefficients, owner)
    got = exchange(send, "tile")
    half = n_tile // 2 * cap
    keep, give = call(
        functools.partial(swap_kernel, cap),
        3,
        [((half + rows, width), F32), ((half + side, width), F32)],
        scratch=[pltpu.VMEM((n_tile, cap, width), F32)],
    )(fields, coefficients, owner)
    arrays, chunks, _ = swap_stage(1, cap, [keep, give], {m: (0, m // 2) for m in range(0, n_tile, 2)})
    (plan,) = call(
        functools.partial(index_kernel, cap, rows),
        5,
        [((PLAN_WAYS + 2 * n_tables, lines, width), BF16)],
        scratch=[pltpu.VMEM((slots, lines), F32)],
    )(owner, dest, table, tables, land_mask)
    arrays, chunks, plan = swap_stage(2, cap, arrays, chunks, plan)
    (part,) = call(functools.partial(flux_kernel, cap, n_tables), 1 + len(arrays), [plane])(got, plan, *arrays[:-1])
    others = [lax.ppermute(part, "sec", [(s, s ^ other) for s in range(n_sec)]) for other in range(n_sec - 1, 0, -1)]
    bit = 4
    while bit < n_tile:
        arrays, chunks, part = swap_stage(bit, cap, arrays, chunks, part)
        bit *= 2
    sources = [chunks[m] for m in range(n_tile)]
    top, back = call(functools.partial(sea_kernel, n_tables), 1 + n_sec, [plane, ((slots, width), F32)])(plan, part, *others)
    got, back = lax.optimization_barrier((got, back))
    (level,) = call(
        functools.partial(levels_kernel, cap), 4, [((levels * rows + 4 * n_tile + side, width), F32)], flops=1 << 32
    )(got, fields, coefficients, top)
    came = exchange(back.reshape(n_tile, cap, width), "tile").reshape(slots, width)
    (total,) = call(
        functools.partial(second_kernel, cap, n_tables, levels, sources),
        2 + len(arrays),
        [plane],
        scratch=[pltpu.VMEM((n_tile, cap, width), F32)],
        flops=1 << 34,
    )(plan, level, *arrays)
    came_total = 0.0
    bit = n_sec // 2
    while bit:
        above = n_sec - 2 * bit
        pairs = [(s, s | bit) for s in range(n_sec) if s & above == above and not s & bit]
        total = total + came_total
        came_total = lax.ppermute(total, "sec", pairs)
        bit //= 2
    (whole,) = call(
        functools.partial(finish_kernel, cap), 1 + len(arrays), [((levels, rows, width), F32)], flops=1 << 28
    )(got, level, *arrays[1:])
    ended, surface = call(
        functools.partial(end_kernel, n_tables),
        3,
        [(fields.shape, F32), ((1, rows, width), F32)],
        scratch=[pltpu.VMEM((rows, width), F32), pltpu.SemaphoreType.DMA((2,))],
        out_space=pltpu.HBM,
    )(came, plan, whole)
    came_total, surface = lax.optimization_barrier((came_total, surface))
    in_hbm, in_vmem = pl.BlockSpec(memory_space=pltpu.HBM), pl.BlockSpec(memory_space=pltpu.VMEM)
    ended = pl.pallas_call(
        forced_kernel,
        out_shape=jax.ShapeDtypeStruct(fields.shape, F32),
        in_specs=[in_hbm] + [in_vmem] * 3,
        out_specs=in_hbm,
        scratch_shapes=[pltpu.VMEM((rows, width), F32), pltpu.SemaphoreType.DMA],
        input_output_aliases={0: 0},
        compiler_params=pltpu.CompilerParams(vmem_limit_bytes=12 * 1024 * 1024),
    )(ended, whole, total, came_total)
    return ended, surface


def solution(mesh):
    placed = (P("sec", None, "tile", None), P("sec", None, "tile", None), P(), P(), P(), P(), P("tile", None))
    return jax.shard_map(
        local,
        mesh=mesh,
        in_specs=placed,
        out_specs=(P("sec", None, "tile", None), P("sec", "tile", None)),
        check_vma=False,
    )
```

```python
import functools

import jax
import jax.numpy as jnp
from jax import lax
from jax.experimental import pallas as pl
from jax.experimental.pallas import tpu as pltpu
from jax.sharding import PartitionSpec as P

FORCING = 0.5
F32, BF16, I32 = jnp.float32, jnp.bfloat16, jnp.int32
N_COEF = 6
PLAN_COLLECT, PLAN_ARRIVE, PLAN_EDGE, PLAN_BACK, PLAN_WAYS = 0, 1, 2, 3, 4


def iota(shape, axis):
    return lax.broadcasted_iota(I32, shape, axis)


def roll(x, shift, axis):
    return pltpu.roll(x, shift % x.shape[axis], axis)


def split(x, parts):
    out = []
    for _ in range(parts):
        out.append(x.astype(BF16))
        x = x - out[-1].astype(F32)
    return out


def mm(a, b):
    return lax.dot_general(a, b, (((1,), (0,)), ((), ())), preferred_element_type=F32)


def mm_t(a, b):
    return lax.dot_general(a, b, (((1,), (1,)), ((), ())), preferred_element_type=F32)


def select_rows(hot, x, parts):
    return mm(jnp.concatenate([hot] * parts, axis=1), jnp.concatenate(split(x, parts)))


def products(lines, plan_ref, rows, dot, axis):
    count = lines.shape[0] // rows
    a1, a2 = split(jnp.concatenate([lines[k * rows : (k + 1) * rows] for k in range(count)], axis=1), 2)
    b1, b2 = [jnp.concatenate([plan_ref[PLAN_WAYS + 2 * k + i] for k in range(count)], axis=axis) for i in range(2)]
    both = dot(jnp.concatenate([a1, a2]), b1)
    return both[:rows] + both[rows:] + dot(a1, b2)


def sideways(x, kappa):
    return x + kappa * (roll(x, 1, x.ndim - 1) + roll(x, -1, x.ndim - 1) - 4.0 * x)


def substep(u, kappa, speed):
    rows = u.shape[1]
    row = iota(u.shape, 1)
    upper = jnp.where(row == 0, 0.0, roll(u, 1, 1))
    lower = jnp.where(row == rows - 1, 0.0, roll(u, -1, 1))
    laplace = upper + lower + roll(u, 1, 2) + roll(u, -1, 2) - 4.0 * u
    return u + kappa * laplace - 0.5 * speed * (lower - upper)


def place():
    sec, tile = lax.axis_index("sec"), lax.axis_index("tile")
    return sec, tile, sec < lax.axis_size("sec") - 1


def own_slots(owner_ref, rows, cap):
    sec, tile, atmos = place()
    n_sec, n_tile = lax.axis_size("sec"), lax.axis_size("tile")
    block = (jnp.minimum(sec, n_sec - 2) * n_tile + tile) * rows
    first = pl.multiple_of(block // 128 * 128, 128)
    half = block - first
    shape = (n_tile * cap, 128)
    lane = iota((1, 128), 1)
    inside = (lane >= half) & (lane < half + rows) & atmos
    owner = jnp.where(inside, owner_ref[:, pl.ds(first, 128)], -1)
    slot = iota(shape, 0)
    hot = [(owner[r : r + 1] == slot // cap).astype(F32) for r in range(owner.shape[0])]
    both = sum(hot)
    before = (iota((128, 128), 0) < iota((128, 128), 1)).astype(BF16)
    rank = mm(both.astype(BF16), before)
    placed = rank == (slot % cap).astype(F32)
    return first, [jnp.where(placed, h, 0.0) for h in hot]


def edge_rows(u, kappa, a, b):
    top, bot = slice(0, 1), slice(u.shape[0] - 1, u.shape[0])
    q_top = sideways(u[top], kappa[top]) + b[top] * u[1:2]
    q_bot = sideways(u[bot], kappa[bot]) + a[bot] * u[-2:-1]
    return [u[top], q_top, u[bot], q_bot]


def padded(lines, count, width):
    if count > len(lines):
        lines = lines + [jnp.zeros((count - len(lines), width), F32)]
    return jnp.concatenate(lines)


def placed_rows(placed, payload):
    return select_rows(sum(placed).astype(BF16), jnp.concatenate([payload] * (128 // payload.shape[0])), 2)


def send_kernel(cap, fields_hbm, coef_hbm, owner_hbm, send_hbm, fields_ref, coef_ref, owner_ref, slots_ref, edge_ref, sems):
    pairs = ((owner_hbm, owner_ref), (coef_hbm.at[0], coef_ref), (fields_hbm.at[0, pl.ds(0, 2)], fields_ref))
    copies = [pltpu.make_async_copy(src, dst, sems.at[i]) for i, (src, dst) in enumerate(pairs)]
    for copy in copies:
        copy.start()
    copies[0].wait()
    _, rows, width = fields_ref.shape
    _, placed = own_slots(owner_ref, rows, cap)
    copies[1].wait()
    copies[2].wait()
    u = fields_ref[...]
    kappa, speed = coef_ref[0], coef_ref[1]
    a = kappa + 0.5 * speed
    b = kappa - 0.5 * speed
    bot = slice(rows - 1, rows)
    extra = [a[0:1], a[0:1] * a[1:2], kappa[0:1], b[bot], b[bot] * b[rows - 2 : rows - 1], kappa[bot]]
    extra += edge_rows(u[0], kappa, a, b) + edge_rows(u[1], kappa, a, b)
    n_tile, side = slots_ref.shape[0], edge_ref.shape[0]
    edge_ref[...] = padded(extra, side, width)
    going = [pltpu.make_async_copy(edge_ref, send_hbm.at[t, pl.ds(cap, side)], sems.at[3 + t]) for t in range(n_tile)]
    going.append(pltpu.make_async_copy(slots_ref, send_hbm.at[:, pl.ds(0, cap)], sems.at[3 + n_tile]))
    for copy in going[:-1]:
        copy.start()
    stepped = substep(substep(u[:1], kappa, speed), kappa, speed)[0]
    slots_ref[...] = placed_rows(placed, stepped).reshape(slots_ref.shape)
    going[-1].start()
    for copy in going:
        copy.wait()


def swap_kernel(cap, fields_ref, coef_ref, owner_ref, keep_ref, give_ref, slots_ref):
    _, tile, _ = place()
    levels, rows, width = fields_ref.shape[1:]
    _, placed = own_slots(owner_ref, rows, cap)
    kappa, speed = coef_ref[0, 0], coef_ref[0, 1]
    stepped = substep(substep(fields_ref[0, :2], kappa, speed), kappa, speed)
    count = slots_ref.shape[0]
    slots_ref[...] = placed_rows(placed, stepped[0] - stepped[1]).reshape(count, cap, width)
    for m in range(count):
        ref = (keep_ref, give_ref)[m % 2]
        ref[m // 2 * cap : (m // 2 + 1) * cap] = slots_ref[tile ^ m]
    a = kappa + 0.5 * speed
    b = kappa - 0.5 * speed
    extra = sum([edge_rows(fields_ref[0, l], kappa, a, b) for l in range(2, levels)], [])
    held = count // 2 * cap
    give_ref[held:] = padded(extra, give_ref.shape[0] - held, width)
    keep_ref[held:] = stepped[0]


def stack_kernel(picks, cap, *refs):
    out_ref = refs[-1]
    for to, (i, j) in enumerate(picks):
        out_ref[to * cap : (to + 1) * cap] = refs[i][j * cap : (j + 1) * cap]
    held = len(picks) * cap
    out_ref[held:] = refs[-2][held:]


def index_kernel(
    cap, rows, owner_ref, dest_ref, table_ref, tables_ref, mask_ref, plan_ref, arrive_sum
):
    n_tables = tables_ref.shape[0]
    for k in range(n_tables):
        at = PLAN_WAYS + 2 * k
        plan_ref[at], plan_ref[at + 1] = split(tables_ref[k], 2)
    sec, tile, atmos = place()
    n_sec, n_tile = lax.axis_size("sec"), lax.axis_size("tile")
    span = n_tile * rows
    start = jnp.minimum(sec, n_sec - 2) * span
    fan = owner_ref.shape[0]
    lines = n_tables * rows
    per = 128 // rows
    g, h = iota((128, 128), 0), iota((128, 128), 1)
    before = ((g < h) & (g // rows == h // rows)).astype(BF16)
    line = iota((lines, 128), 0)
    seat = iota((per * cap, 128), 0)
    lane = iota((per * cap, 128), 1)
    edges = jnp.zeros((lines, 128), F32)
    for group in range(span // 128):
        at = pl.ds(pl.multiple_of(start + group * 128, 128), 128)
        mine = [(owner_ref[r : r + 1, at] == tile) & atmos for r in range(fan)]
        key = jnp.full((1, 128), -1, I32)
        for r in range(fan):
            key = jnp.where(mine[r], table_ref[r : r + 1, at] * rows + dest_ref[r : r + 1, at], key)
        held = (key >= 0).astype(F32)
        rank = mm(jnp.broadcast_to(held, (16, 128)).astype(BF16), before)[:1]
        sits = (rank == (seat % cap).astype(F32)) & (lane // rows == seat // cap) & (held > 0)
        hit = (line == key).astype(BF16)
        arrive = mm_t(sits.astype(BF16), hit)
        arrive_sum[group * per * cap : (group + 1) * per * cap] = arrive
        block, within = group * per + g // rows, g % rows
        column = sum(jnp.where(within == w, i, 0) for i, w in enumerate((0, 1, rows - 2, rows - 1)))
        is_edge = (within < 2) | (within >= rows - 2)
        edges += mm(hit, (is_edge & (h == column * n_tile + block)).astype(BF16))
    arrive = arrive_sum[...]
    plan_ref[PLAN_ARRIVE] = arrive.astype(BF16)
    plan_ref[PLAN_COLLECT] = arrive.T.astype(BF16)
    plan_ref[PLAN_EDGE, :, :128] = edges.astype(BF16)
    for i in range(mask_ref.shape[1] // 128):
        plan_ref[PLAN_EDGE, i * rows : (i + 1) * rows, 128:] = mask_ref[:, i * 128 : (i + 1) * 128].astype(F32).astype(BF16)
    first, placed = own_slots(owner_ref, rows, cap)
    table = table_ref[:, pl.ds(first, 128)]
    for k in range(n_tables):
        here = sum(jnp.where(table[r : r + 1] == k, placed[r], 0.0) for r in range(fan))
        here = here.T
        plan_ref[PLAN_BACK, k * rows : (k + 1) * rows] = sum(here[i : i + rows] for i in range(0, 128, rows)).astype(BF16)


def shifted(x, by):
    row = iota(x.shape, 0)
    return jnp.where(row == (0 if by > 0 else x.shape[0] - 1), 0.0, roll(x, by, 0))


def corrections(coef, edges):
    a0, aa, k0, b1, bb, k1 = coef
    u0, q0, u1, q1 = edges
    b_prev, a_next = shifted(b1, 1), shifted(a0, -1)
    u_prev, q_prev, u_next, q_next = shifted(u1, 1), shifted(q1, 1), shifted(u0, -1), shifted(q0, -1)
    return [
        sideways(a0 * u_prev, k0) + a0 * (q_prev + b_prev * u0),
        aa * u_prev,
        bb * u_next,
        sideways(b1 * u_next, k1) + b1 * (q_next + a_next * u1),
    ]


def whole_level(plane, correction):
    _, tile, _ = place()
    rows = plane.shape[0]
    here = iota(correction[0].shape, 0) == tile
    own = [jnp.sum(jnp.where(here, c, 0.0), axis=0, keepdims=True) for c in correction]
    return jnp.concatenate(
        [plane[:2] + jnp.concatenate(own[:2]), plane[2 : rows - 2], plane[rows - 2 :] + jnp.concatenate(own[2:])]
    )


def water(plan_ref, rows):
    parts = plan_ref.shape[2] // 128
    return jnp.concatenate([plan_ref[PLAN_EDGE, i * rows : (i + 1) * rows, 128:] for i in range(parts)], axis=1).astype(F32)


def grouped_edges(correction, plan_ref):
    short = 128 - correction.shape[0]
    if short:
        correction = jnp.concatenate([correction, jnp.zeros((short, correction.shape[1]), F32)])
    return select_rows(plan_ref[PLAN_EDGE, :, :128], correction, 2)


def flux_of(slots, edges, plan_ref, n_tables, rows):
    grouped = select_rows(plan_ref[PLAN_COLLECT], slots, 2) + edges
    return products(grouped, plan_ref, rows, mm, 0)


def lines_of(ref, first, count):
    return [ref[:, first + i, :] for i in range(count)]


def flux_kernel(cap, n_tables, got_ref, plan_ref, keep_ref, *refs):
    part_ref = refs[-1]
    _, _, atmos = place()
    n_tile, _, width = got_ref.shape
    rows = part_ref.shape[0]
    stepped = keep_ref[keep_ref.shape[0] - rows :]
    correction = corrections(lines_of(got_ref, cap, N_COEF), lines_of(got_ref, cap + N_COEF, 4))
    whole = whole_level(stepped, correction)
    slots = got_ref[:, :cap, :].reshape(n_tile * cap, width)
    flux = flux_of(slots, grouped_edges(jnp.concatenate(correction), plan_ref), plan_ref, n_tables, rows)
    part_ref[...] = jnp.where(atmos, FORCING * water(plan_ref, rows) * flux, whole)


def levels_kernel(cap, got_ref, fields_ref, coef_ref, top_ref, level_ref):
    _, _, atmos = place()
    kappa, speed = coef_ref[0, 0], coef_ref[0, 1]
    levels, rows, width = fields_ref.shape[1:]
    n_tile = got_ref.shape[0]
    stepped = substep(substep(fields_ref[0], kappa, speed), kappa, speed)
    coef = lines_of(got_ref, cap, N_COEF)
    first, second = [corrections(coef, lines_of(got_ref, cap + N_COEF + 4 * l, 4)) for l in range(2)]
    level_ref[:rows] = jnp.where(atmos, whole_level(stepped[0], first), top_ref[...])
    level_ref[rows : 2 * rows] = whole_level(stepped[1], second)
    level_ref[2 * rows : levels * rows] = stepped[2:].reshape((levels - 2) * rows, width)
    at = levels * rows + 4 * n_tile
    level_ref[levels * rows : at] = jnp.concatenate([x - y for x, y in zip(first, second)])
    level_ref[at:] = padded(
        sum([[u[:1], u[:1], u[rows - 1 :], u[rows - 1 :]] for u in [fields_ref[0, l] for l in range(2, levels)]], []),
        level_ref.shape[0] - at,
        width,
    )


def second_kernel(cap, n_tables, levels, sources, plan_ref, level_ref, *refs):
    swapped, (part_ref, came_ref) = refs[:-2], refs[-2:]
    _, tile, atmos = place()
    n_tile, _, width = came_ref.shape
    rows = part_ref.shape[0]
    edges = level_ref[levels * rows : levels * rows + 4 * n_tile]
    for m, (i, j) in enumerate(sources):
        came_ref[tile ^ m] = swapped[i][j * cap : (j + 1) * cap]
    flux = flux_of(came_ref[...].reshape(n_tile * cap, width), grouped_edges(edges, plan_ref), plan_ref, n_tables, rows)
    part_ref[...] = jnp.where(atmos, FORCING * water(plan_ref, rows) * flux, 0.0)


def finish_kernel(cap, got_ref, level_ref, *refs):
    swapped, whole_ref = refs[:-1], refs[-1]
    _, tile, _ = place()
    levels, rows, width = whole_ref.shape
    n_tile = got_ref.shape[0]
    whole_ref[...] = level_ref[: levels * rows].reshape(levels, rows, width)
    count = 4 * (levels - 2)
    held = n_tile // 2 * cap
    prev = jnp.zeros((count, width), F32)
    after = prev
    for i, ref in enumerate(swapped):
        other = tile ^ (2 ** (i + 1) - 1)
        came = ref[held : held + count]
        prev = jnp.where(other == tile - 1, came, prev)
        after = jnp.where(other == tile + 1, came, after)
    own = got_ref[tile, cap : cap + 8]
    a0, aa, k0, b1, bb, k1 = [own[i : i + 1] for i in range(N_COEF)]
    b_prev = jnp.where(tile > 0, got_ref[jnp.maximum(tile - 1, 0), cap : cap + 8][3:4], 0.0)
    a_next = jnp.where(tile < n_tile - 1, got_ref[jnp.minimum(tile + 1, n_tile - 1), cap : cap + 8][0:1], 0.0)
    for l in range(2, levels):
        u0, _, u1, _ = [level_ref[levels * rows + 4 * n_tile + 4 * (l - 2) + i : levels * rows + 4 * n_tile + 4 * (l - 2) + i + 1] for i in range(4)]
        u_prev, q_prev = [prev[4 * (l - 2) + i : 4 * (l - 2) + i + 1] for i in (2, 3)]
        u_next, q_next = [after[4 * (l - 2) + i : 4 * (l - 2) + i + 1] for i in (0, 1)]
        whole_ref[l, :2] += jnp.concatenate([sideways(a0 * u_prev, k0) + a0 * (q_prev + b_prev * u0), aa * u_prev])
        whole_ref[l, rows - 2 :] += jnp.concatenate([bb * u_next, sideways(b1 * u_next, k1) + b1 * (q_next + a_next * u1)])


def sea_kernel(n_tables, plan_ref, *refs):
    parts, (top_ref, back_ref) = refs[:-2], refs[-2:]
    top = sum(part[...] for part in parts)
    top_ref[...] = top
    sea = water(plan_ref, top.shape[0]) * top
    back_ref[...] = select_rows(plan_ref[PLAN_ARRIVE], jnp.concatenate([sea] * n_tables), 2)


def end_kernel(n_tables, came_ref, plan_ref, whole_ref, fields_hbm, surface_hbm, surface_ref, sems):
    _, _, atmos = place()
    _, rows, width = whole_ref.shape
    copies = [
        pltpu.make_async_copy(whole_ref, fields_hbm.at[0], sems.at[0]),
        pltpu.make_async_copy(surface_ref, surface_hbm.at[0], sems.at[1]),
    ]
    copies[0].start()
    picked = select_rows(plan_ref[PLAN_BACK], came_ref[...], 2)
    seen = products(picked, plan_ref, rows, mm_t, 1)
    surface_ref[...] = jnp.where(atmos, seen, water(plan_ref, rows) * whole_ref[0])
    copies[1].start()
    for copy in copies:
        copy.wait()


def forced_kernel(_, whole_ref, total_ref, last_ref, fields_hbm, plane_ref, sem):
    _, _, atmos = place()

    @pl.when(jnp.logical_not(atmos))
    def _():
        plane_ref[...] = whole_ref[1] + total_ref[...] + last_ref[...]
        copy = pltpu.make_async_copy(plane_ref, fields_hbm.at[0, 1], sem)
        copy.start()
        copy.wait()


def call(kernel, n_in, outs, flops=0, scratch=(), space=pltpu.VMEM, out_space=pltpu.VMEM, vmem=12):
    shapes = [jax.ShapeDtypeStruct(s, d) for s, d in outs]
    return pl.pallas_call(
        kernel,
        out_shape=shapes,
        in_specs=[pl.BlockSpec(memory_space=space)] * n_in,
        out_specs=[pl.BlockSpec(memory_space=out_space)] * len(shapes),
        scratch_shapes=scratch,
        compiler_params=pltpu.CompilerParams(vmem_limit_bytes=vmem * 1024 * 1024),
        cost_estimate=pl.CostEstimate(flops=flops, bytes_accessed=1 << 10, transcendentals=0),
    )


def swap_stage(bit, cap, arrays, chunks, after=None):
    n_tile = lax.axis_size("tile")
    going = [m for m in range(n_tile) if m & bit]
    if after is not None:
        arrays, after = lax.optimization_barrier((arrays, after))
    if bit == 1:
        give = arrays.pop()
    else:
        picks = [chunks[m] for m in going]
        used = sorted({i for i, _ in picks})
        picks = [(used.index(i), j) for i, j in picks]
        taken = [arrays[i] for i in used]
        if used[-1] != len(arrays) - 1:
            taken.append(arrays[-1])
        kernel = functools.partial(stack_kernel, picks, cap)
        (give,) = call(kernel, len(taken), [(arrays[-1].shape, F32)])(*taken)
    came = lax.ppermute(give, "tile", [(t, t ^ bit) for t in range(n_tile)])
    chunks = chunks | {m: (len(arrays), i) for i, m in enumerate(going)}
    return arrays + [came], chunks, after


def local(fields, coefficients, owner_tile, dest_block, table_index, tables, land_mask):
    n_sec, n_tile = lax.axis_size("sec"), lax.axis_size("tile")
    levels, rows, width = fields.shape[1:]
    fan = owner_tile.shape[1]
    n_tables = tables.shape[0]
    cap = 2 * fan * rows // n_tile
    slots, lines = n_tile * cap, n_tables * rows
    up8 = lambda n: -(-n // 8) * 8
    chunk, side = up8(cap + N_COEF + 8), up8(4 * (levels - 2))
    owner, dest, table = owner_tile.T, dest_block.T, table_index.T
    exchange = lambda x, axis: lax.all_to_all(x, axis, split_axis=0, concat_axis=0, tiled=True)
    plane = ((rows, width), F32)

    (send,) = call(
        functools.partial(send_kernel, cap),
        3,
        [((n_tile, chunk, width), F32)],
        scratch=[
            pltpu.VMEM((2, rows, width), F32),
            pltpu.VMEM((2, rows, width), F32),
            pltpu.VMEM(owner.shape, I32),
            pltpu.VMEM((n_tile, cap, width), F32),
            pltpu.VMEM((chunk - cap, width), F32),
            pltpu.SemaphoreType.DMA((4 + n_tile,)),
        ],
        space=pltpu.HBM,
        out_space=pltpu.HBM,
        vmem=60,
    )(fields, coefficients, owner)
    got = exchange(send, "tile")
    half = n_tile // 2 * cap
    keep, give = call(
        functools.partial(swap_kernel, cap),
        3,
        [((half + rows, width), F32), ((half + side, width), F32)],
        scratch=[pltpu.VMEM((n_tile, cap, width), F32)],
    )(fields, coefficients, owner)
    arrays, chunks, _ = swap_stage(1, cap, [keep, give], {m: (0, m // 2) for m in range(0, n_tile, 2)})
    (plan,) = call(
        functools.partial(index_kernel, cap, rows),
        5,
        [((PLAN_WAYS + 2 * n_tables, lines, width), BF16)],
        scratch=[pltpu.VMEM((slots, lines), F32)],
    )(owner, dest, table, tables, land_mask)
    arrays, chunks, plan = swap_stage(2, cap, arrays, chunks, plan)
    (part,) = call(functools.partial(flux_kernel, cap, n_tables), 1 + len(arrays), [plane])(got, plan, *arrays[:-1])
    others = [lax.ppermute(part, "sec", [(s, s ^ other) for s in range(n_sec)]) for other in range(n_sec - 1, 0, -1)]
    bit = 4
    while bit < n_tile:
        arrays, chunks, part = swap_stage(bit, cap, arrays, chunks, part)
        bit *= 2
    sources = [chunks[m] for m in range(n_tile)]
    top, back = call(functools.partial(sea_kernel, n_tables), 1 + n_sec, [plane, ((slots, width), F32)])(plan, part, *others)
    got, back = lax.optimization_barrier((got, back))
    (level,) = call(
        functools.partial(levels_kernel, cap), 4, [((levels * rows + 4 * n_tile + side, width), F32)], flops=1 << 32
    )(got, fields, coefficients, top)
    came = exchange(back.reshape(n_tile, cap, width), "tile").reshape(slots, width)
    (total,) = call(
        functools.partial(second_kernel, cap, n_tables, levels, sources),
        2 + len(arrays),
        [plane],
        scratch=[pltpu.VMEM((n_tile, cap, width), F32)],
        flops=1 << 34,
    )(plan, level, *arrays)
    came_total = 0.0
    bit = n_sec // 2
    while bit:
        above = n_sec - 2 * bit
        pairs = [(s, s | bit) for s in range(n_sec) if s & above == above and not s & bit]
        total = total + came_total
        came_total = lax.ppermute(total, "sec", pairs)
        bit //= 2
    (whole,) = call(
        functools.partial(finish_kernel, cap), 1 + len(arrays), [((levels, rows, width), F32)], flops=1 << 28
    )(got, level, *arrays[1:])
    ended, surface = call(
        functools.partial(end_kernel, n_tables),
        3,
        [(fields.shape, F32), ((1, rows, width), F32)],
        scratch=[pltpu.VMEM((rows, width), F32), pltpu.SemaphoreType.DMA((2,))],
        out_space=pltpu.HBM,
    )(came, plan, whole)
    came_total, surface = lax.optimization_barrier((came_total, surface))
    in_hbm, in_vmem = pl.BlockSpec(memory_space=pltpu.HBM), pl.BlockSpec(memory_space=pltpu.VMEM)
    ended = pl.pallas_call(
        forced_kernel,
        out_shape=jax.ShapeDtypeStruct(fields.shape, F32),
        in_specs=[in_hbm] + [in_vmem] * 3,
        out_specs=in_hbm,
        scratch_shapes=[pltpu.VMEM((rows, width), F32), pltpu.SemaphoreType.DMA],
        input_output_aliases={0: 0},
        compiler_params=pltpu.CompilerParams(vmem_limit_bytes=12 * 1024 * 1024),
    )(ended, whole, total, came_total)
    return ended, surface


def solution(mesh):
    placed = (P("sec", None, "tile", None), P("sec", None, "tile", None), P(), P(), P(), P(), P("tile", None))
    return jax.shard_map(
        local,
        mesh=mesh,
        in_specs=placed,
        out_specs=(P("sec", None, "tile", None), P("sec", "tile", None)),
        check_vma=False,
    )
```

```python
import functools

import jax
import jax.numpy as jnp
from jax import lax
from jax.experimental import pallas as pl
from jax.experimental.pallas import tpu as pltpu
from jax.sharding import PartitionSpec as P

FORCING = 0.5
F32, BF16, I32 = jnp.float32, jnp.bfloat16, jnp.int32
N_COEF = 6
PLAN_COLLECT, PLAN_ARRIVE, PLAN_EDGE, PLAN_BACK, PLAN_WAYS = 0, 1, 2, 3, 4


def iota(shape, axis):
    return lax.broadcasted_iota(I32, shape, axis)


def roll(x, shift, axis):
    return pltpu.roll(x, shift % x.shape[axis], axis)


def split(x, parts):
    out = []
    for _ in range(parts):
        out.append(x.astype(BF16))
        x = x - out[-1].astype(F32)
    return out


def mm(a, b):
    return lax.dot_general(a, b, (((1,), (0,)), ((), ())), preferred_element_type=F32)


def mm_t(a, b):
    return lax.dot_general(a, b, (((1,), (1,)), ((), ())), preferred_element_type=F32)


def select_rows(hot, x, parts):
    return mm(jnp.concatenate([hot] * parts, axis=1), jnp.concatenate(split(x, parts)))


def products(lines, plan_ref, rows, dot, axis):
    count = lines.shape[0] // rows
    a1, a2 = split(jnp.concatenate([lines[k * rows : (k + 1) * rows] for k in range(count)], axis=1), 2)
    b1, b2 = [jnp.concatenate([plan_ref[PLAN_WAYS + 2 * k + i] for k in range(count)], axis=axis) for i in range(2)]
    both = dot(jnp.concatenate([a1, a2]), b1)
    return both[:rows] + both[rows:] + dot(a1, b2)


def sideways(x, kappa):
    return x + kappa * (roll(x, 1, x.ndim - 1) + roll(x, -1, x.ndim - 1) - 4.0 * x)


def substep(u, kappa, speed):
    rows = u.shape[1]
    row = iota(u.shape, 1)
    upper = jnp.where(row == 0, 0.0, roll(u, 1, 1))
    lower = jnp.where(row == rows - 1, 0.0, roll(u, -1, 1))
    laplace = upper + lower + roll(u, 1, 2) + roll(u, -1, 2) - 4.0 * u
    return u + kappa * laplace - 0.5 * speed * (lower - upper)


def place():
    sec, tile = lax.axis_index("sec"), lax.axis_index("tile")
    return sec, tile, sec < lax.axis_size("sec") - 1


def own_slots(owner_ref, rows, cap):
    sec, tile, atmos = place()
    n_sec, n_tile = lax.axis_size("sec"), lax.axis_size("tile")
    block = (jnp.minimum(sec, n_sec - 2) * n_tile + tile) * rows
    first = pl.multiple_of(block // 128 * 128, 128)
    half = block - first
    shape = (n_tile * cap, 128)
    lane = iota((1, 128), 1)
    inside = (lane >= half) & (lane < half + rows) & atmos
    owner = jnp.where(inside, owner_ref[:, pl.ds(first, 128)], -1)
    slot = iota(shape, 0)
    hot = [(owner[r : r + 1] == slot // cap).astype(F32) for r in range(owner.shape[0])]
    both = sum(hot)
    before = (iota((128, 128), 0) < iota((128, 128), 1)).astype(BF16)
    rank = mm(both.astype(BF16), before)
    placed = rank == (slot % cap).astype(F32)
    return first, [jnp.where(placed, h, 0.0) for h in hot]


def edge_rows(u, kappa, a, b):
    top, bot = slice(0, 1), slice(u.shape[0] - 1, u.shape[0])
    q_top = sideways(u[top], kappa[top]) + b[top] * u[1:2]
    q_bot = sideways(u[bot], kappa[bot]) + a[bot] * u[-2:-1]
    return [u[top], q_top, u[bot], q_bot]


def padded(lines, count, width):
    if count > len(lines):
        lines = lines + [jnp.zeros((count - len(lines), width), F32)]
    return jnp.concatenate(lines)


def placed_rows(placed, payload):
    return select_rows(sum(placed).astype(BF16), jnp.concatenate([payload] * (128 // payload.shape[0])), 2)


def send_kernel(cap, fields_hbm, coef_hbm, owner_hbm, send_hbm, fields_ref, coef_ref, owner_ref, slots_ref, edge_ref, sems):
    pairs = ((owner_hbm, owner_ref), (coef_hbm.at[0], coef_ref), (fields_hbm.at[0, pl.ds(0, 2)], fields_ref))
    copies = [pltpu.make_async_copy(src, dst, sems.at[i]) for i, (src, dst) in enumerate(pairs)]
    for copy in copies:
        copy.start()
    copies[0].wait()
    _, rows, width = fields_ref.shape
    _, placed = own_slots(owner_ref, rows, cap)
    copies[1].wait()
    copies[2].wait()
    u = fields_ref[...]
    kappa, speed = coef_ref[0], coef_ref[1]
    a = kappa + 0.5 * speed
    b = kappa - 0.5 * speed
    bot = slice(rows - 1, rows)
    extra = [a[0:1], a[0:1] * a[1:2], kappa[0:1], b[bot], b[bot] * b[rows - 2 : rows - 1], kappa[bot]]
    extra += edge_rows(u[0], kappa, a, b) + edge_rows(u[1], kappa, a, b)
    n_tile, side = slots_ref.shape[0], edge_ref.shape[0]
    edge_ref[...] = padded(extra, side, width)
    going = [pltpu.make_async_copy(edge_ref, send_hbm.at[t, pl.ds(cap, side)], sems.at[3 + t]) for t in range(n_tile)]
    going.append(pltpu.make_async_copy(slots_ref, send_hbm.at[:, pl.ds(0, cap)], sems.at[3 + n_tile]))
    for copy in going[:-1]:
        copy.start()
    stepped = substep(substep(u[:1], kappa, speed), kappa, speed)[0]
    slots_ref[...] = placed_rows(placed, stepped).reshape(slots_ref.shape)
    going[-1].start()
    for copy in going:
        copy.wait()


def swap_kernel(cap, fields_ref, coef_ref, owner_ref, keep_ref, give_ref, slots_ref):
    _, tile, _ = place()
    levels, rows, width = fields_ref.shape[1:]
    _, placed = own_slots(owner_ref, rows, cap)
    kappa, speed = coef_ref[0, 0], coef_ref[0, 1]
    stepped = substep(substep(fields_ref[0, :2], kappa, speed), kappa, speed)
    count = slots_ref.shape[0]
    slots_ref[...] = placed_rows(placed, stepped[0] - stepped[1]).reshape(count, cap, width)
    for m in range(count):
        ref = (keep_ref, give_ref)[m % 2]
        ref[m // 2 * cap : (m // 2 + 1) * cap] = slots_ref[tile ^ m]
    a = kappa + 0.5 * speed
    b = kappa - 0.5 * speed
    extra = sum([edge_rows(fields_ref[0, l], kappa, a, b) for l in range(2, levels)], [])
    held = count // 2 * cap
    give_ref[held:] = padded(extra, give_ref.shape[0] - held, width)
    keep_ref[held:] = stepped[0]


def stack_kernel(picks, cap, *refs):
    out_ref = refs[-1]
    for to, (i, j) in enumerate(picks):
        out_ref[to * cap : (to + 1) * cap] = refs[i][j * cap : (j + 1) * cap]
    held = len(picks) * cap
    out_ref[held:] = refs[-2][held:]


def index_kernel(
    cap, rows, owner_ref, dest_ref, table_ref, tables_ref, mask_ref, plan_ref, arrive_sum
):
    n_tables = tables_ref.shape[0]
    for k in range(n_tables):
        at = PLAN_WAYS + 2 * k
        plan_ref[at], plan_ref[at + 1] = split(tables_ref[k], 2)
    sec, tile, atmos = place()
    n_sec, n_tile = lax.axis_size("sec"), lax.axis_size("tile")
    span = n_tile * rows
    start = jnp.minimum(sec, n_sec - 2) * span
    fan = owner_ref.shape[0]
    lines = n_tables * rows
    per = 128 // rows
    g, h = iota((128, 128), 0), iota((128, 128), 1)
    before = ((g < h) & (g // rows == h // rows)).astype(BF16)
    line = iota((lines, 128), 0)
    seat = iota((per * cap, 128), 0)
    lane = iota((per * cap, 128), 1)
    edges = jnp.zeros((lines, 128), F32)
    for group in range(span // 128):
        at = pl.ds(pl.multiple_of(start + group * 128, 128), 128)
        mine = [(owner_ref[r : r + 1, at] == tile) & atmos for r in range(fan)]
        key = jnp.full((1, 128), -1, I32)
        for r in range(fan):
            key = jnp.where(mine[r], table_ref[r : r + 1, at] * rows + dest_ref[r : r + 1, at], key)
        held = (key >= 0).astype(F32)
        rank = mm(jnp.broadcast_to(held, (16, 128)).astype(BF16), before)[:1]
        sits = (rank == (seat % cap).astype(F32)) & (lane // rows == seat // cap) & (held > 0)
        hit = (line == key).astype(BF16)
        arrive = mm_t(sits.astype(BF16), hit)
        arrive_sum[group * per * cap : (group + 1) * per * cap] = arrive
        block, within = group * per + g // rows, g % rows
        column = sum(jnp.where(within == w, i, 0) for i, w in enumerate((0, 1, rows - 2, rows - 1)))
        is_edge = (within < 2) | (within >= rows - 2)
        edges += mm(hit, (is_edge & (h == column * n_tile + block)).astype(BF16))
    arrive = arrive_sum[...]
    spread = sum(arrive[:, k * rows : (k + 1) * rows] for k in range(n_tables))
    plan_ref[PLAN_ARRIVE, :, : 2 * rows] = jnp.concatenate([spread] * 2, axis=1).astype(BF16)
    plan_ref[PLAN_COLLECT] = arrive.T.astype(BF16)
    plan_ref[PLAN_EDGE, :, :128] = edges.astype(BF16)
    for i in range(mask_ref.shape[1] // 128):
        plan_ref[PLAN_EDGE, i * rows : (i + 1) * rows, 128:] = mask_ref[:, i * 128 : (i + 1) * 128].astype(F32).astype(BF16)
    first, placed = own_slots(owner_ref, rows, cap)
    table = table_ref[:, pl.ds(first, 128)]
    for k in range(n_tables):
        here = sum(jnp.where(table[r : r + 1] == k, placed[r], 0.0) for r in range(fan))
        here = here.T
        plan_ref[PLAN_BACK, k * rows : (k + 1) * rows] = sum(here[i : i + rows] for i in range(0, 128, rows)).astype(BF16)


def shifted(x, by):
    row = iota(x.shape, 0)
    return jnp.where(row == (0 if by > 0 else x.shape[0] - 1), 0.0, roll(x, by, 0))


def corrections(coef, edges):
    a0, aa, k0, b1, bb, k1 = coef
    u0, q0, u1, q1 = edges
    b_prev, a_next = shifted(b1, 1), shifted(a0, -1)
    u_prev, q_prev, u_next, q_next = shifted(u1, 1), shifted(q1, 1), shifted(u0, -1), shifted(q0, -1)
    return [
        sideways(a0 * u_prev, k0) + a0 * (q_prev + b_prev * u0),
        aa * u_prev,
        bb * u_next,
        sideways(b1 * u_next, k1) + b1 * (q_next + a_next * u1),
    ]


def whole_level(plane, correction):
    _, tile, _ = place()
    rows = plane.shape[0]
    here = iota(correction[0].shape, 0) == tile
    own = [jnp.sum(jnp.where(here, c, 0.0), axis=0, keepdims=True) for c in correction]
    return jnp.concatenate(
        [plane[:2] + jnp.concatenate(own[:2]), plane[2 : rows - 2], plane[rows - 2 :] + jnp.concatenate(own[2:])]
    )


def water(plan_ref, rows):
    parts = plan_ref.shape[2] // 128
    return jnp.concatenate([plan_ref[PLAN_EDGE, i * rows : (i + 1) * rows, 128:] for i in range(parts)], axis=1).astype(F32)


def flux_of(slots, edges, plan_ref, rows):
    short = 128 - edges.shape[0]
    if short:
        edges = jnp.concatenate([edges, jnp.zeros((short, edges.shape[1]), F32)])
    hot = jnp.concatenate([plan_ref[PLAN_COLLECT], plan_ref[PLAN_EDGE, :, :128]], axis=1)
    return products(select_rows(hot, jnp.concatenate([slots, edges]), 2), plan_ref, rows, mm, 0)


def lines_of(ref, first, count):
    return [ref[:, first + i, :] for i in range(count)]


def flux_kernel(cap, n_tables, got_ref, plan_ref, keep_ref, *refs):
    part_ref = refs[-1]
    _, _, atmos = place()
    n_tile, _, width = got_ref.shape
    rows = part_ref.shape[0]
    stepped = keep_ref[keep_ref.shape[0] - rows :]
    correction = corrections(lines_of(got_ref, cap, N_COEF), lines_of(got_ref, cap + N_COEF, 4))
    whole = whole_level(stepped, correction)
    slots = got_ref[:, :cap, :].reshape(n_tile * cap, width)
    flux = flux_of(slots, jnp.concatenate(correction), plan_ref, rows)
    part_ref[...] = jnp.where(atmos, FORCING * water(plan_ref, rows) * flux, whole)


def levels_kernel(cap, got_ref, fields_ref, coef_ref, top_ref, level_ref):
    _, _, atmos = place()
    kappa, speed = coef_ref[0, 0], coef_ref[0, 1]
    levels, rows, width = fields_ref.shape[1:]
    n_tile = got_ref.shape[0]
    stepped = substep(substep(fields_ref[0], kappa, speed), kappa, speed)
    coef = lines_of(got_ref, cap, N_COEF)
    first, second = [corrections(coef, lines_of(got_ref, cap + N_COEF + 4 * l, 4)) for l in range(2)]
    level_ref[:rows] = jnp.where(atmos, whole_level(stepped[0], first), top_ref[...])
    level_ref[rows : 2 * rows] = whole_level(stepped[1], second)
    level_ref[2 * rows : levels * rows] = stepped[2:].reshape((levels - 2) * rows, width)
    at = levels * rows + 4 * n_tile
    level_ref[levels * rows : at] = jnp.concatenate([x - y for x, y in zip(first, second)])
    level_ref[at:] = padded(
        sum([[u[:1], u[:1], u[rows - 1 :], u[rows - 1 :]] for u in [fields_ref[0, l] for l in range(2, levels)]], []),
        level_ref.shape[0] - at,
        width,
    )


def second_kernel(cap, n_tables, levels, sources, plan_ref, level_ref, *refs):
    swapped, (part_ref, came_ref) = refs[:-2], refs[-2:]
    _, tile, atmos = place()
    n_tile, _, width = came_ref.shape
    rows = part_ref.shape[0]
    edges = level_ref[levels * rows : levels * rows + 4 * n_tile]
    for m, (i, j) in enumerate(sources):
        came_ref[tile ^ m] = swapped[i][j * cap : (j + 1) * cap]
    flux = flux_of(came_ref[...].reshape(n_tile * cap, width), edges, plan_ref, rows)
    part_ref[...] = jnp.where(atmos, FORCING * water(plan_ref, rows) * flux, 0.0)


def finish_kernel(cap, got_ref, level_ref, *refs):
    swapped, whole_ref = refs[:-1], refs[-1]
    _, tile, _ = place()
    levels, rows, width = whole_ref.shape
    n_tile = got_ref.shape[0]
    whole_ref[...] = level_ref[: levels * rows].reshape(levels, rows, width)
    count = 4 * (levels - 2)
    held = n_tile // 2 * cap
    prev = jnp.zeros((count, width), F32)
    after = prev
    for i, ref in enumerate(swapped):
        other = tile ^ (2 ** (i + 1) - 1)
        came = ref[held : held + count]
        prev = jnp.where(other == tile - 1, came, prev)
        after = jnp.where(other == tile + 1, came, after)
    own = got_ref[tile, cap : cap + 8]
    a0, aa, k0, b1, bb, k1 = [own[i : i + 1] for i in range(N_COEF)]
    b_prev = jnp.where(tile > 0, got_ref[jnp.maximum(tile - 1, 0), cap : cap + 8][3:4], 0.0)
    a_next = jnp.where(tile < n_tile - 1, got_ref[jnp.minimum(tile + 1, n_tile - 1), cap : cap + 8][0:1], 0.0)
    for l in range(2, levels):
        u0, _, u1, _ = [level_ref[levels * rows + 4 * n_tile + 4 * (l - 2) + i : levels * rows + 4 * n_tile + 4 * (l - 2) + i + 1] for i in range(4)]
        u_prev, q_prev = [prev[4 * (l - 2) + i : 4 * (l - 2) + i + 1] for i in (2, 3)]
        u_next, q_next = [after[4 * (l - 2) + i : 4 * (l - 2) + i + 1] for i in (0, 1)]
        whole_ref[l, :2] += jnp.concatenate([sideways(a0 * u_prev, k0) + a0 * (q_prev + b_prev * u0), aa * u_prev])
        whole_ref[l, rows - 2 :] += jnp.concatenate([bb * u_next, sideways(b1 * u_next, k1) + b1 * (q_next + a_next * u1)])


def sea_kernel(n_tables, plan_ref, *refs):
    parts, (top_ref, back_ref) = refs[:-2], refs[-2:]
    top = sum(part[...] for part in parts)
    top_ref[...] = top
    sea = water(plan_ref, top.shape[0]) * top
    back_ref[...] = mm(plan_ref[PLAN_ARRIVE, :, : 2 * sea.shape[0]], jnp.concatenate(split(sea, 2)))


def end_kernel(n_tables, came_ref, plan_ref, whole_ref, fields_hbm, surface_hbm, surface_ref, sems):
    _, _, atmos = place()
    _, rows, width = whole_ref.shape
    copies = [
        pltpu.make_async_copy(whole_ref, fields_hbm.at[0], sems.at[0]),
        pltpu.make_async_copy(surface_ref, surface_hbm.at[0], sems.at[1]),
    ]
    copies[0].start()
    picked = select_rows(plan_ref[PLAN_BACK], came_ref[...], 2)
    seen = products(picked, plan_ref, rows, mm_t, 1)
    surface_ref[...] = jnp.where(atmos, seen, water(plan_ref, rows) * whole_ref[0])
    copies[1].start()
    for copy in copies:
        copy.wait()


def forced_kernel(_, whole_ref, total_ref, last_ref, fields_hbm, plane_ref, sem):
    _, _, atmos = place()

    @pl.when(jnp.logical_not(atmos))
    def _():
        plane_ref[...] = whole_ref[1] + total_ref[...] + last_ref[...]
        copy = pltpu.make_async_copy(plane_ref, fields_hbm.at[0, 1], sem)
        copy.start()
        copy.wait()


def call(kernel, n_in, outs, flops=0, scratch=(), space=pltpu.VMEM, out_space=pltpu.VMEM, vmem=12):
    shapes = [jax.ShapeDtypeStruct(s, d) for s, d in outs]
    return pl.pallas_call(
        kernel,
        out_shape=shapes,
        in_specs=[pl.BlockSpec(memory_space=space)] * n_in,
        out_specs=[pl.BlockSpec(memory_space=out_space)] * len(shapes),
        scratch_shapes=scratch,
        compiler_params=pltpu.CompilerParams(vmem_limit_bytes=vmem * 1024 * 1024),
        cost_estimate=pl.CostEstimate(flops=flops, bytes_accessed=1 << 10, transcendentals=0),
    )


def swap_stage(bit, cap, arrays, chunks, after=None):
    n_tile = lax.axis_size("tile")
    going = [m for m in range(n_tile) if m & bit]
    if after is not None:
        arrays, after = lax.optimization_barrier((arrays, after))
    if bit == 1:
        give = arrays.pop()
    else:
        picks = [chunks[m] for m in going]
        used = sorted({i for i, _ in picks})
        picks = [(used.index(i), j) for i, j in picks]
        taken = [arrays[i] for i in used]
        if used[-1] != len(arrays) - 1:
            taken.append(arrays[-1])
        kernel = functools.partial(stack_kernel, picks, cap)
        (give,) = call(kernel, len(taken), [(arrays[-1].shape, F32)])(*taken)
    came = lax.ppermute(give, "tile", [(t, t ^ bit) for t in range(n_tile)])
    chunks = chunks | {m: (len(arrays), i) for i, m in enumerate(going)}
    return arrays + [came], chunks, after


def local(fields, coefficients, owner_tile, dest_block, table_index, tables, land_mask):
    n_sec, n_tile = lax.axis_size("sec"), lax.axis_size("tile")
    levels, rows, width = fields.shape[1:]
    fan = owner_tile.shape[1]
    n_tables = tables.shape[0]
    cap = 2 * fan * rows // n_tile
    slots, lines = n_tile * cap, n_tables * rows
    up8 = lambda n: -(-n // 8) * 8
    chunk, side = up8(cap + N_COEF + 8), up8(4 * (levels - 2))
    owner, dest, table = owner_tile.T, dest_block.T, table_index.T
    exchange = lambda x, axis: lax.all_to_all(x, axis, split_axis=0, concat_axis=0, tiled=True)
    plane = ((rows, width), F32)

    (send,) = call(
        functools.partial(send_kernel, cap),
        3,
        [((n_tile, chunk, width), F32)],
        scratch=[
            pltpu.VMEM((2, rows, width), F32),
            pltpu.VMEM((2, rows, width), F32),
            pltpu.VMEM(owner.shape, I32),
            pltpu.VMEM((n_tile, cap, width), F32),
            pltpu.VMEM((chunk - cap, width), F32),
            pltpu.SemaphoreType.DMA((4 + n_tile,)),
        ],
        space=pltpu.HBM,
        out_space=pltpu.HBM,
        vmem=60,
    )(fields, coefficients, owner)
    got = exchange(send, "tile")
    half = n_tile // 2 * cap
    keep, give = call(
        functools.partial(swap_kernel, cap),
        3,
        [((half + rows, width), F32), ((half + side, width), F32)],
        scratch=[pltpu.VMEM((n_tile, cap, width), F32)],
    )(fields, coefficients, owner)
    arrays, chunks, _ = swap_stage(1, cap, [keep, give], {m: (0, m // 2) for m in range(0, n_tile, 2)})
    (plan,) = call(
        functools.partial(index_kernel, cap, rows),
        5,
        [((PLAN_WAYS + 2 * n_tables, lines, width), BF16)],
        scratch=[pltpu.VMEM((slots, lines), F32)],
    )(owner, dest, table, tables, land_mask)
    arrays, chunks, plan = swap_stage(2, cap, arrays, chunks, plan)
    (part,) = call(functools.partial(flux_kernel, cap, n_tables), 1 + len(arrays), [plane])(got, plan, *arrays[:-1])
    others = [lax.ppermute(part, "sec", [(s, s ^ other) for s in range(n_sec)]) for other in range(n_sec - 1, 0, -1)]
    bit = 4
    while bit < n_tile:
        arrays, chunks, part = swap_stage(bit, cap, arrays, chunks, part)
        bit *= 2
    sources = [chunks[m] for m in range(n_tile)]
    top, back = call(functools.partial(sea_kernel, n_tables), 1 + n_sec, [plane, ((slots, width), F32)])(plan, part, *others)
    got, back = lax.optimization_barrier((got, back))
    (level,) = call(
        functools.partial(levels_kernel, cap), 4, [((levels * rows + 4 * n_tile + side, width), F32)], flops=1 << 32
    )(got, fields, coefficients, top)
    came = exchange(back.reshape(n_tile, cap, width), "tile").reshape(slots, width)
    (total,) = call(
        functools.partial(second_kernel, cap, n_tables, levels, sources),
        2 + len(arrays),
        [plane],
        scratch=[pltpu.VMEM((n_tile, cap, width), F32)],
        flops=1 << 34,
    )(plan, level, *arrays)
    came_total = 0.0
    bit = n_sec // 2
    while bit:
        above = n_sec - 2 * bit
        pairs = [(s, s | bit) for s in range(n_sec) if s & above == above and not s & bit]
        total = total + came_total
        came_total = lax.ppermute(total, "sec", pairs)
        bit //= 2
    (whole,) = call(
        functools.partial(finish_kernel, cap), 1 + len(arrays), [((levels, rows, width), F32)], flops=1 << 28
    )(got, level, *arrays[1:])
    ended, surface = call(
        functools.partial(end_kernel, n_tables),
        3,
        [(fields.shape, F32), ((1, rows, width), F32)],
        scratch=[pltpu.VMEM((rows, width), F32), pltpu.SemaphoreType.DMA((2,))],
        out_space=pltpu.HBM,
    )(came, plan, whole)
    came_total, surface = lax.optimization_barrier((came_total, surface))
    in_hbm, in_vmem = pl.BlockSpec(memory_space=pltpu.HBM), pl.BlockSpec(memory_space=pltpu.VMEM)
    ended = pl.pallas_call(
        forced_kernel,
        out_shape=jax.ShapeDtypeStruct(fields.shape, F32),
        in_specs=[in_hbm] + [in_vmem] * 3,
        out_specs=in_hbm,
        scratch_shapes=[pltpu.VMEM((rows, width), F32), pltpu.SemaphoreType.DMA],
        input_output_aliases={0: 0},
        compiler_params=pltpu.CompilerParams(vmem_limit_bytes=12 * 1024 * 1024),
    )(ended, whole, total, came_total)
    return ended, surface


def solution(mesh):
    placed = (P("sec", None, "tile", None), P("sec", None, "tile", None), P(), P(), P(), P(), P("tile", None))
    return jax.shard_map(
        local,
        mesh=mesh,
        in_specs=placed,
        out_specs=(P("sec", None, "tile", None), P("sec", "tile", None)),
        check_vma=False,
    )
```

```python
import functools

import jax
import jax.numpy as jnp
from jax import lax
from jax.experimental import pallas as pl
from jax.experimental.pallas import tpu as pltpu
from jax.sharding import PartitionSpec as P

FORCING = 0.5
F32, BF16, I32 = jnp.float32, jnp.bfloat16, jnp.int32
N_COEF = 6
PLAN_COLLECT, PLAN_ARRIVE, PLAN_EDGE, PLAN_BACK, PLAN_WAYS = 0, 1, 2, 3, 4


def iota(shape, axis):
    return lax.broadcasted_iota(I32, shape, axis)


def roll(x, shift, axis):
    return pltpu.roll(x, shift % x.shape[axis], axis)


def split(x, parts):
    out = []
    for _ in range(parts):
        out.append(x.astype(BF16))
        x = x - out[-1].astype(F32)
    return out


def mm(a, b):
    return lax.dot_general(a, b, (((1,), (0,)), ((), ())), preferred_element_type=F32)


def mm_t(a, b):
    return lax.dot_general(a, b, (((1,), (1,)), ((), ())), preferred_element_type=F32)


def select_rows(hot, x, parts):
    return mm(jnp.concatenate([hot] * parts, axis=1), jnp.concatenate(split(x, parts)))


def products(lines, plan_ref, rows, dot, axis):
    count = lines.shape[0] // rows
    a1, a2 = split(jnp.concatenate([lines[k * rows : (k + 1) * rows] for k in range(count)], axis=1), 2)
    b1, b2 = [jnp.concatenate([plan_ref[PLAN_WAYS + 2 * k + i] for k in range(count)], axis=axis) for i in range(2)]
    both = dot(jnp.concatenate([a1, a2]), b1)
    return both[:rows] + both[rows:] + dot(a1, b2)


def sideways(x, kappa):
    return x + kappa * (roll(x, 1, x.ndim - 1) + roll(x, -1, x.ndim - 1) - 4.0 * x)


def substep(u, kappa, speed):
    rows = u.shape[1]
    row = iota(u.shape, 1)
    upper = jnp.where(row == 0, 0.0, roll(u, 1, 1))
    lower = jnp.where(row == rows - 1, 0.0, roll(u, -1, 1))
    laplace = upper + lower + roll(u, 1, 2) + roll(u, -1, 2) - 4.0 * u
    return u + kappa * laplace - 0.5 * speed * (lower - upper)


def place():
    sec, tile = lax.axis_index("sec"), lax.axis_index("tile")
    return sec, tile, sec < lax.axis_size("sec") - 1


def own_slots(owner_ref, rows, cap):
    sec, tile, atmos = place()
    n_sec, n_tile = lax.axis_size("sec"), lax.axis_size("tile")
    block = (jnp.minimum(sec, n_sec - 2) * n_tile + tile) * rows
    first = pl.multiple_of(block // 128 * 128, 128)
    half = block - first
    shape = (n_tile * cap, 128)
    lane = iota((1, 128), 1)
    inside = (lane >= half) & (lane < half + rows) & atmos
    owner = jnp.where(inside, owner_ref[:, pl.ds(first, 128)], -1)
    slot = iota(shape, 0)
    hot = [(owner[r : r + 1] == slot // cap).astype(F32) for r in range(owner.shape[0])]
    both = sum(hot)
    before = (iota((128, 128), 0) < iota((128, 128), 1)).astype(BF16)
    rank = mm(both.astype(BF16), before)
    placed = rank == (slot % cap).astype(F32)
    return first, [jnp.where(placed, h, 0.0) for h in hot]


def edge_rows(u, kappa, a, b):
    top, bot = slice(0, 1), slice(u.shape[0] - 1, u.shape[0])
    q_top = sideways(u[top], kappa[top]) + b[top] * u[1:2]
    q_bot = sideways(u[bot], kappa[bot]) + a[bot] * u[-2:-1]
    return [u[top], q_top, u[bot], q_bot]


def padded(lines, count, width):
    if count > len(lines):
        lines = lines + [jnp.zeros((count - len(lines), width), F32)]
    return jnp.concatenate(lines)


def placed_rows(placed, payload):
    return select_rows(sum(placed).astype(BF16), jnp.concatenate([payload] * (128 // payload.shape[0])), 2)


def send_kernel(cap, fields_hbm, coef_hbm, owner_hbm, send_hbm, fields_ref, coef_ref, owner_ref, slots_ref, edge_ref, sems):
    pairs = ((owner_hbm, owner_ref), (coef_hbm.at[0], coef_ref), (fields_hbm.at[0, pl.ds(0, 2)], fields_ref))
    copies = [pltpu.make_async_copy(src, dst, sems.at[i]) for i, (src, dst) in enumerate(pairs)]
    for copy in copies:
        copy.start()
    copies[0].wait()
    _, rows, width = fields_ref.shape
    _, placed = own_slots(owner_ref, rows, cap)
    copies[1].wait()
    copies[2].wait()
    u = fields_ref[...]
    kappa, speed = coef_ref[0], coef_ref[1]
    a = kappa + 0.5 * speed
    b = kappa - 0.5 * speed
    bot = slice(rows - 1, rows)
    extra = [a[0:1], a[0:1] * a[1:2], kappa[0:1], b[bot], b[bot] * b[rows - 2 : rows - 1], kappa[bot]]
    extra += edge_rows(u[0], kappa, a, b) + edge_rows(u[1], kappa, a, b)
    n_tile, side = slots_ref.shape[0], edge_ref.shape[0]
    edge_ref[...] = padded(extra, side, width)
    going = [pltpu.make_async_copy(edge_ref, send_hbm.at[t, pl.ds(cap, side)], sems.at[3 + t]) for t in range(n_tile)]
    going.append(pltpu.make_async_copy(slots_ref, send_hbm.at[:, pl.ds(0, cap)], sems.at[3 + n_tile]))
    for copy in going[:-1]:
        copy.start()
    stepped = substep(substep(u[:1], kappa, speed), kappa, speed)[0]
    slots_ref[...] = placed_rows(placed, stepped).reshape(slots_ref.shape)
    going[-1].start()
    for copy in going:
        copy.wait()


def swap_kernel(cap, fields_ref, coef_ref, owner_ref, keep_ref, give_ref, slots_ref):
    _, tile, _ = place()
    levels, rows, width = fields_ref.shape[1:]
    _, placed = own_slots(owner_ref, rows, cap)
    kappa, speed = coef_ref[0, 0], coef_ref[0, 1]
    stepped = substep(substep(fields_ref[0, :2], kappa, speed), kappa, speed)
    count = slots_ref.shape[0]
    slots_ref[...] = placed_rows(placed, stepped[0] - stepped[1]).reshape(count, cap, width)
    for m in range(count):
        ref = (keep_ref, give_ref)[m % 2]
        ref[m // 2 * cap : (m // 2 + 1) * cap] = slots_ref[tile ^ m]
    a = kappa + 0.5 * speed
    b = kappa - 0.5 * speed
    extra = sum([edge_rows(fields_ref[0, l], kappa, a, b) for l in range(2, levels)], [])
    held = count // 2 * cap
    give_ref[held:] = padded(extra, give_ref.shape[0] - held, width)
    keep_ref[held:] = stepped[0]


def stack_kernel(picks, cap, *refs):
    out_ref = refs[-1]
    for to, (i, j) in enumerate(picks):
        out_ref[to * cap : (to + 1) * cap] = refs[i][j * cap : (j + 1) * cap]
    held = len(picks) * cap
    out_ref[held:] = refs[-2][held:]


def index_kernel(
    cap, rows, owner_ref, dest_ref, table_ref, tables_ref, mask_ref, plan_ref, arrive_sum
):
    n_tables = tables_ref.shape[0]
    for k in range(n_tables):
        at = PLAN_WAYS + 2 * k
        plan_ref[at], plan_ref[at + 1] = split(tables_ref[k], 2)
    sec, tile, atmos = place()
    n_sec, n_tile = lax.axis_size("sec"), lax.axis_size("tile")
    span = n_tile * rows
    start = jnp.minimum(sec, n_sec - 2) * span
    fan = owner_ref.shape[0]
    lines = n_tables * rows
    per = 128 // rows
    g, h = iota((128, 128), 0), iota((128, 128), 1)
    before = ((g < h) & (g // rows == h // rows)).astype(BF16)
    line = iota((lines, 128), 0)
    seat = iota((per * cap, 128), 0)
    lane = iota((per * cap, 128), 1)
    edges = jnp.zeros((lines, 128), F32)
    for group in range(span // 128):
        at = pl.ds(pl.multiple_of(start + group * 128, 128), 128)
        mine = [(owner_ref[r : r + 1, at] == tile) & atmos for r in range(fan)]
        key = jnp.full((1, 128), -1, I32)
        for r in range(fan):
            key = jnp.where(mine[r], table_ref[r : r + 1, at] * rows + dest_ref[r : r + 1, at], key)
        held = (key >= 0).astype(F32)
        rank = mm(jnp.broadcast_to(held, (16, 128)).astype(BF16), before)[:1]
        sits = (rank == (seat % cap).astype(F32)) & (lane // rows == seat // cap) & (held > 0)
        hit = (line == key).astype(BF16)
        arrive = mm_t(sits.astype(BF16), hit)
        arrive_sum[group * per * cap : (group + 1) * per * cap] = arrive
        block, within = group * per + g // rows, g % rows
        column = sum(jnp.where(within == w, i, 0) for i, w in enumerate((0, 1, rows - 2, rows - 1)))
        is_edge = (within < 2) | (within >= rows - 2)
        edges += mm(hit, (is_edge & (h == column * n_tile + block)).astype(BF16))
    arrive = arrive_sum[...]
    plan_ref[PLAN_ARRIVE] = arrive.astype(BF16)
    plan_ref[PLAN_COLLECT] = arrive.T.astype(BF16)
    plan_ref[PLAN_EDGE, :, :128] = edges.astype(BF16)
    for i in range(mask_ref.shape[1] // 128):
        plan_ref[PLAN_EDGE, i * rows : (i + 1) * rows, 128:] = mask_ref[:, i * 128 : (i + 1) * 128].astype(F32).astype(BF16)
    first, placed = own_slots(owner_ref, rows, cap)
    table = table_ref[:, pl.ds(first, 128)]
    for k in range(n_tables):
        here = sum(jnp.where(table[r : r + 1] == k, placed[r], 0.0) for r in range(fan))
        here = here.T
        plan_ref[PLAN_BACK, k * rows : (k + 1) * rows] = sum(here[i : i + rows] for i in range(0, 128, rows)).astype(BF16)


def shifted(x, by):
    row = iota(x.shape, 0)
    return jnp.where(row == (0 if by > 0 else x.shape[0] - 1), 0.0, roll(x, by, 0))


def corrections(coef, edges):
    a0, aa, k0, b1, bb, k1 = coef
    u0, q0, u1, q1 = edges
    b_prev, a_next = shifted(b1, 1), shifted(a0, -1)
    u_prev, q_prev, u_next, q_next = shifted(u1, 1), shifted(q1, 1), shifted(u0, -1), shifted(q0, -1)
    return [
        sideways(a0 * u_prev, k0) + a0 * (q_prev + b_prev * u0),
        aa * u_prev,
        bb * u_next,
        sideways(b1 * u_next, k1) + b1 * (q_next + a_next * u1),
    ]


def whole_level(plane, correction):
    _, tile, _ = place()
    rows = plane.shape[0]
    here = iota(correction[0].shape, 0) == tile
    own = [jnp.sum(jnp.where(here, c, 0.0), axis=0, keepdims=True) for c in correction]
    return jnp.concatenate(
        [plane[:2] + jnp.concatenate(own[:2]), plane[2 : rows - 2], plane[rows - 2 :] + jnp.concatenate(own[2:])]
    )


def water(plan_ref, rows):
    parts = plan_ref.shape[2] // 128
    return jnp.concatenate([plan_ref[PLAN_EDGE, i * rows : (i + 1) * rows, 128:] for i in range(parts)], axis=1).astype(F32)


def flux_of(slots, edges, plan_ref, rows):
    short = 128 - edges.shape[0]
    if short:
        edges = jnp.concatenate([edges, jnp.zeros((short, edges.shape[1]), F32)])
    hot = jnp.concatenate([plan_ref[PLAN_COLLECT], plan_ref[PLAN_EDGE, :, :128]], axis=1)
    return products(select_rows(hot, jnp.concatenate([slots, edges]), 2), plan_ref, rows, mm, 0)


def lines_of(ref, first, count):
    return [ref[:, first + i, :] for i in range(count)]


def flux_kernel(cap, n_tables, got_ref, plan_ref, keep_ref, *refs):
    part_ref = refs[-1]
    _, _, atmos = place()
    n_tile, _, width = got_ref.shape
    rows = part_ref.shape[0]
    stepped = keep_ref[keep_ref.shape[0] - rows :]
    correction = corrections(lines_of(got_ref, cap, N_COEF), lines_of(got_ref, cap + N_COEF, 4))
    whole = whole_level(stepped, correction)
    slots = got_ref[:, :cap, :].reshape(n_tile * cap, width)
    flux = flux_of(slots, jnp.concatenate(correction), plan_ref, rows)
    part_ref[...] = jnp.where(atmos, FORCING * water(plan_ref, rows) * flux, whole)


def levels_kernel(cap, got_ref, fields_ref, coef_ref, top_ref, level_ref):
    _, _, atmos = place()
    kappa, speed = coef_ref[0, 0], coef_ref[0, 1]
    levels, rows, width = fields_ref.shape[1:]
    n_tile = got_ref.shape[0]
    stepped = substep(substep(fields_ref[0], kappa, speed), kappa, speed)
    coef = lines_of(got_ref, cap, N_COEF)
    first, second = [corrections(coef, lines_of(got_ref, cap + N_COEF + 4 * l, 4)) for l in range(2)]
    level_ref[:rows] = jnp.where(atmos, whole_level(stepped[0], first), top_ref[...])
    level_ref[rows : 2 * rows] = whole_level(stepped[1], second)
    level_ref[2 * rows : levels * rows] = stepped[2:].reshape((levels - 2) * rows, width)
    at = levels * rows + 4 * n_tile
    level_ref[levels * rows : at] = jnp.concatenate([x - y for x, y in zip(first, second)])
    level_ref[at:] = padded(
        sum([[u[:1], u[:1], u[rows - 1 :], u[rows - 1 :]] for u in [fields_ref[0, l] for l in range(2, levels)]], []),
        level_ref.shape[0] - at,
        width,
    )


def second_kernel(cap, n_tables, levels, sources, plan_ref, level_ref, *refs):
    swapped, (part_ref, came_ref) = refs[:-2], refs[-2:]
    _, tile, atmos = place()
    n_tile, _, width = came_ref.shape
    rows = part_ref.shape[0]
    edges = level_ref[levels * rows : levels * rows + 4 * n_tile]
    for m, (i, j) in enumerate(sources):
        came_ref[tile ^ m] = swapped[i][j * cap : (j + 1) * cap]
    flux = flux_of(came_ref[...].reshape(n_tile * cap, width), edges, plan_ref, rows)
    part_ref[...] = jnp.where(atmos, FORCING * water(plan_ref, rows) * flux, 0.0)


def finish_kernel(cap, got_ref, level_ref, *refs):
    swapped, whole_ref = refs[:-1], refs[-1]
    _, tile, _ = place()
    levels, rows, width = whole_ref.shape
    n_tile = got_ref.shape[0]
    whole_ref[...] = level_ref[: levels * rows].reshape(levels, rows, width)
    count = 4 * (levels - 2)
    held = n_tile // 2 * cap
    prev = jnp.zeros((count, width), F32)
    after = prev
    for i, ref in enumerate(swapped):
        other = tile ^ (2 ** (i + 1) - 1)
        came = ref[held : held + count]
        prev = jnp.where(other == tile - 1, came, prev)
        after = jnp.where(other == tile + 1, came, after)
    own = got_ref[tile, cap : cap + 8]
    a0, aa, k0, b1, bb, k1 = [own[i : i + 1] for i in range(N_COEF)]
    b_prev = jnp.where(tile > 0, got_ref[jnp.maximum(tile - 1, 0), cap : cap + 8][3:4], 0.0)
    a_next = jnp.where(tile < n_tile - 1, got_ref[jnp.minimum(tile + 1, n_tile - 1), cap : cap + 8][0:1], 0.0)
    for l in range(2, levels):
        u0, _, u1, _ = [level_ref[levels * rows + 4 * n_tile + 4 * (l - 2) + i : levels * rows + 4 * n_tile + 4 * (l - 2) + i + 1] for i in range(4)]
        u_prev, q_prev = [prev[4 * (l - 2) + i : 4 * (l - 2) + i + 1] for i in (2, 3)]
        u_next, q_next = [after[4 * (l - 2) + i : 4 * (l - 2) + i + 1] for i in (0, 1)]
        whole_ref[l, :2] += jnp.concatenate([sideways(a0 * u_prev, k0) + a0 * (q_prev + b_prev * u0), aa * u_prev])
        whole_ref[l, rows - 2 :] += jnp.concatenate([bb * u_next, sideways(b1 * u_next, k1) + b1 * (q_next + a_next * u1)])


def sea_kernel(n_tables, plan_ref, *refs):
    parts, (top_ref, back_ref) = refs[:-2], refs[-2:]
    top = sum(part[...] for part in parts)
    top_ref[...] = top
    sea = water(plan_ref, top.shape[0]) * top
    back_ref[...] = select_rows(plan_ref[PLAN_ARRIVE], jnp.concatenate([sea] * n_tables), 2)


def end_kernel(n_tables, came_ref, plan_ref, whole_ref, fields_hbm, surface_hbm, surface_ref, sems):
    _, _, atmos = place()
    _, rows, width = whole_ref.shape
    copies = [
        pltpu.make_async_copy(whole_ref, fields_hbm.at[0], sems.at[0]),
        pltpu.make_async_copy(surface_ref, surface_hbm.at[0], sems.at[1]),
    ]
    copies[0].start()
    picked = select_rows(plan_ref[PLAN_BACK], came_ref[...], 2)
    seen = products(picked, plan_ref, rows, mm_t, 1)
    surface_ref[...] = jnp.where(atmos, seen, water(plan_ref, rows) * whole_ref[0])
    copies[1].start()
    for copy in copies:
        copy.wait()


def forced_kernel(_, whole_ref, total_ref, last_ref, fields_hbm, plane_ref, sem):
    _, _, atmos = place()

    @pl.when(jnp.logical_not(atmos))
    def _():
        plane_ref[...] = whole_ref[1] + total_ref[...] + last_ref[...]
        copy = pltpu.make_async_copy(plane_ref, fields_hbm.at[0, 1], sem)
        copy.start()
        copy.wait()


def call(kernel, n_in, outs, flops=0, scratch=(), space=pltpu.VMEM, out_space=pltpu.VMEM, vmem=12):
    shapes = [jax.ShapeDtypeStruct(s, d) for s, d in outs]
    return pl.pallas_call(
        kernel,
        out_shape=shapes,
        in_specs=[pl.BlockSpec(memory_space=space)] * n_in,
        out_specs=[pl.BlockSpec(memory_space=out_space)] * len(shapes),
        scratch_shapes=scratch,
        compiler_params=pltpu.CompilerParams(vmem_limit_bytes=vmem * 1024 * 1024),
        cost_estimate=pl.CostEstimate(flops=flops, bytes_accessed=1 << 10, transcendentals=0),
    )


def swap_stage(bit, cap, arrays, chunks, after=None):
    n_tile = lax.axis_size("tile")
    going = [m for m in range(n_tile) if m & bit]
    if after is not None:
        arrays, after = lax.optimization_barrier((arrays, after))
    if bit == 1:
        give = arrays.pop()
    else:
        picks = [chunks[m] for m in going]
        used = sorted({i for i, _ in picks})
        picks = [(used.index(i), j) for i, j in picks]
        taken = [arrays[i] for i in used]
        if used[-1] != len(arrays) - 1:
            taken.append(arrays[-1])
        kernel = functools.partial(stack_kernel, picks, cap)
        (give,) = call(kernel, len(taken), [(arrays[-1].shape, F32)])(*taken)
    came = lax.ppermute(give, "tile", [(t, t ^ bit) for t in range(n_tile)])
    chunks = chunks | {m: (len(arrays), i) for i, m in enumerate(going)}
    return arrays + [came], chunks, after


def local(fields, coefficients, owner_tile, dest_block, table_index, tables, land_mask):
    n_sec, n_tile = lax.axis_size("sec"), lax.axis_size("tile")
    levels, rows, width = fields.shape[1:]
    fan = owner_tile.shape[1]
    n_tables = tables.shape[0]
    cap = 2 * fan * rows // n_tile
    slots, lines = n_tile * cap, n_tables * rows
    up8 = lambda n: -(-n // 8) * 8
    chunk, side = up8(cap + N_COEF + 8), up8(4 * (levels - 2))
    owner, dest, table = owner_tile.T, dest_block.T, table_index.T
    exchange = lambda x, axis: lax.all_to_all(x, axis, split_axis=0, concat_axis=0, tiled=True)
    plane = ((rows, width), F32)

    (send,) = call(
        functools.partial(send_kernel, cap),
        3,
        [((n_tile, chunk, width), F32)],
        scratch=[
            pltpu.VMEM((2, rows, width), F32),
            pltpu.VMEM((2, rows, width), F32),
            pltpu.VMEM(owner.shape, I32),
            pltpu.VMEM((n_tile, cap, width), F32),
            pltpu.VMEM((chunk - cap, width), F32),
            pltpu.SemaphoreType.DMA((4 + n_tile,)),
        ],
        space=pltpu.HBM,
        out_space=pltpu.HBM,
        vmem=60,
    )(fields, coefficients, owner)
    got = exchange(send, "tile")
    half = n_tile // 2 * cap
    keep, give = call(
        functools.partial(swap_kernel, cap),
        3,
        [((half + rows, width), F32), ((half + side, width), F32)],
        scratch=[pltpu.VMEM((n_tile, cap, width), F32)],
    )(fields, coefficients, owner)
    arrays, chunks, _ = swap_stage(1, cap, [keep, give], {m: (0, m // 2) for m in range(0, n_tile, 2)})
    (plan,) = call(
        functools.partial(index_kernel, cap, rows),
        5,
        [((PLAN_WAYS + 2 * n_tables, lines, width), BF16)],
        scratch=[pltpu.VMEM((slots, lines), F32)],
    )(owner, dest, table, tables, land_mask)
    arrays, chunks, plan = swap_stage(2, cap, arrays, chunks, plan)
    (part,) = call(functools.partial(flux_kernel, cap, n_tables), 1 + len(arrays), [plane])(got, plan, *arrays[:-1])
    others = [lax.ppermute(part, "sec", [(s, s ^ other) for s in range(n_sec)]) for other in range(n_sec - 1, 0, -1)]
    bit = 4
    while bit < n_tile:
        arrays, chunks, part = swap_stage(bit, cap, arrays, chunks, part)
        bit *= 2
    sources = [chunks[m] for m in range(n_tile)]
    top, back = call(functools.partial(sea_kernel, n_tables), 1 + n_sec, [plane, ((slots, width), F32)])(plan, part, *others)
    got, back = lax.optimization_barrier((got, back))
    (level,) = call(
        functools.partial(levels_kernel, cap), 4, [((levels * rows + 4 * n_tile + side, width), F32)], flops=1 << 32
    )(got, fields, coefficients, top)
    came = exchange(back.reshape(n_tile, cap, width), "tile").reshape(slots, width)
    (total,) = call(
        functools.partial(second_kernel, cap, n_tables, levels, sources),
        2 + len(arrays),
        [plane],
        scratch=[pltpu.VMEM((n_tile, cap, width), F32)],
        flops=1 << 34,
    )(plan, level, *arrays)
    came_total = 0.0
    bit = n_sec // 2
    while bit:
        above = n_sec - 2 * bit
        pairs = [(s, s | bit) for s in range(n_sec) if s & above == above and not s & bit]
        total = total + came_total
        came_total = lax.ppermute(total, "sec", pairs)
        bit //= 2
    (whole,) = call(
        functools.partial(finish_kernel, cap), 1 + len(arrays), [((levels, rows, width), F32)], flops=1 << 28
    )(got, level, *arrays[1:])
    ended, surface = call(
        functools.partial(end_kernel, n_tables),
        3,
        [(fields.shape, F32), ((1, rows, width), F32)],
        scratch=[pltpu.VMEM((rows, width), F32), pltpu.SemaphoreType.DMA((2,))],
        out_space=pltpu.HBM,
    )(came, plan, whole)
    came_total, surface = lax.optimization_barrier((came_total, surface))
    in_hbm, in_vmem = pl.BlockSpec(memory_space=pltpu.HBM), pl.BlockSpec(memory_space=pltpu.VMEM)
    ended = pl.pallas_call(
        forced_kernel,
        out_shape=jax.ShapeDtypeStruct(fields.shape, F32),
        in_specs=[in_hbm] + [in_vmem] * 3,
        out_specs=in_hbm,
        scratch_shapes=[pltpu.VMEM((rows, width), F32), pltpu.SemaphoreType.DMA],
        input_output_aliases={0: 0},
        compiler_params=pltpu.CompilerParams(vmem_limit_bytes=12 * 1024 * 1024),
    )(ended, whole, total, came_total)
    return ended, surface


def solution(mesh):
    placed = (P("sec", None, "tile", None), P("sec", None, "tile", None), P(), P(), P(), P(), P("tile", None))
    return jax.shard_map(
        local,
        mesh=mesh,
        in_specs=placed,
        out_specs=(P("sec", None, "tile", None), P("sec", "tile", None)),
        check_vma=False,
    )
```
